512 devices in a mesh: section: 2 (over y_hi), dp: 32 (over y_lo, z), mp: 8 (over x, core).
Axes of the slice: x: 4, y: 4 (y_hi: 2, y_lo: 2; y = y_hi * 2 + y_lo), z: 16, core: 2. Of those that a mesh axis runs over, the one named last changes fastest.
Arguments:
- layer_rows: bfloat16 [2, 8192, 4096], P('section', 'dp'), may hold values from -6 to 6
- cotangent: bfloat16 [8192, 4096], P('dp', 'mp'), may hold values from -6 to 6
- norm_gains: float32 [2, 4096], P('section'), may hold values from 0.5 to 1.5
- projections: bfloat16 [2, 4096, 2, 2048], P('section', 'dp', None, 'mp'), may hold values from -0.09375 to 0.09375
- enc_len: int32 [256], replicated, may hold values from 1 to 64, as said below
- dec_len: int32 [256], replicated, may hold values from 1 to 64, as said below
- enc_dev: int32 [256], replicated, may hold values from 0 to 31, as said below
- dec_dev: int32 [256], replicated, may hold values from 0 to 31, as said below
Outputs:
- grad_rows: bfloat16 [2, 8192, 4096], P('section', 'dp', 'mp')
The draws below stay inside these ranges and needn't reach their ends.
Inputs may be any that keep to these rules, and one draw needn't show every extreme that they name: The 8 examples of one encoder device (equal enc_dev) have enc_len summing to exactly 256; in every draw some example has exactly 64. The 8 examples of one decoder device (equal dec_dev) have dec_len summing to exactly 256; in every draw some example has exactly 64. Each device number is the enc_dev of exactly 8 examples. Each device number is the dec_dev of exactly 8 examples; the examples of one encoder device have different dec_dev, and those of one decoder device have different enc_dev.
All inputs are finite; a program needn't handle non-finite values.
Results may differ from the reference program's by a relative error of at most 0.022.
Values may be sent and summed in bfloat16 or wider, within the bound.
A program may use at most 64 MiB of HBM per device.

```python
import jax
import jax.numpy as jnp
from jax import lax

D = 4096
HEAD = 64
HEADS = 32
ROWS = 256
EX_DEV = 8
MOST = 64
TOKENS = 8192
EXAMPLES = 256
HWD = 2048
N_DP = 32
N_MP = 8


def length_rows(key, peer_total, count, half_len):
    key_pair, key_forced, key_pick, key_one, key_perm = jax.random.split(key, 5)
    spread = jax.random.randint(key_pair, (peer_total, count // 2), 0, half_len)
    pairs = jnp.stack([half_len + spread, half_len - spread], axis=2).reshape(peer_total, count)
    cut = jax.random.randint(key_forced, (peer_total,), 1, half_len)
    full = jnp.full((peer_total,), 2 * half_len, jnp.int32)
    same = jnp.full((peer_total,), half_len, jnp.int32)
    forced_head = jnp.stack([full, half_len - cut, cut, same], axis=1)
    forced_rows = jnp.concatenate([forced_head, pairs[:, 4:]], axis=1)
    chosen = jax.random.randint(key_one, (), 0, peer_total)
    pick = (jax.random.randint(key_pick, (peer_total,), 0, 2) == 1) | (jnp.arange(peer_total) == chosen)
    pattern = jnp.where(pick[:, None], forced_rows, pairs).astype(jnp.int32)
    shuffle_keys = jax.random.randint(key_perm, (peer_total, count), 0, 1 << 20) * count + jnp.arange(count)[None, :]
    shuffle = jnp.argsort(shuffle_keys, axis=1)
    return jnp.take_along_axis(pattern, shuffle, axis=1)


def example_tables(key):
    peer_total = N_DP
    count = EX_DEV
    example_total = EXAMPLES
    half_len = ROWS // EX_DEV
    key_ids, key_dest, key_enc, key_dec = jax.random.split(key, 4)
    example_ids = jax.random.permutation(key_ids, example_total).astype(jnp.int32)
    positions = jnp.arange(example_total, dtype=jnp.int32)
    source_of = positions // count
    rank_of = positions % count
    enc_table = jnp.zeros((example_total,), jnp.int32).at[example_ids].set(source_of)
    device_perm = jax.random.permutation(key_dest, peer_total).astype(jnp.int32)
    destination = device_perm[(source_of + rank_of) % peer_total]
    dec_table = jnp.zeros((example_total,), jnp.int32).at[example_ids].set(destination)
    enc_pattern = length_rows(key_enc, peer_total, count, half_len).reshape(-1)
    enc_lengths = jnp.zeros((example_total,), jnp.int32).at[example_ids].set(enc_pattern)
    dec_pattern = length_rows(key_dec, peer_total, count, half_len)
    dec_lengths = jnp.zeros((example_total,), jnp.int32).at[example_ids].set(dec_pattern[destination, rank_of])
    return (enc_lengths, dec_lengths, enc_table, dec_table)


def draw_enc_len(key, part):
    return example_tables(key)[0]


def draw_dec_len(key, part):
    return example_tables(key)[1]


def draw_enc_dev(key, part):
    return example_tables(key)[2]


def draw_dec_dev(key, part):
    return example_tables(key)[3]


def steps_of(own_key, extent, cuts, least, largest):
    loudness = 1.0
    for dim, parts in cuts:
        steps = jax.random.uniform(jax.random.fold_in(jax.random.fold_in(own_key, 6), dim), (parts,), jnp.float32, least / len(cuts), largest / len(cuts))
        loudness = loudness * jnp.repeat(jnp.exp(steps), extent[dim] // parts).reshape((-1,) + (1,) * (len(extent) - 1 - dim))
    return loudness


def noise(rng, extent, scale, bound, cuts=(), held_as=jnp.bfloat16):
    array = scale * jax.random.normal(rng, extent, jnp.float32)
    if cuts:
        array = array * steps_of(rng, extent, cuts, -0.22, 0.18)
    return jnp.clip(array, -bound, bound).astype(held_as)


def setup_inputs(seed: int = 0) -> dict:
    key_of = jax.random.split(jax.random.key(seed), 9)
    return {
        "layer_rows": noise(key_of[0], (2, TOKENS, D), 1.0, 6.0, ((0, 2), (1, 32))),
        "cotangent": noise(key_of[1], (TOKENS, D), 1.0, 6.0, ((0, 32), (1, 8))),
        "norm_gains": jnp.clip(1.0 + 0.1 * jax.random.normal(key_of[2], (2, D), jnp.float32), 0.5, 1.5),
        "projections": noise(key_of[3], (2, D, 2, HWD), D ** -0.5, 0.09375, ((0, 2), (1, 32), (3, 8))),
        "enc_len": draw_enc_len(jax.random.fold_in(key_of[8], 71), 0),
        "dec_len": draw_dec_len(jax.random.fold_in(key_of[8], 71), 0),
        "enc_dev": draw_enc_dev(jax.random.fold_in(key_of[8], 71), 0),
        "dec_dev": draw_dec_dev(jax.random.fold_in(key_of[8], 71), 0),
    }


norm_eps = 1e-06

def normalize(stream, gain_row):
    values = stream.astype(jnp.float32)
    inverse = lax.rsqrt(lax.optimization_barrier(jnp.mean(values * values, axis=1, keepdims=True)) + norm_eps)
    return ((values * inverse * gain_row[None, :]).astype(jnp.bfloat16), inverse)

def packed_starts(len_table, dev_table):
    example_total = dev_table.shape[0]
    identity = jnp.arange(example_total, dtype=jnp.int32)
    ordering = jnp.argsort(dev_table * example_total + identity).astype(jnp.int32)
    sorted_lengths = len_table[ordering]
    sorted_starts = (jnp.cumsum(sorted_lengths) - sorted_lengths).astype(jnp.int32)
    starts = jnp.zeros((example_total,), jnp.int32).at[ordering].set(sorted_starts)
    return (starts, ordering, sorted_starts)

def norm_grad(stream, gain_row, inverse, grad_normed):
    values = stream.astype(jnp.float32)
    weighted = grad_normed * gain_row[None, :]
    row_stat = lax.optimization_barrier(jnp.sum(weighted * values, axis=1, keepdims=True))
    return (inverse * weighted - values * inverse ** 3 * row_stat / D).astype(jnp.bfloat16)

def reference(layer_rows, cotangent, norm_gains, projections, enc_len, dec_len, enc_dev, dec_dev):
    scale_factor = 1.0 / float(HEAD) ** 0.5
    enc_normed, enc_inverse = normalize(layer_rows[0], norm_gains[0])
    dec_normed, dec_inverse = normalize(layer_rows[1], norm_gains[1])
    keys_all = jnp.dot(enc_normed, projections[0, :, 0, :], preferred_element_type=jnp.float32).astype(jnp.bfloat16)
    values_all = jnp.dot(enc_normed, projections[0, :, 1, :], preferred_element_type=jnp.float32).astype(jnp.bfloat16)
    queries_all = jnp.dot(dec_normed, projections[1, :, 0, :], preferred_element_type=jnp.float32).astype(jnp.bfloat16)
    grad_attended = jnp.dot(cotangent, projections[1, :, 1, :], preferred_element_type=jnp.float32).astype(jnp.bfloat16)
    enc_start, enc_order, enc_sorted = packed_starts(enc_len, enc_dev)
    dec_start, dec_order, dec_sorted = packed_starts(dec_len, dec_dev)
    row_index = jnp.arange(TOKENS, dtype=jnp.int32)
    row_example = dec_order[(jnp.searchsorted(dec_sorted, row_index, side='right') - 1).astype(jnp.int32)]
    offsets = jnp.arange(MOST, dtype=jnp.int32)
    stacked_kv = jnp.stack([keys_all, values_all], axis=1)

    def per_device(device):
        examples = lax.dynamic_slice_in_dim(dec_order, (device * EX_DEV).astype(jnp.int32), EX_DEV, 0)
        slot_rows = enc_start[examples][:, None] + offsets[None, :]
        slot_valid = offsets[None, :] < enc_len[examples][:, None]
        gathered = stacked_kv[jnp.clip(slot_rows, 0, TOKENS - 1)]
        slot_kv = jnp.where(slot_valid[:, :, None, None], gathered, jnp.zeros_like(gathered))
        first_row = (device * ROWS).astype(jnp.int32)
        query_heads = lax.dynamic_slice_in_dim(queries_all, first_row, ROWS, 0).reshape(ROWS, HEADS, HEAD).astype(jnp.float32)
        dout_heads = lax.dynamic_slice_in_dim(grad_attended, first_row, ROWS, 0).reshape(ROWS, HEADS, HEAD).astype(jnp.float32)
        example_rows = lax.dynamic_slice_in_dim(row_example, first_row, ROWS, 0)
        key_mask = (example_rows[:, None, None] == examples[None, :, None]) & slot_valid[None, :, :]
        key_mask = key_mask.reshape(ROWS, EX_DEV * MOST)
        key_heads = slot_kv[:, :, 0, :].reshape(EX_DEV * MOST, HEADS, HEAD).astype(jnp.float32)
        value_heads = slot_kv[:, :, 1, :].reshape(EX_DEV * MOST, HEADS, HEAD).astype(jnp.float32)
        scores = jnp.einsum('thc,khc->htk', query_heads, key_heads) * scale_factor
        exp_scores = jnp.where(key_mask[None, :, :], jnp.exp(scores), 0.0)
        probs = exp_scores / lax.optimization_barrier(jnp.sum(exp_scores, axis=2, keepdims=True))
        probs_bf = probs.astype(jnp.bfloat16)
        attended = jnp.einsum('htk,khc->thc', probs_bf.astype(jnp.float32), value_heads).astype(jnp.bfloat16)
        grad_probs = jnp.einsum('thc,khc->htk', dout_heads, value_heads)
        row_delta = lax.optimization_barrier(jnp.sum(dout_heads * attended.astype(jnp.float32), axis=2)).T[:, :, None]
        grad_scores = (probs * (grad_probs - row_delta) * scale_factor).astype(jnp.bfloat16).astype(jnp.float32)
        grad_query = jnp.einsum('htk,khc->thc', grad_scores, key_heads).astype(jnp.bfloat16).reshape(ROWS, HWD)
        grad_keys = jnp.einsum('htk,thc->khc', grad_scores, query_heads).astype(jnp.bfloat16)
        grad_values = jnp.einsum('htk,thc->khc', probs_bf.astype(jnp.float32), dout_heads).astype(jnp.bfloat16)
        slot_grads = jnp.stack([grad_keys, grad_values], axis=1).reshape(EX_DEV, MOST, 2, HWD)
        target = jnp.where(slot_valid, slot_rows, TOKENS).astype(jnp.int32)
        return (grad_query, slot_grads, target)
    grad_query, slot_grads, targets = lax.map(per_device, jnp.arange(N_DP, dtype=jnp.int32))
    enc_grads = jnp.zeros((TOKENS + 1, 2, HWD), jnp.float32).at[targets.reshape(-1)].add(slot_grads.reshape(-1, 2, HWD).astype(jnp.float32))[:TOKENS].astype(jnp.bfloat16)
    grad_query = grad_query.reshape(TOKENS, HWD)
    group_cols = HWD // N_MP

    def branch_sum(grad_list, section_index):
        summed = jnp.zeros((TOKENS, D), jnp.float32)
        for mp_group in range(N_MP):
            low = mp_group * group_cols
            row_term = jnp.zeros((TOKENS, D), jnp.float32)
            for grads, which_half in grad_list:
                row_term = row_term + jnp.dot(grads[:, low:low + group_cols], projections[section_index, :, which_half, low:low + group_cols].T, preferred_element_type=jnp.float32)
            rounded = lax.optimization_barrier(row_term.astype(jnp.bfloat16))
            summed = summed + rounded.astype(jnp.float32)
        return summed
    enc_dn = branch_sum([(enc_grads[:, 0, :], 0), (enc_grads[:, 1, :], 1)], 0)
    dec_dn = branch_sum([(grad_query, 0)], 1)
    return jnp.stack([norm_grad(layer_rows[0], norm_gains[0], enc_inverse, enc_dn), norm_grad(layer_rows[1], norm_gains[1], dec_inverse, dec_dn)])
```

```python
import functools

import jax
import jax.numpy as jnp
from jax import lax
from jax.experimental import pallas as pl
from jax.experimental.pallas import tpu as pltpu
from jax.sharding import PartitionSpec as P

HEAD = 64
EX_DEV = 8
EPS = 1e-06
LANES = 128
CUT = 48
MESH = pl.DeviceIdType.MESH
F32 = jnp.float32
BF16 = jnp.bfloat16


def nt(a, b):
    return lax.dot_general(a, b, (((1,), (1,)), ((), ())), preferred_element_type=F32)


def tn(a, b):
    return lax.dot_general(a, b, (((0,), (0,)), ((), ())), preferred_element_type=F32)


def nn(a, b):
    return jnp.dot(a, b, preferred_element_type=F32)


def kernel(
    n_dp,
    n_mp,
    x_ref,
    gain_ref,
    w_ref,
    cot_ref,
    tab_r,
    tab_c,
    out_ref,
    wall,
    left0,
    left1,
    inv_ref,
    acc,
    qkv,
    grad,
    fidx_ref,
    ridx_ref,
    rank_ref,
    wide,
    send1,
    in1,
    send2,
    in2,
    send3,
    in3,
    send4,
    in4,
    sib_send,
    sib_recv,
    x_send,
    x_recv,
    z_sems,
    y_sems,
    cot_sems,
    w_send_sem,
    cot_send_sem,
    hop_send,
    hop_recv,
    hop_local,
    c_send,
    c_sib,
    c_x,
):
    nz = n_dp // 2
    nx = n_mp // 2
    half = nz // 2
    slots = 2 * n_dp
    rows, features = x_ref.shape
    depth = w_ref.shape[0]
    keep = rows // slots
    section = lax.axis_index("section")
    dp = lax.axis_index("dp")
    mp = lax.axis_index("mp")
    yl = dp // nz
    z = dp % nz
    xx = mp // 2
    core = mp % 2
    me = section * n_dp + dp
    encoder = section == 0
    decoder = section == 1

    barrier = pltpu.get_barrier_semaphore()

    def greet(j, carry):
        peer = (me + j) % slots
        pl.semaphore_signal(
            barrier, inc=1, device_id=(peer // n_dp, peer % n_dp, mp), device_id_type=MESH
        )
        return carry

    def greet_mp(j, carry):
        pl.semaphore_signal(
            barrier, inc=1, device_id=(section, dp, (mp + j) % n_mp), device_id_type=MESH
        )
        return carry

    lax.fori_loop(1, slots, greet, 0)
    lax.fori_loop(1, n_mp, greet_mp, 0)
    pl.semaphore_wait(barrier, slots - 1 + n_mp - 1)

    spans = {"b": (CUT, depth - CUT), "a": (0, CUT), "o": (0, CUT)}
    order = ("b", "a", "o")

    def span(kind, y, zb):
        first, size = spans[kind]
        return wall.at[pl.ds(pl.multiple_of((y * nz + zb) * depth + first, 16), size), :]

    def exists(sign, kind, hop):
        if hop < half:
            return True
        return hop == half and ((kind == "b") == (sign == 1))

    def z_copy(sign, kind, hop, sending):
        y = 1 - yl if kind == "o" else yl
        back = hop - 1 if sending else hop
        part = span(kind, y, (z - sign * back + nz) % nz)
        return pltpu.make_async_remote_copy(
            src_ref=part,
            dst_ref=part,
            send_sem=w_send_sem,
            recv_sem=z_sems.at[(1 - sign) // 2, order.index(kind), hop - 1],
            device_id=(section, yl * nz + (z + sign + nz) % nz, mp),
            device_id_type=MESH,
        )

    def y_slot(sign, hop):
        if hop == 0:
            return 0
        return hop if sign == 1 else half + hop

    def y_copy(kind, sign, hop, sending):
        y = yl if sending else 1 - yl
        part = span(kind, y, (z - sign * hop + nz) % nz)
        slot = nz if kind == "a" else y_slot(sign, hop)
        return pltpu.make_async_remote_copy(
            src_ref=part,
            dst_ref=part,
            send_sem=w_send_sem,
            recv_sem=y_sems.at[slot],
            device_id=(section, (1 - yl) * nz + z, mp),
            device_id_type=MESH,
        )

    wall[pl.ds(pl.multiple_of(dp * depth, depth), depth), :] = w_ref[...]
    for kind in ("b", "a"):
        for sign in (1, -1):
            if exists(sign, kind, 1):
                z_copy(sign, kind, 1, True).start()
        y_copy("a" if kind == "b" else "b", 1, 0, True).start()

    per_mp = features // n_mp // LANES

    def cot_copy(owner, slot, target):
        part = left1.at[pl.ds(owner * per_mp, per_mp)]
        return pltpu.make_async_remote_copy(
            src_ref=part,
            dst_ref=part,
            send_sem=cot_send_sem,
            recv_sem=cot_sems.at[slot],
            device_id=(section, dp, target),
            device_id_type=MESH,
        )

    sibling = xx * 2 + 1 - core

    @pl.when(decoder)
    def _():
        for c in range(per_mp):
            left1[mp * per_mp + c] = cot_ref[:, c * LANES : (c + 1) * LANES]
        for o in (2, 1, 3):
            if o < nx:
                cot_copy(mp, o, (xx + o) % nx * 2 + core).start()
        cot_copy(mp, nx, sibling).start()

    y_copy("a", 1, 0, False).wait_recv()
    for sign in (1, -1):
        if exists(sign, "o", 1):
            z_copy(sign, "o", 1, True).start()

    step = 32 if rows % 32 == 0 else rows

    def norm_rows(i, carry):
        at = pl.ds(pl.multiple_of(i * step, step), step)
        values = x_ref[at, :].astype(F32)
        inverse = lax.rsqrt(jnp.mean(values * values, axis=1, keepdims=True) + EPS)
        inv_ref[at, :] = jnp.broadcast_to(inverse, (step, LANES))
        normed = (values * inverse * gain_ref[...]).astype(BF16)
        for c in range(features // LANES):
            left0[c, at, :] = normed[:, c * LANES : (c + 1) * LANES]

        @pl.when(encoder)
        def _():
            for c in range(features // LANES):
                left1[c, at, :] = normed[:, c * LANES : (c + 1) * LANES]

        return carry

    lax.fori_loop(0, rows // step, norm_rows, 0)

    def tables():
        count = EX_DEV * n_dp
        el_r, dl_r, ed_r, dd_r = (tab_r[k : k + 1, :] for k in range(4))
        el_c, dl_c, ed_c, dd_c = (tab_c[:, k : k + 1] for k in range(4))
        shape = (count, count)
        down = lax.broadcasted_iota(jnp.int32, shape, 0).astype(F32)
        along = lax.broadcasted_iota(jnp.int32, shape, 1).astype(F32)
        zero = jnp.zeros(shape, F32)
        same_enc = ed_r == ed_c
        same_dec = dd_r == dd_c
        dstart_r = jnp.sum(
            jnp.where(same_dec & (down < along), dl_c + zero, 0.0), axis=0, keepdims=True
        )
        rank_r = jnp.sum(jnp.where(same_enc & (down < along), 1.0 + zero, 0.0), axis=0, keepdims=True)
        estart_c = jnp.sum(
            jnp.where(same_enc & (along < down), el_r + zero, 0.0), axis=1, keepdims=True
        )
        rank_c = jnp.sum(jnp.where(same_enc & (along < down), 1.0 + zero, 0.0), axis=1, keepdims=True)
        start_i = dstart_r.astype(jnp.int32)
        offset = (me - start_i) & (slots - 1)
        slot = (start_i + offset) // slots
        source = dd_r * float(4 * keep) + slot.astype(F32)
        value = jnp.where(offset.astype(F32) < dl_r, source + 1.0, 0.0)
        place = ed_r * float(EX_DEV) + rank_r
        fidx = jnp.sum(jnp.where(place == down, value + zero, 0.0), axis=1, keepdims=True) - 1.0
        fidx_ref[...] = jnp.broadcast_to(fidx, fidx_ref.shape)
        q_i = lax.broadcasted_iota(jnp.int32, (n_dp * 2 * keep, count), 0)
        dev_q = (q_i // (2 * keep)).astype(F32)
        side_q = (q_i % (2 * keep) // keep).astype(F32)
        row_q = (q_i % keep * slots + me).astype(F32)
        hit = (dd_r == dev_q) & (dstart_r <= row_q) & (row_q < dstart_r + dl_r)
        target = ed_r * float(2 * EX_DEV) + rank_r + side_q * float(EX_DEV) + 1.0
        ridx = jnp.sum(jnp.where(hit, target, 0.0), axis=1, keepdims=True) - 1.0
        ridx_ref[...] = jnp.broadcast_to(ridx, ridx_ref.shape)
        u_r = lax.broadcasted_iota(jnp.int32, (count, rows), 1).astype(F32)
        mine = (ed_c == dp.astype(F32)) & (estart_c <= u_r) & (u_r < estart_c + el_c)
        rank_u = jnp.sum(jnp.where(mine, rank_c + jnp.zeros_like(u_r), 0.0), axis=0, keepdims=True)
        rank_ref[...] = jnp.broadcast_to(rank_u, rank_ref.shape)

    tables()
    acc[...] = jnp.zeros_like(acc)

    width = w_ref.shape[1] // 2

    def product(blocks):
        total0 = total1 = None
        for y, zb in blocks:
            block = y * nz + zb
            at = pl.ds(pl.multiple_of(block * depth, depth), depth)
            p0 = nn(left0[block], wall[at, :width])
            p1 = nn(left1[block], wall[at, width:])
            total0 = p0 if total0 is None else total0 + p0
            total1 = p1 if total1 is None else total1 + p1
        acc[:, :width] += total0
        acc[:, width:] += total1

    def arrived(hop):
        blocks = []
        for sign in (1, -1):
            if hop == 0 and sign == -1 or hop == half and sign == -1:
                continue
            y_copy("b", sign, hop, False).wait_recv()
            zb = (z - sign * hop + nz) % nz
            blocks += [(yl, zb), (1 - yl, zb)]
        return blocks

    ready = []
    for hop in range(1, half + 1):
        for kind in order:
            for sign in (1, -1):
                if exists(sign, kind, hop):
                    z_copy(sign, kind, hop, False).wait_recv()
                    if exists(sign, kind, hop + 1):
                        z_copy(sign, kind, hop + 1, True).start()
                    if kind == "b":
                        y_copy("b", sign, hop, True).start()
        if hop == max(1, half - 5):

            @pl.when(decoder)
            def _():
                for o in (1, 3, 2):
                    if o < nx:
                        owner = (xx - o + nx) % nx * 2 + core
                        cot_copy(owner, o, sibling).wait_recv()
                        cot_copy(owner, nx + o, sibling).start()

        if hop == max(1, half - 4):

            @pl.when(decoder)
            def _():
                for o in range(nx):
                    owner = (xx - o + nx) % nx * 2 + 1 - core
                    cot_copy(owner, nx + o, sibling).wait_recv()

        ready += [arrived(hop - 1)]
        if hop >= max(1, half - 4):
            for blocks in ready:
                product(blocks)
            ready = []
    product(arrived(half))

    def hop_send_copy(k, src, dst, target_section, target_dp):
        return pltpu.make_async_remote_copy(
            src_ref=src,
            dst_ref=dst,
            send_sem=hop_send.at[k],
            recv_sem=hop_recv.at[k],
            device_id=(target_section, target_dp, mp),
            device_id_type=MESH,
        )

    def block_of(buf, i, size):
        if size is None:
            return buf.at[i]
        return buf.at[pl.ds(pl.multiple_of(i * size, size), size)]

    def wait_bytes(sem, buf, count, size):
        part = buf.at[pl.ds(0, count if size is None else count * size)]
        pltpu.make_async_copy(part, part, sem).wait()

    def spread(k, is_source, src, dst, size=None):
        @pl.when(is_source)
        def _():
            pltpu.make_async_copy(
                block_of(src, me, size), block_of(dst, dp, size), hop_local.at[k]
            ).start()

            def one(j, carry):
                i = (me + j) % slots
                hop_send_copy(
                    k, block_of(src, i, size), block_of(dst, dp, size), i // n_dp, i % n_dp
                ).start()
                return carry

            lax.fori_loop(1, slots, one, 0)
            pltpu.make_async_copy(
                block_of(src, me, size), block_of(dst, dp, size), hop_local.at[k]
            ).wait()
            wait_bytes(hop_recv.at[k], dst, n_dp - 1, size)

        @pl.when(jnp.logical_not(is_source))
        def _():
            wait_bytes(hop_recv.at[k], dst, n_dp, size)

    def collect(k, is_target, target_section, src, dst, size=None):
        def one(j, carry):
            t = (dp + j) % n_dp
            hop_send_copy(
                k, block_of(src, t, size), block_of(dst, me, size), target_section, t
            ).start()
            return carry

        @pl.when(is_target)
        def _():
            pltpu.make_async_copy(
                block_of(src, dp, size), block_of(dst, me, size), hop_local.at[k]
            ).start()

        lax.fori_loop(1, n_dp, one, 0)

        @pl.when(jnp.logical_not(is_target))
        def _():
            one(0, 0)

        @pl.when(is_target)
        def _():
            pltpu.make_async_copy(
                block_of(src, dp, size), block_of(dst, me, size), hop_local.at[k]
            ).wait()
            wait_bytes(hop_recv.at[k], dst, slots - 1, size)

    quarters = 2 * width // LANES
    halves = width // LANES
    qkv[...] = acc[...].astype(BF16)

    @pl.when(decoder)
    def _():
        for b in range(quarters):
            for a in range(keep):
                wide[pl.ds(b * keep + a, slots, stride=quarters * keep), :] = qkv[
                    a * slots : (a + 1) * slots, b * LANES : (b + 1) * LANES
                ].astype(F32)
        send1[...] = wide[...].astype(BF16).reshape(send1.shape)

    spread(0, decoder, send1, in1)

    first_in = in1[...].reshape(n_dp * quarters * keep, LANES)
    span_f = lax.broadcasted_iota(
        jnp.int32, (n_dp * EX_DEV, n_dp * quarters * keep), 1
    ).astype(F32)
    pieces = []
    for b in range(quarters):
        at = jnp.where(fidx_ref[:, :1] >= 0.0, fidx_ref[:, :1] + float(b * keep), -1.0)
        pick = jnp.where(span_f == at, 1.0, 0.0).astype(BF16)
        pieces += [nn(pick, first_in).reshape(n_dp, EX_DEV, LANES)]
    send2[...] = jnp.concatenate(pieces, axis=1).astype(BF16)
    collect(1, encoder, 0, send2, in2)

    @pl.when(encoder)
    def _():
        scale = 1.0 / float(HEAD) ** 0.5
        total = slots * EX_DEV
        incoming = in2[...].astype(F32)
        parts = [
            incoming[:, b * EX_DEV : (b + 1) * EX_DEV, :].reshape(total, LANES).astype(BF16)
            for b in range(quarters)
        ]
        example = (lax.broadcasted_iota(jnp.int32, (total, rows), 0) % EX_DEV).astype(F32)
        mask = example == rank_ref[:1, :]
        back = []
        for b in range(halves):
            both = []
            for s in range(LANES // HEAD):
                low = b * LANES + s * HEAD
                q = parts[b][:, s * HEAD : (s + 1) * HEAD]
                dout = parts[halves + b][:, s * HEAD : (s + 1) * HEAD]
                k = qkv[:, low : low + HEAD]
                v = qkv[:, width + low : width + low + HEAD]
                weight = jnp.where(mask, jnp.exp(nt(q, k) * scale), 0.0)
                probs = weight / jnp.sum(weight, axis=1, keepdims=True)
                probs_bf = probs.astype(BF16)
                attended = nn(probs_bf, v).astype(BF16)
                delta = jnp.sum(
                    dout.astype(F32) * attended.astype(F32), axis=1, keepdims=True
                )
                dscore = (probs * (nt(dout, v) - delta) * scale).astype(BF16)
                both += [nn(dscore, k)]
                grad[:, low : low + HEAD] = tn(dscore, q).astype(BF16)
                grad[:, width + low : width + low + HEAD] = tn(probs_bf, dout).astype(BF16)
            back += [jnp.concatenate(both, axis=1).reshape(slots, EX_DEV, LANES)]
        send3[...] = jnp.concatenate(back, axis=1).astype(BF16)

    spread(2, encoder, send3, in3)
    third_in = in3[...].reshape(n_dp * halves * EX_DEV, LANES)
    span_r = lax.broadcasted_iota(
        jnp.int32, (n_dp * halves * keep, n_dp * halves * EX_DEV), 1
    ).astype(F32)
    pick_r = jnp.where(span_r == ridx_ref[:, :1], 1.0, 0.0).astype(BF16)
    send4[...] = nn(pick_r, third_in)
    collect(3, decoder, 1, send4, in4, halves * keep)

    @pl.when(decoder)
    def _():
        for b in range(halves):
            for a in range(keep):
                grad[a * slots : (a + 1) * slots, b * LANES : (b + 1) * LANES] = in4[
                    pl.ds(b * keep + a, slots, stride=halves * keep), :
                ].astype(BF16)
        grad[:, width:] = jnp.zeros((rows, width), BF16)

    columns = features // n_mp
    share = jnp.sum(grad[...].astype(F32) * qkv[...].astype(F32), axis=1, keepdims=True)
    inverse = inv_ref[:, :1]
    slope = inverse * inverse * share * (1.0 / features)

    def term(owner):
        at = pl.ds(pl.multiple_of(owner * columns, columns), columns)
        raw = nt(grad[...], wall[at, :])
        return inverse * (raw * gain_ref[:, at]) - x_ref[:, at].astype(F32) * slope

    def sib_copy(o):
        return pltpu.make_async_remote_copy(
            src_ref=sib_send.at[o],
            dst_ref=sib_recv.at[o],
            send_sem=c_send.at[0],
            recv_sem=c_sib.at[o],
            device_id=(section, dp, sibling),
            device_id_type=MESH,
        )

    def x_copy(o):
        return pltpu.make_async_remote_copy(
            src_ref=x_send.at[o],
            dst_ref=x_recv.at[o],
            send_sem=c_send.at[1],
            recv_sem=c_x.at[o],
            device_id=(section, dp, (xx + o) % nx * 2 + core),
            device_id_type=MESH,
        )

    def to_sibling(o):
        sib_send[o] = term((xx + o) % nx * 2 + 1 - core).astype(BF16)
        sib_copy(o).start()

    turns = [o for o in (2, 1, 3, 0) if o < nx]
    to_sibling(turns[0])
    for k, o in enumerate(turns):
        if k + 1 < len(turns):
            to_sibling(turns[k + 1])
        own = term((xx + o) % nx * 2 + core)
        sib_copy(o).wait_recv()
        both = own + sib_recv[o].astype(F32)
        if o:
            x_send[o] = both.astype(BF16)
            x_copy(o).start()
        else:
            result = both
    for o in (1, 3, 2):
        if o < nx:
            x_copy(o).wait_recv()
            result = result + x_recv[o].astype(F32)
    out_ref[...] = result.astype(out_ref.dtype)

    for kind in order:
        for sign in (1, -1):
            for hop in range(1, half + 1):
                if exists(sign, kind, hop):
                    z_copy(sign, kind, hop, True).wait_send()
    y_copy("a", 1, 0, True).wait_send()
    for hop in range(half + 1):
        for sign in (1, -1):
            if (hop == 0 or hop == half) and sign == -1:
                continue
            y_copy("b", sign, hop, True).wait_send()

    @pl.when(decoder)
    def _():
        for o in range(1, 2 * nx):
            cot_copy(mp, o, sibling).wait_send()

    def sent(k, buf, count, size=None):
        wait_bytes(hop_send.at[k], buf, count, size)

    @pl.when(decoder)
    def _():
        sent(0, send1, slots - 1)
        sent(1, send2, n_dp)
        sent(3, send4, n_dp - 1, halves * keep)

    @pl.when(encoder)
    def _():
        sent(1, send2, n_dp - 1)
        sent(2, send3, slots - 1)
        sent(3, send4, n_dp, halves * keep)

    for o in range(nx):
        sib_copy(o).wait_send()
        if o:
            x_copy(o).wait_send()


def shards(n_dp, n_mp, layer_rows, cotangent, norm_gains, projections, enc_len, dec_len, enc_dev, dec_dev):
    x = layer_rows[0]
    rows, features = x.shape
    depth, _, width = projections.shape[1:]
    w = projections[0].reshape(depth, 2 * width)
    count = enc_len.shape[0]
    tab_r = jnp.stack([enc_len, dec_len, enc_dev, dec_dev]).astype(F32)
    tab_c = tab_r.T
    slots = 2 * n_dp
    keep = rows // slots
    quarters = 2 * width // LANES
    halves = width // LANES
    nx = n_mp // 2
    nz = n_dp // 2
    columns = features // n_mp
    vmem = pl.BlockSpec(memory_space=pltpu.VMEM)
    dma = pltpu.SemaphoreType.DMA
    out = pl.pallas_call(
        functools.partial(kernel, n_dp, n_mp),
        out_shape=jax.ShapeDtypeStruct((rows, columns), BF16),
        in_specs=[vmem] * 6,
        out_specs=vmem,
        scratch_shapes=[
            pltpu.VMEM((features, 2 * width), BF16),
            pltpu.VMEM((features // LANES, rows, LANES), BF16),
            pltpu.VMEM((features // LANES, rows, LANES), BF16),
            pltpu.VMEM((rows, LANES), F32),
            pltpu.VMEM((rows, 2 * width), F32),
            pltpu.VMEM((rows, 2 * width), BF16),
            pltpu.VMEM((rows, 2 * width), BF16),
            pltpu.VMEM((count, LANES), F32),
            pltpu.VMEM((n_dp * halves * keep, LANES), F32),
            pltpu.VMEM((8, rows), F32),
            pltpu.VMEM((slots * quarters * keep, LANES), F32),
            pltpu.VMEM((slots, quarters * keep, LANES), BF16),
            pltpu.VMEM((n_dp, quarters * keep, LANES), BF16),
            pltpu.VMEM((n_dp, quarters * EX_DEV, LANES), BF16),
            pltpu.VMEM((slots, quarters * EX_DEV, LANES), BF16),
            pltpu.VMEM((slots, halves * EX_DEV, LANES), BF16),
            pltpu.VMEM((n_dp, halves * EX_DEV, LANES), BF16),
            pltpu.VMEM((n_dp * halves * keep, LANES), F32),
            pltpu.VMEM((slots * halves * keep, LANES), F32),
            pltpu.VMEM((nx, rows, columns), BF16),
            pltpu.VMEM((nx, rows, columns), BF16),
            pltpu.VMEM((nx, rows, columns), BF16),
            pltpu.VMEM((nx, rows, columns), BF16),
            dma((2, 3, max(1, nz // 2))),
            dma((nz + 1,)),
            dma((2 * nx,)),
            dma,
            dma,
            dma((4,)),
            dma((4,)),
            dma((4,)),
            dma((2,)),
            dma((nx,)),
            dma((nx,)),
        ],
        compiler_params=pltpu.CompilerParams(
            collective_id=0, has_side_effects=True, vmem_limit_bytes=52 * 2**20
        ),
    )(x, norm_gains, w, cotangent, tab_r, tab_c)
    return out[None]


def solution(mesh):
    placed = (
        P("section", "dp", None),
        P("dp", "mp"),
        P("section", None),
        P("section", "dp", None, "mp"),
        P(),
        P(),
        P(),
        P(),
    )
    return jax.shard_map(
        functools.partial(shards, mesh.shape["dp"], mesh.shape["mp"]),
        mesh=mesh,
        in_specs=placed,
        out_specs=P("section", "dp", "mp"),
        check_vma=False,
    )
```

```python
import functools

import jax
import jax.numpy as jnp
from jax import lax
from jax.experimental import pallas as pl
from jax.experimental.pallas import tpu as pltpu
from jax.sharding import PartitionSpec as P

HEAD = 64
EX_DEV = 8
EPS = 1e-06
LANES = 128
CUT = 48
MESH = pl.DeviceIdType.MESH
F32 = jnp.float32
BF16 = jnp.bfloat16


def nt(a, b):
    return lax.dot_general(a, b, (((1,), (1,)), ((), ())), preferred_element_type=F32)


def tn(a, b):
    return lax.dot_general(a, b, (((0,), (0,)), ((), ())), preferred_element_type=F32)


def nn(a, b):
    return jnp.dot(a, b, preferred_element_type=F32)


def kernel(
    n_dp,
    n_mp,
    x_hbm,
    gain_hbm,
    w_hbm,
    cot_hbm,
    el_ref,
    dl_ref,
    ed_ref,
    dd_ref,
    out_ref,
    x_ref,
    gain_ref,
    w_ref,
    cot_ref,
    wall,
    left0,
    left1,
    inv_ref,
    acc,
    qkv,
    grad,
    pick_ref,
    pick_back,
    rank_ref,
    wide,
    send1,
    in1,
    send2,
    in2,
    send3,
    in3,
    send4,
    in4,
    sib_send,
    sib_recv,
    x_send,
    x_recv,
    in_sems,
    cross_sem,
    z_sems,
    y_sems,
    cot_sems,
    w_send_sem,
    cot_send_sem,
    hop_send,
    hop_recv,
    hop_local,
    c_send,
    c_sib,
    c_x,
):
    nz = n_dp // 2
    nx = n_mp // 2
    half = nz // 2
    slots = 2 * n_dp
    rows, features = x_ref.shape
    depth, _, width = w_ref.shape
    keep = rows // slots
    quarters = 2 * width // LANES
    halves = width // LANES
    section = lax.axis_index("section")
    dp = lax.axis_index("dp")
    mp = lax.axis_index("mp")
    yl = dp // nz
    z = dp % nz
    xx = mp // 2
    core = mp % 2
    me = section * n_dp + dp
    encoder = section == 0
    decoder = section == 1

    inputs = [
        pltpu.make_async_copy(source, target, in_sems.at[k])
        for k, (source, target) in enumerate(
            ((w_hbm, w_ref), (cot_hbm, cot_ref), (x_hbm, x_ref), (gain_hbm, gain_ref))
        )
    ]
    for copy in inputs:
        copy.start()

    sibling = xx * 2 + 1 - core
    across = 1 - section
    greeted = [(section, yl * nz + (z + 1) % nz, mp), (section, yl * nz + (z + nz - 1) % nz, mp)]
    greeted += [(section, (1 - yl) * nz + z, mp), (across, dp, mp), (section, dp, sibling)]
    greeted += [(section, dp, (xx + o) % nx * 2 + core) for o in range(1, nx)]
    barrier = pltpu.get_barrier_semaphore()
    for target in greeted:
        pl.semaphore_signal(barrier, inc=1, device_id=target, device_id_type=MESH)
    inputs[0].wait()
    own = pl.ds(pl.multiple_of(dp * depth, depth), depth)
    wall[own, :width] = w_ref[:, 0, :]
    wall[own, width:] = w_ref[:, 1, :]
    pl.semaphore_wait(barrier, len(greeted))

    spans = {"b": (CUT, depth - CUT), "a": (0, CUT), "o": (0, CUT)}
    order = ("b", "a", "o")

    def span(kind, y, zb):
        first, size = spans[kind]
        return wall.at[pl.ds(pl.multiple_of((y * nz + zb) * depth + first, 16), size), :]

    def exists(sign, kind, hop):
        if hop < half:
            return True
        return hop == half and ((kind == "b") == (sign == 1))

    def z_copy(sign, kind, hop, sending):
        y = 1 - yl if kind == "o" else yl
        back = hop - 1 if sending else hop
        part = span(kind, y, (z - sign * back + nz) % nz)
        return pltpu.make_async_remote_copy(
            src_ref=part,
            dst_ref=part,
            send_sem=w_send_sem,
            recv_sem=z_sems.at[(1 - sign) // 2, order.index(kind), hop - 1],
            device_id=(section, yl * nz + (z + sign + nz) % nz, mp),
            device_id_type=MESH,
        )

    def y_slot(sign, hop):
        if hop == 0:
            return 0
        return hop if sign == 1 else half + hop

    def y_copy(kind, sign, hop, sending):
        y = yl if sending else 1 - yl
        part = span(kind, y, (z - sign * hop + nz) % nz)
        slot = nz if kind == "a" else y_slot(sign, hop)
        return pltpu.make_async_remote_copy(
            src_ref=part,
            dst_ref=part,
            send_sem=w_send_sem,
            recv_sem=y_sems.at[slot],
            device_id=(section, (1 - yl) * nz + z, mp),
            device_id_type=MESH,
        )

    for kind in ("b", "a"):
        for sign in (1, -1):
            if exists(sign, kind, 1):
                z_copy(sign, kind, 1, True).start()
        y_copy("a" if kind == "b" else "b", 1, 0, True).start()

    per_mp = features // n_mp // LANES

    def cot_copy(owner, slot, target):
        part = left1.at[pl.ds(owner * per_mp, per_mp)]
        return pltpu.make_async_remote_copy(
            src_ref=part,
            dst_ref=part,
            send_sem=cot_send_sem,
            recv_sem=cot_sems.at[slot],
            device_id=(section, dp, target),
            device_id_type=MESH,
        )

    inputs[1].wait()

    @pl.when(decoder)
    def _():
        for c in range(per_mp):
            left1[mp * per_mp + c] = cot_ref[:, c * LANES : (c + 1) * LANES]
        for o in (2, 1, 3):
            if o < nx:
                cot_copy(mp, o, (xx + o) % nx * 2 + core).start()
        cot_copy(mp, nx, sibling).start()

    y_copy("a", 1, 0, False).wait_recv()
    for sign in (1, -1):
        if exists(sign, "o", 1):
            z_copy(sign, "o", 1, True).start()

    step = 32 if rows % 32 == 0 else rows

    def norm_rows(i):
        at = pl.ds(i * step, step)
        values = x_ref[at, :].astype(F32)
        inverse = lax.rsqrt(jnp.mean(values * values, axis=1, keepdims=True) + EPS)
        inv_ref[at, :] = jnp.broadcast_to(inverse, (step, LANES))
        normed = (values * inverse * gain_ref[...]).astype(BF16)
        for c in range(features // LANES):
            left0[c, at, :] = normed[:, c * LANES : (c + 1) * LANES]

        @pl.when(encoder)
        def _():
            for c in range(features // LANES):
                left1[c, at, :] = normed[:, c * LANES : (c + 1) * LANES]

    count = EX_DEV * n_dp
    el_r, dl_r, ed_r, dd_r = (t[...].astype(F32) for t in (el_ref, dl_ref, ed_ref, dd_ref))
    found = {}

    def starts():
        shape = (count, count)
        down = lax.broadcasted_iota(jnp.int32, shape, 0).astype(F32)
        along = lax.broadcasted_iota(jnp.int32, shape, 1).astype(F32)

        def column(row):
            return jnp.sum(jnp.where(down == along, row, 0.0), axis=1, keepdims=True)

        el_c, dl_c, ed_c, dd_c = (column(t) for t in (el_r, dl_r, ed_r, dd_r))
        same_enc = ed_r == ed_c
        same_dec = dd_r == dd_c
        one = jnp.ones(shape, F32)
        dstart_r = jnp.sum(
            jnp.where(same_dec & (down < along), dl_c * one, 0.0), axis=0, keepdims=True
        )
        rank_r = jnp.sum(jnp.where(same_enc & (down < along), one, 0.0), axis=0, keepdims=True)
        estart_c = jnp.sum(
            jnp.where(same_enc & (along < down), el_r * one, 0.0), axis=1, keepdims=True
        )
        rank_c = jnp.sum(jnp.where(same_enc & (along < down), one, 0.0), axis=1, keepdims=True)
        found.update(down=down, dstart_r=dstart_r, rank_r=rank_r)
        u_r = lax.broadcasted_iota(jnp.int32, (count, rows), 1).astype(F32)
        mine = (ed_c == dp.astype(F32)) & (estart_c <= u_r) & (u_r < estart_c + el_c)
        rank_u = jnp.sum(jnp.where(mine, rank_c * jnp.ones_like(u_r), 0.0), axis=0, keepdims=True)
        rank_ref[...] = jnp.broadcast_to(rank_u, rank_ref.shape)

    def pick_rows():
        start_i = found["dstart_r"].astype(jnp.int32)
        offset = (me - start_i) & (slots - 1)
        slot = (start_i + offset) // slots
        source = dd_r * float(quarters * keep) + slot.astype(F32)
        value = jnp.where(offset.astype(F32) < dl_r, source + 1.0, 0.0)
        place = ed_r * float(EX_DEV) + found["rank_r"]
        down = found["down"]
        found["fidx"] = (
            jnp.sum(jnp.where(place == down, value * jnp.ones_like(down), 0.0), axis=1, keepdims=True)
            - 1.0
        )

    def pick_side(b):
        fidx = found["fidx"]
        place = lax.broadcasted_iota(
            jnp.int32, (n_dp * EX_DEV, n_dp * quarters * keep), 1
        ).astype(F32)
        at = jnp.where(fidx >= 0.0, fidx + float(b * keep), -1.0)
        pick_ref[b] = jnp.where(place == at, 1.0, 0.0).astype(BF16)

    def pick_back_rows():
        q_i = lax.broadcasted_iota(jnp.int32, (n_dp * halves * keep, count), 0)
        dev_q = (q_i // (halves * keep)).astype(F32)
        side_q = (q_i % (halves * keep) // keep).astype(F32)
        row_q = (q_i % keep * slots + me).astype(F32)
        dstart_r = found["dstart_r"]
        hit = (dd_r == dev_q) & (dstart_r <= row_q) & (row_q < dstart_r + dl_r)
        target = (
            ed_r * float(halves * EX_DEV) + found["rank_r"] + side_q * float(EX_DEV) + 1.0
        )
        ridx = jnp.sum(jnp.where(hit, target, 0.0), axis=1, keepdims=True) - 1.0
        place = lax.broadcasted_iota(
            jnp.int32, (n_dp * halves * keep, n_dp * halves * EX_DEV), 1
        ).astype(F32)
        pick_back[...] = jnp.where(place == ridx, 1.0, 0.0).astype(BF16)

    def product(y, zb):
        total0 = total1 = None
        for row in (y, 1 - y):
            block = row * nz + zb
            at = pl.ds(pl.multiple_of(block * depth, depth), depth)
            p0 = nn(left0[block], wall[at, :width])
            p1 = nn(left1[block], wall[at, width:])
            total0 = p0 if total0 is None else total0 + p0
            total1 = p1 if total1 is None else total1 + p1
        acc[:, :width] += total0
        acc[:, width:] += total1

    def arrived(sign, hop):
        y_copy("b", sign, hop, False).wait_recv()
        product(yl, (z - sign * hop + nz) % nz)

    def cot_pass(o):
        @pl.when(decoder)
        def _():
            owner = (xx - o + nx) % nx * 2 + core
            cot_copy(owner, o, sibling).wait_recv()
            cot_copy(owner, nx + o, sibling).start()

    def cot_wait():
        @pl.when(decoder)
        def _():
            for o in range(nx):
                owner = (xx - o + nx) % nx * 2 + 1 - core
                cot_copy(owner, nx + o, sibling).wait_recv()

    def first_norm():
        inputs[2].wait()
        inputs[3].wait()
        norm_rows(0)

    acc[...] = jnp.zeros_like(acc)
    items = [first_norm] + [functools.partial(norm_rows, i) for i in range(1, rows // step)]
    items += [starts, pick_rows] + [functools.partial(pick_side, b) for b in range(quarters)]
    items += [pick_back_rows]
    late = [functools.partial(cot_pass, o) for o in (1, 3, 2) if o < nx] + [cot_wait]
    late += [functools.partial(arrived, 1, 0)]
    for hop in range(1, half + 1):
        if hop == max(1, half - 3):
            items += late
            late = []
        for kind in order:
            for sign in (1, -1):
                if exists(sign, kind, hop):
                    z_copy(sign, kind, hop, False).wait_recv()
                    if exists(sign, kind, hop + 1):
                        z_copy(sign, kind, hop + 1, True).start()
                    if kind == "b":
                        y_copy("b", sign, hop, True).start()
                    if items:
                        items.pop(0)()
        for sign in (1, -1) if hop < half else (1,):
            (late if late else items).append(functools.partial(arrived, sign, hop))
    for item in items:
        item()

    pl.semaphore_signal(cross_sem, inc=1, device_id=(across, dp, mp), device_id_type=MESH)
    pl.semaphore_wait(cross_sem, 1)

    def hop_send_copy(k, src, dst, target_section, target_dp):
        return pltpu.make_async_remote_copy(
            src_ref=src,
            dst_ref=dst,
            send_sem=hop_send.at[k],
            recv_sem=hop_recv.at[k],
            device_id=(target_section, target_dp, mp),
            device_id_type=MESH,
        )

    def block_of(buf, i, size):
        if size is None:
            return buf.at[i]
        return buf.at[pl.ds(pl.multiple_of(i * size, size), size)]

    def wait_bytes(sem, buf, count, size):
        part = buf.at[pl.ds(0, count if size is None else count * size)]
        pltpu.make_async_copy(part, part, sem).wait()

    def spread(k, is_source, src, dst, size=None):
        @pl.when(is_source)
        def _():
            pltpu.make_async_copy(
                block_of(src, me, size), block_of(dst, dp, size), hop_local.at[k]
            ).start()

            run = 9 if (slots - 1) % 9 == 0 else 1

            def some(g, carry):
                for r in range(run):
                    i = (me + 1 + g * run + r) & (slots - 1)
                    hop_send_copy(
                        k,
                        block_of(src, i, size),
                        block_of(dst, dp, size),
                        i // n_dp,
                        i & (n_dp - 1),
                    ).start()
                return carry

            lax.fori_loop(0, (slots - 1) // run, some, 0)
            pltpu.make_async_copy(
                block_of(src, me, size), block_of(dst, dp, size), hop_local.at[k]
            ).wait()
            wait_bytes(hop_recv.at[k], dst, n_dp - 1, size)

        @pl.when(jnp.logical_not(is_source))
        def _():
            wait_bytes(hop_recv.at[k], dst, n_dp, size)

    def collect(k, is_target, target_section, src, dst, size=None):
        def one(j):
            t = (dp + j) & (n_dp - 1)
            hop_send_copy(
                k, block_of(src, t, size), block_of(dst, me, size), target_section, t
            ).start()

        run = 10 if (n_dp - 2) % 10 == 0 else 1

        def some(g, carry):
            for r in range(run):
                one(1 + g * run + r)
            return carry

        @pl.when(is_target)
        def _():
            pltpu.make_async_copy(
                block_of(src, dp, size), block_of(dst, me, size), hop_local.at[k]
            ).start()

        lax.fori_loop(0, (n_dp - 2) // run, some, 0)
        one(n_dp - 1)

        @pl.when(jnp.logical_not(is_target))
        def _():
            one(0)

        @pl.when(is_target)
        def _():
            pltpu.make_async_copy(
                block_of(src, dp, size), block_of(dst, me, size), hop_local.at[k]
            ).wait()
            wait_bytes(hop_recv.at[k], dst, slots - 1, size)

    qkv[...] = acc[...].astype(BF16)

    @pl.when(decoder)
    def _():
        for b in range(quarters):
            for a in range(keep):
                wide[pl.ds(b * keep + a, slots, stride=quarters * keep), :] = qkv[
                    a * slots : (a + 1) * slots, b * LANES : (b + 1) * LANES
                ].astype(F32)
        send1[...] = wide[...].astype(BF16).reshape(send1.shape)

    spread(0, decoder, send1, in1)

    first_in = in1[...].reshape(n_dp * quarters * keep, LANES)
    pieces = [nn(pick_ref[b], first_in).reshape(n_dp, EX_DEV, LANES) for b in range(quarters)]
    send2[...] = jnp.concatenate(pieces, axis=1).astype(BF16)
    collect(1, encoder, 0, send2, in2)

    @pl.when(encoder)
    def _():
        scale = 1.0 / float(HEAD) ** 0.5
        total = slots * EX_DEV
        incoming = in2[...].astype(F32)
        parts = [
            incoming[:, b * EX_DEV : (b + 1) * EX_DEV, :].reshape(total, LANES).astype(BF16)
            for b in range(quarters)
        ]
        example = (lax.broadcasted_iota(jnp.int32, (total, rows), 0) % EX_DEV).astype(F32)
        mask = example == rank_ref[:1, :]
        back = []
        lane = lax.broadcasted_iota(jnp.int32, (1, LANES), 1) // HEAD
        for b in range(halves):
            q, dout = parts[b], parts[halves + b]
            k = qkv[:, b * LANES : (b + 1) * LANES]
            v = qkv[:, width + b * LANES : width + (b + 1) * LANES]
            sums = []
            for s in range(LANES // HEAD):
                here = lane == s
                q_s = jnp.where(here, q, jnp.zeros_like(q))
                dout_s = jnp.where(here, dout, jnp.zeros_like(dout))
                weight = jnp.where(mask, jnp.exp(nt(q_s, k) * scale), 0.0)
                probs = weight * (1.0 / jnp.sum(weight, axis=1, keepdims=True))
                probs_bf = probs.astype(BF16)
                attended = nn(probs_bf, v).astype(BF16)
                delta = jnp.sum(
                    dout_s.astype(F32) * attended.astype(F32), axis=1, keepdims=True
                )
                dscore = (probs * (nt(dout_s, v) - delta) * scale).astype(BF16)
                news = (nn(dscore, k), tn(dscore, q), tn(probs_bf, dout))
                sums = [jnp.where(here, new, old) for new, old in zip(news, sums)] if s else news
            grad[:, b * LANES : (b + 1) * LANES] = sums[1].astype(BF16)
            grad[:, width + b * LANES : width + (b + 1) * LANES] = sums[2].astype(BF16)
            back += [sums[0].reshape(slots, EX_DEV, LANES)]
        send3[...] = jnp.concatenate(back, axis=1).astype(BF16)

    spread(2, encoder, send3, in3)
    third_in = in3[...].reshape(n_dp * halves * EX_DEV, LANES)
    send4[...] = nn(pick_back[...], third_in)
    collect(3, decoder, 1, send4, in4, halves * keep)

    @pl.when(decoder)
    def _():
        for b in range(halves):
            for a in range(keep):
                grad[a * slots : (a + 1) * slots, b * LANES : (b + 1) * LANES] = in4[
                    pl.ds(b * keep + a, slots, stride=halves * keep), :
                ].astype(BF16)
        grad[:, width:] = jnp.zeros((rows, width), BF16)

    columns = features // n_mp
    share = jnp.sum(grad[...].astype(F32) * qkv[...].astype(F32), axis=1, keepdims=True)
    inverse = inv_ref[:, :1]
    slope = inverse * inverse * share * (1.0 / features)

    def term(owner):
        at = pl.ds(pl.multiple_of(owner * columns, columns), columns)
        raw = nt(grad[...], wall[at, :])
        return inverse * (raw * gain_ref[:, at]) - x_ref[:, at].astype(F32) * slope

    def sib_copy(o):
        return pltpu.make_async_remote_copy(
            src_ref=sib_send.at[o],
            dst_ref=sib_recv.at[o],
            send_sem=c_send.at[0],
            recv_sem=c_sib.at[o],
            device_id=(section, dp, sibling),
            device_id_type=MESH,
        )

    def to_sibling(o):
        sib_send[o] = term((xx + o) % nx * 2 + 1 - core).astype(BF16)
        sib_copy(o).start()

    def combined(o):
        own_term = term((xx + o) % nx * 2 + core)
        sib_copy(o).wait_recv()
        return own_term + sib_recv[o].astype(F32)

    def part_copy(slot, o, low, size, sign):
        return pltpu.make_async_remote_copy(
            src_ref=x_send.at[o, pl.ds(low, size), :],
            dst_ref=x_recv.at[o, pl.ds(low, size), :],
            send_sem=c_send.at[1],
            recv_sem=c_x.at[slot],
            device_id=(section, dp, (xx + sign + nx) % nx * 2 + core),
            device_id_type=MESH,
        )

    middle = rows // 2
    parts_sent = []
    if nx == 4:
        far_up = part_copy(0, 2, 0, middle, 1)
        far_down = part_copy(1, 2, middle, middle, -1)
        up_plain = part_copy(2, 1, middle, middle, 1)
        up_added = part_copy(3, 1, 0, middle, 1)
        down_plain = part_copy(4, 3, 0, middle, -1)
        down_added = part_copy(5, 3, middle, middle, -1)
        parts_sent = [far_up, far_down, up_plain, up_added, down_plain, down_added]
        to_sibling(2)
        to_sibling(1)
        x_send[2] = combined(2).astype(BF16)
        far_up.start()
        far_down.start()
        to_sibling(3)
        up = combined(1)
        x_send[1, middle:, :] = up[middle:].astype(BF16)
        up_plain.start()
        to_sibling(0)
        down = combined(3)
        x_send[3, :middle, :] = down[:middle].astype(BF16)
        down_plain.start()
        far_up.wait_recv()
        x_send[1, :middle, :] = (up[:middle] + x_recv[2, :middle, :].astype(F32)).astype(BF16)
        up_added.start()
        far_down.wait_recv()
        x_send[3, middle:, :] = (down[middle:] + x_recv[2, middle:, :].astype(F32)).astype(BF16)
        down_added.start()
        result = combined(0)
        for copy in (up_plain, down_plain, up_added, down_added):
            copy.wait_recv()
        result = result + x_recv[1].astype(F32) + x_recv[3].astype(F32)
    else:
        turns = [o for o in (1, 0) if o < nx]
        to_sibling(turns[0])
        for k, o in enumerate(turns):
            if k + 1 < len(turns):
                to_sibling(turns[k + 1])
            result = combined(o)
            if o:
                x_send[o] = result.astype(BF16)
                whole = part_copy(0, 1, 0, rows, 1)
                whole.start()
                parts_sent += [whole]
        for copy in parts_sent:
            copy.wait_recv()
            result = result + x_recv[1].astype(F32)
    out_ref[...] = result.astype(out_ref.dtype)

    for kind in order:
        for sign in (1, -1):
            for hop in range(1, half + 1):
                if exists(sign, kind, hop):
                    z_copy(sign, kind, hop, True).wait_send()
    y_copy("a", 1, 0, True).wait_send()
    for hop in range(half + 1):
        for sign in (1, -1):
            if (hop == 0 or hop == half) and sign == -1:
                continue
            y_copy("b", sign, hop, True).wait_send()

    @pl.when(decoder)
    def _():
        for o in range(1, 2 * nx):
            cot_copy(mp, o, sibling).wait_send()

    def sent(k, buf, count, size=None):
        wait_bytes(hop_send.at[k], buf, count, size)

    @pl.when(decoder)
    def _():
        sent(0, send1, slots - 1)
        sent(1, send2, n_dp)
        sent(3, send4, n_dp - 1, halves * keep)

    @pl.when(encoder)
    def _():
        sent(1, send2, n_dp - 1)
        sent(2, send3, slots - 1)
        sent(3, send4, n_dp, halves * keep)

    for o in range(nx):
        sib_copy(o).wait_send()
    for copy in parts_sent:
        copy.wait_send()


def shards(n_dp, n_mp, layer_rows, cotangent, norm_gains, projections, enc_len, dec_len, enc_dev, dec_dev):
    x = layer_rows[0]
    rows, features = x.shape
    depth, _, width = projections.shape[1:]
    count = enc_len.shape[0]
    tables = [t.reshape(1, count) for t in (enc_len, dec_len, enc_dev, dec_dev)]
    slots = 2 * n_dp
    keep = rows // slots
    quarters = 2 * width // LANES
    halves = width // LANES
    nx = n_mp // 2
    nz = n_dp // 2
    columns = features // n_mp
    vmem = pl.BlockSpec(memory_space=pltpu.VMEM)
    hbm = pl.BlockSpec(memory_space=pl.ANY)
    dma = pltpu.SemaphoreType.DMA
    out = pl.pallas_call(
        functools.partial(kernel, n_dp, n_mp),
        out_shape=jax.ShapeDtypeStruct((rows, columns), BF16),
        in_specs=[hbm] * 4 + [vmem] * 4,
        out_specs=vmem,
        scratch_shapes=[
            pltpu.VMEM((rows, features), BF16),
            pltpu.VMEM((1, features), F32),
            pltpu.VMEM((depth, 2, width), BF16),
            pltpu.VMEM((rows, columns), BF16),
            pltpu.VMEM((features, 2 * width), BF16),
            pltpu.VMEM((features // LANES, rows, LANES), BF16),
            pltpu.VMEM((features // LANES, rows, LANES), BF16),
            pltpu.VMEM((rows, LANES), F32),
            pltpu.VMEM((rows, 2 * width), F32),
            pltpu.VMEM((rows, 2 * width), BF16),
            pltpu.VMEM((rows, 2 * width), BF16),
            pltpu.VMEM((quarters, count, n_dp * quarters * keep), BF16),
            pltpu.VMEM((n_dp * halves * keep, n_dp * halves * EX_DEV), BF16),
            pltpu.VMEM((8, rows), F32),
            pltpu.VMEM((slots * quarters * keep, LANES), F32),
            pltpu.VMEM((slots, quarters * keep, LANES), BF16),
            pltpu.VMEM((n_dp, quarters * keep, LANES), BF16),
            pltpu.VMEM((n_dp, quarters * EX_DEV, LANES), BF16),
            pltpu.VMEM((slots, quarters * EX_DEV, LANES), BF16),
            pltpu.VMEM((slots, halves * EX_DEV, LANES), BF16),
            pltpu.VMEM((n_dp, halves * EX_DEV, LANES), BF16),
            pltpu.VMEM((n_dp * halves * keep, LANES), F32),
            pltpu.VMEM((slots * halves * keep, LANES), F32),
            pltpu.VMEM((nx, rows, columns), BF16),
            pltpu.VMEM((nx, rows, columns), BF16),
            pltpu.VMEM((nx, rows, columns), BF16),
            pltpu.VMEM((nx, rows, columns), BF16),
            dma((4,)),
            pltpu.SemaphoreType.REGULAR,
            dma((2, 3, max(1, nz // 2))),
            dma((nz + 1,)),
            dma((2 * nx,)),
            dma,
            dma,
            dma((4,)),
            dma((4,)),
            dma((4,)),
            dma((2,)),
            dma((nx,)),
            dma((6,)),
        ],
        compiler_params=pltpu.CompilerParams(
            collective_id=0, has_side_effects=True, vmem_limit_bytes=60 * 2**20
        ),
    )(x, norm_gains, projections[0], cotangent, *tables)
    return out[None]


def solution(mesh):
    placed = (
        P("section", "dp", None),
        P("dp", "mp"),
        P("section", None),
        P("section", "dp", None, "mp"),
        P(),
        P(),
        P(),
        P(),
    )
    return jax.shard_map(
        functools.partial(shards, mesh.shape["dp"], mesh.shape["mp"]),
        mesh=mesh,
        in_specs=placed,
        out_specs=P("section", "dp", "mp"),
        check_vma=False,
    )
```

```python
import functools

import jax
import jax.numpy as jnp
from jax import lax
from jax.experimental import pallas as pl
from jax.experimental.pallas import tpu as pltpu
from jax.sharding import PartitionSpec as P

HEAD = 64
EX_DEV = 8
EPS = 1e-06
LANES = 128
CUT = 64
MESH = pl.DeviceIdType.MESH
F32 = jnp.float32
BF16 = jnp.bfloat16


def nt(a, b):
    return lax.dot_general(a, b, (((1,), (1,)), ((), ())), preferred_element_type=F32)


def tn(a, b):
    return lax.dot_general(a, b, (((0,), (0,)), ((), ())), preferred_element_type=F32)


def nn(a, b):
    return jnp.dot(a, b, preferred_element_type=F32)


def kernel(
    n_dp,
    n_mp,
    x_hbm,
    gain_hbm,
    w_hbm,
    cot_hbm,
    el_ref,
    dl_ref,
    ed_ref,
    dd_ref,
    out_ref,
    x_ref,
    gain_ref,
    w_ref,
    cot_ref,
    wall,
    left0,
    left1,
    inv_ref,
    acc,
    qkv,
    grad,
    pick_ref,
    own_ref,
    far_ref,
    probs_ref,
    wide,
    send1,
    in1,
    send2,
    in2,
    sib_send,
    sib_recv,
    x_send,
    x_recv,
    in_sems,
    cross_sem,
    z_sems,
    y_sems,
    cot_sems,
    w_send_sem,
    cot_send_sem,
    hop_send,
    hop_recv,
    hop_local,
    c_send,
    c_sib,
    c_x,
):
    nz = n_dp // 2
    nx = n_mp // 2
    half = nz // 2
    rows, features = x_ref.shape
    depth, _, width = w_ref.shape
    keep = rows // n_dp
    turns = 2 * rows // EX_DEV // n_dp
    sides = width // LANES
    section = lax.axis_index("section")
    dp = lax.axis_index("dp")
    mp = lax.axis_index("mp")
    yl = dp // nz
    z = dp % nz
    xx = mp // 2
    core = mp % 2
    encoder = section == 0
    decoder = section == 1

    inputs = [
        pltpu.make_async_copy(source, target, in_sems.at[k])
        for k, (source, target) in enumerate(
            ((w_hbm, w_ref), (cot_hbm, cot_ref), (x_hbm, x_ref), (gain_hbm, gain_ref))
        )
    ]
    for copy in inputs:
        copy.start()

    sibling = xx * 2 + 1 - core
    across = 1 - section
    greeted = [(section, yl * nz + (z + 1) % nz, mp), (section, yl * nz + (z + nz - 1) % nz, mp)]
    greeted += [(section, (1 - yl) * nz + z, mp), (across, dp, mp), (section, dp, sibling)]
    greeted += [(section, dp, (xx + o) % nx * 2 + core) for o in range(1, nx)]
    barrier = pltpu.get_barrier_semaphore()
    for target in greeted:
        pl.semaphore_signal(barrier, inc=1, device_id=target, device_id_type=MESH)
    inputs[0].wait()
    own = pl.ds(pl.multiple_of(dp * depth, depth), depth)
    wall[own, :width] = w_ref[:, 0, :]
    wall[own, width:] = w_ref[:, 1, :]
    pl.semaphore_wait(barrier, len(greeted))

    spans = {"b": (CUT, depth - CUT), "a": (0, CUT), "o": (0, CUT)}
    order = ("b", "a", "o")

    def span(kind, y, zb):
        first, size = spans[kind]
        return wall.at[pl.ds(pl.multiple_of((y * nz + zb) * depth + first, 16), size), :]

    def exists(sign, kind, hop):
        if hop < half:
            return True
        return hop == half and ((kind == "b") == (sign == 1))

    def z_copy(sign, kind, hop, sending):
        y = 1 - yl if kind == "o" else yl
        back = hop - 1 if sending else hop
        part = span(kind, y, (z - sign * back + nz) % nz)
        return pltpu.make_async_remote_copy(
            src_ref=part,
            dst_ref=part,
            send_sem=w_send_sem,
            recv_sem=z_sems.at[(1 - sign) // 2, order.index(kind), hop - 1],
            device_id=(section, yl * nz + (z + sign + nz) % nz, mp),
            device_id_type=MESH,
        )

    def y_slot(sign, hop):
        if hop == 0:
            return 0
        return hop if sign == 1 else half + hop

    def y_copy(kind, sign, hop, sending):
        y = yl if sending else 1 - yl
        part = span(kind, y, (z - sign * hop + nz) % nz)
        slot = nz if kind == "a" else y_slot(sign, hop)
        return pltpu.make_async_remote_copy(
            src_ref=part,
            dst_ref=part,
            send_sem=w_send_sem,
            recv_sem=y_sems.at[slot],
            device_id=(section, (1 - yl) * nz + z, mp),
            device_id_type=MESH,
        )

    for kind in ("b", "a"):
        for sign in (1, -1):
            if exists(sign, kind, 1):
                z_copy(sign, kind, 1, True).start()
        y_copy("a" if kind == "b" else "b", 1, 0, True).start()

    per_mp = features // n_mp // LANES

    def cot_copy(owner, slot, target):
        part = left1.at[pl.ds(owner * per_mp, per_mp)]
        return pltpu.make_async_remote_copy(
            src_ref=part,
            dst_ref=part,
            send_sem=cot_send_sem,
            recv_sem=cot_sems.at[slot],
            device_id=(section, dp, target),
            device_id_type=MESH,
        )

    inputs[1].wait()

    @pl.when(decoder)
    def _():
        for c in range(per_mp):
            left1[mp * per_mp + c] = cot_ref[:, c * LANES : (c + 1) * LANES]
        for o in (2, 1, 3):
            if o < nx:
                cot_copy(mp, o, (xx + o) % nx * 2 + core).start()
        cot_copy(mp, nx, sibling).start()

    y_copy("a", 1, 0, False).wait_recv()
    for sign in (1, -1):
        if exists(sign, "o", 1):
            z_copy(sign, "o", 1, True).start()

    step = 32 if rows % 32 == 0 else rows

    def norm_rows(i):
        at = pl.ds(i * step, step)
        values = x_ref[at, :].astype(F32)
        inverse = lax.rsqrt(jnp.mean(values * values, axis=1, keepdims=True) + EPS)
        inv_ref[at, :] = jnp.broadcast_to(inverse, (step, LANES))
        normed = (values * inverse * gain_ref[...]).astype(BF16)
        for c in range(features // LANES):
            left0[c, at, :] = normed[:, c * LANES : (c + 1) * LANES]

        @pl.when(encoder)
        def _():
            for c in range(features // LANES):
                left1[c, at, :] = normed[:, c * LANES : (c + 1) * LANES]

    count = EX_DEV * n_dp
    far_rows = n_dp * turns * EX_DEV
    enc_r = tuple(t[...].astype(F32) for t in (el_ref, ed_ref))
    dec_r = tuple(t[...].astype(F32) for t in (dl_ref, dd_ref))
    len_r, dev_r = (jnp.where(encoder, a, b) for a, b in zip(enc_r, dec_r))
    far_len_r, far_dev_r = (jnp.where(encoder, b, a) for a, b in zip(enc_r, dec_r))
    here = dp.astype(F32)
    found = {}

    def starts():
        shape = (count, count)
        down = lax.broadcasted_iota(jnp.int32, shape, 0).astype(F32)
        along = lax.broadcasted_iota(jnp.int32, shape, 1).astype(F32)
        one = jnp.ones(shape, F32)

        def column(row):
            return jnp.sum(jnp.where(down == along, row, 0.0), axis=1, keepdims=True)

        len_c, dev_c, far_len_c, far_dev_c = (
            column(t) for t in (len_r, dev_r, far_len_r, far_dev_r)
        )
        above = (dev_r == dev_c) & (down < along)
        before = (dev_r == dev_c) & (along < down)
        found.update(
            down=down,
            len_c=len_c,
            dev_c=dev_c,
            far_len_c=far_len_c,
            start_r=jnp.sum(jnp.where(above, len_c * one, 0.0), axis=0, keepdims=True),
            rank_r=jnp.sum(jnp.where(above, one, 0.0), axis=0, keepdims=True),
            start_c=jnp.sum(jnp.where(before, len_r * one, 0.0), axis=1, keepdims=True),
            rank_c=jnp.sum(jnp.where(before, one, 0.0), axis=1, keepdims=True),
            far_rank_r=jnp.sum(
                jnp.where((far_dev_r == far_dev_c) & (down < along), one, 0.0),
                axis=0,
                keepdims=True,
            ),
            far_start_c=jnp.sum(
                jnp.where((far_dev_r == far_dev_c) & (along < down), far_len_r * one, 0.0),
                axis=1,
                keepdims=True,
            ),
        )

    def own_ranks():
        u_r = lax.broadcasted_iota(jnp.int32, (count, rows), 1).astype(F32)
        start_c, start_r = found["start_c"], found["start_r"]
        mine = (found["dev_c"] == here) & (start_c <= u_r) & (u_r < start_c + found["len_c"])
        along = jnp.sum(
            jnp.where(mine, found["rank_c"] * jnp.ones_like(u_r), 0.0), axis=0, keepdims=True
        )
        u_c = lax.broadcasted_iota(jnp.int32, (rows, count), 0).astype(F32)
        mine = (dev_r == here) & (start_r <= u_c) & (u_c < start_r + len_r)
        down = jnp.sum(
            jnp.where(mine, found["rank_r"] * jnp.ones_like(u_c), 0.0), axis=1, keepdims=True
        )
        far_ref[:, :rows] = jnp.broadcast_to(along, (far_ref.shape[0], rows))
        own_ref[...] = jnp.broadcast_to(down, own_ref.shape)

    def far_ranks():
        c_i = lax.broadcasted_iota(jnp.int32, (count, far_rows), 1)
        rank = (c_i % EX_DEV).astype(F32)
        hit = (found["dev_c"] == here) & (found["rank_c"] == rank)
        one = jnp.ones_like(rank)
        start = jnp.sum(jnp.where(hit, found["far_start_c"] * one, 0.0), axis=0, keepdims=True)
        length = jnp.sum(jnp.where(hit, found["far_len_c"] * one, 0.0), axis=0, keepdims=True)
        c_r = lax.broadcasted_iota(jnp.int32, (1, far_rows), 1)
        offset = (c_r // (turns * EX_DEV) - start.astype(jnp.int32)) & (n_dp - 1)
        offset = offset + c_r % (turns * EX_DEV) // EX_DEV * n_dp
        rank_r = jnp.where(offset.astype(F32) < length, (c_r % EX_DEV).astype(F32), -1.0)

        @pl.when(decoder)
        def _():
            far_ref[...] = jnp.broadcast_to(rank_r, far_ref.shape)

    def pick_rows(turn):
        start_i = found["start_r"].astype(jnp.int32)
        offset = ((dp - start_i) & (n_dp - 1)) + turn * n_dp
        source = dev_r * float(sides * keep) + ((start_i + offset) // n_dp).astype(F32)
        value = jnp.where(offset.astype(F32) < len_r, source + 1.0, 0.0)
        place = far_dev_r * float(EX_DEV) + found["far_rank_r"]
        down = found["down"]
        one = jnp.ones_like(down)
        found[turn] = (
            jnp.sum(jnp.where(place == down, value * one, 0.0), axis=1, keepdims=True) - 1.0
        )

    def pick_side(b, turn):
        fidx = found[turn]
        place = lax.broadcasted_iota(jnp.int32, (count, n_dp * sides * keep), 1).astype(F32)
        at = jnp.where(fidx >= 0.0, fidx + float(b * keep), -1.0)
        pick_ref[b * turns + turn] = jnp.where(place == at, 1.0, 0.0).astype(BF16)

    def product(y, zb):
        total0 = total1 = None
        for row in (y, 1 - y):
            block = row * nz + zb
            at = pl.ds(pl.multiple_of(block * depth, depth), depth)
            p0 = nn(left0[block], wall[at, :width])
            p1 = nn(left1[block], wall[at, width:])
            total0 = p0 if total0 is None else total0 + p0
            total1 = p1 if total1 is None else total1 + p1
        acc[:, :width] += total0
        acc[:, width:] += total1

    def arrived(sign, hop):
        y_copy("b", sign, hop, False).wait_recv()
        product(yl, (z - sign * hop + nz) % nz)

    def cot_pass(o):
        @pl.when(decoder)
        def _():
            owner = (xx - o + nx) % nx * 2 + core
            cot_copy(owner, o, sibling).wait_recv()
            cot_copy(owner, nx + o, sibling).start()

    def cot_wait():
        @pl.when(decoder)
        def _():
            for o in range(nx):
                owner = (xx - o + nx) % nx * 2 + 1 - core
                cot_copy(owner, nx + o, sibling).wait_recv()

    def first_norm():
        inputs[2].wait()
        inputs[3].wait()
        norm_rows(0)

    acc[...] = jnp.zeros_like(acc)
    items = [first_norm] + [functools.partial(norm_rows, i) for i in range(1, rows // step)]
    items += [starts, own_ranks, far_ranks] + [functools.partial(pick_rows, t) for t in range(turns)]
    items += [functools.partial(pick_side, b, t) for b in range(sides) for t in range(turns)]
    late = [functools.partial(cot_pass, o) for o in (1, 3, 2) if o < nx] + [cot_wait]
    late += [functools.partial(arrived, 1, 0)]
    for hop in range(1, half + 1):
        if hop == max(1, half - 3):
            items += late
            late = []
        for kind in order:
            for sign in (1, -1):
                if exists(sign, kind, hop):
                    z_copy(sign, kind, hop, False).wait_recv()
                    if exists(sign, kind, hop + 1):
                        z_copy(sign, kind, hop + 1, True).start()
                    if kind == "b":
                        y_copy("b", sign, hop, True).start()
                    if items:
                        items.pop(0)()
        for sign in (1, -1) if hop < half else (1,):
            (late if late else items).append(functools.partial(arrived, sign, hop))
    for item in items:
        item()

    pl.semaphore_signal(cross_sem, inc=1, device_id=(across, dp, mp), device_id_type=MESH)

    def hop_copy(k, src, dst, target_section, target):
        return pltpu.make_async_remote_copy(
            src_ref=src,
            dst_ref=dst,
            send_sem=hop_send.at[k],
            recv_sem=hop_recv.at[k],
            device_id=(target_section, target, mp),
            device_id_type=MESH,
        )

    def wait_bytes(sem, buf, size):
        pltpu.make_async_copy(buf.at[pl.ds(0, size)], buf.at[pl.ds(0, size)], sem).wait()

    def local_copy(part):
        return pltpu.make_async_copy(
            send1.at[part, dp], in1.at[part, dp], hop_local.at[part]
        )

    qkv[...] = acc[...].astype(BF16)
    for part in range(2):
        for b in range(sides):
            low = part * width + b * LANES
            for a in range(keep):
                wide[pl.ds(b * keep + a, n_dp, stride=sides * keep), :] = qkv[
                    a * n_dp : (a + 1) * n_dp, low : low + LANES
                ].astype(F32)
        send1[part] = wide[...].astype(BF16).reshape(n_dp, sides * keep, LANES)
        local_copy(part).start()
        for j in range(1, n_dp):
            target = (dp + j) & (n_dp - 1)
            hop_copy(part, send1.at[part, target], in1.at[part, dp], section, target).start()

    for part in range(2):
        local_copy(part).wait()
        wait_bytes(hop_recv.at[part], in1.at[part], n_dp - 1)
        first_in = in1[part].reshape(n_dp * sides * keep, LANES)
        pieces = [
            nn(pick_ref[k], first_in).reshape(n_dp, EX_DEV, LANES) for k in range(sides * turns)
        ]
        send2[part] = jnp.concatenate(pieces, axis=1).astype(BF16)
        if part == 0:
            pl.semaphore_wait(cross_sem, 1)
        for j in range(n_dp):
            target = (dp + j) & (n_dp - 1)
            hop_copy(2 + part, send2.at[part, target], in2.at[part, dp], across, target).start()

    scale = 1.0 / float(HEAD) ** 0.5
    lane = lax.broadcasted_iota(jnp.int32, (1, LANES), 1) // HEAD
    heads = LANES // HEAD
    per_side = turns * EX_DEV

    def came(part, b):
        return in2[part, :, b * per_side : (b + 1) * per_side, :].reshape(far_rows, LANES)

    def own(part, b):
        return qkv[:, part * width + b * LANES : part * width + (b + 1) * LANES]

    def one_head(t, s):
        return jnp.where(lane == s, t, jnp.zeros_like(t))

    def softmax(q, k, mask):
        weight = jnp.where(mask, jnp.exp(nt(q, k) * scale), 0.0)
        return weight * (1.0 / jnp.sum(weight, axis=1, keepdims=True))

    def backward(probs, dout_s, v):
        probs_bf = probs.astype(BF16)
        attended = nn(probs_bf, v).astype(BF16)
        delta = jnp.sum(dout_s.astype(F32) * attended.astype(F32), axis=1, keepdims=True)
        return probs_bf, (probs * (nt(dout_s, v) - delta) * scale).astype(BF16)

    def merge(news, sums, s):
        return [jnp.where(lane == s, new, old) for new, old in zip(news, sums)] if s else news

    wait_bytes(hop_recv.at[2], in2.at[0], n_dp)

    @pl.when(encoder)
    def _():
        example = lax.broadcasted_iota(jnp.int32, (far_rows, rows), 0) % EX_DEV
        mask = example.astype(F32) == far_ref[:1, :rows]
        for b in range(sides):
            q = came(0, b)
            for s in range(heads):
                probs_ref[b * heads + s] = softmax(one_head(q, s), own(0, b), mask)

    @pl.when(decoder)
    def _():
        mask = own_ref[:, :1] == far_ref[:1, :]
        for b in range(sides):
            k = came(0, b)
            for s in range(heads):
                probs = softmax(one_head(own(0, b), s), k, mask)
                for c in range(far_rows // rows):
                    probs_ref[b * heads + s, c * rows : (c + 1) * rows, :] = probs[
                        :, c * rows : (c + 1) * rows
                    ]

    wait_bytes(hop_recv.at[3], in2.at[1], n_dp)

    @pl.when(encoder)
    def _():
        for b in range(sides):
            q, dout = came(0, b), came(1, b)
            sums = []
            for s in range(heads):
                probs_bf, dscore = backward(
                    probs_ref[b * heads + s], one_head(dout, s), own(1, b)
                )
                sums = merge((tn(dscore, q), tn(probs_bf, dout)), sums, s)
            for part in range(2):
                low = part * width + b * LANES
                grad[:, low : low + LANES] = sums[part].astype(BF16)

    @pl.when(decoder)
    def _():
        for b in range(sides):
            k, v = came(0, b), came(1, b)
            sums = []
            for s in range(heads):
                probs = jnp.concatenate(
                    [
                        probs_ref[b * heads + s, c * rows : (c + 1) * rows, :]
                        for c in range(far_rows // rows)
                    ],
                    axis=1,
                )
                dscore = backward(probs, one_head(own(1, b), s), v)[1]
                sums = merge((nn(dscore, k),), sums, s)
            grad[:, b * LANES : (b + 1) * LANES] = sums[0].astype(BF16)
        grad[:, width:] = jnp.zeros((rows, width), BF16)

    columns = features // n_mp
    share = jnp.sum(grad[...].astype(F32) * qkv[...].astype(F32), axis=1, keepdims=True)
    inverse = inv_ref[:, :1]
    slope = inverse * inverse * share * (1.0 / features)

    def term(owner):
        at = pl.ds(pl.multiple_of(owner * columns, columns), columns)
        raw = nt(grad[...], wall[at, :])
        return inverse * (raw * gain_ref[:, at]) - x_ref[:, at].astype(F32) * slope

    def sib_copy(o):
        return pltpu.make_async_remote_copy(
            src_ref=sib_send.at[o],
            dst_ref=sib_recv.at[o],
            send_sem=c_send.at[0],
            recv_sem=c_sib.at[o],
            device_id=(section, dp, sibling),
            device_id_type=MESH,
        )

    def to_sibling(o):
        sib_send[o] = term((xx + o) % nx * 2 + 1 - core).astype(BF16)
        sib_copy(o).start()

    def combined(o):
        own_term = term((xx + o) % nx * 2 + core)
        sib_copy(o).wait_recv()
        return own_term + sib_recv[o].astype(F32)

    def part_copy(slot, o, low, size, sign):
        return pltpu.make_async_remote_copy(
            src_ref=x_send.at[o, pl.ds(low, size), :],
            dst_ref=x_recv.at[o, pl.ds(low, size), :],
            send_sem=c_send.at[1],
            recv_sem=c_x.at[slot],
            device_id=(section, dp, (xx + sign + nx) % nx * 2 + core),
            device_id_type=MESH,
        )

    middle = rows // 2
    parts_sent = []
    if nx == 4:
        far_up = part_copy(0, 2, 0, middle, 1)
        far_down = part_copy(1, 2, middle, middle, -1)
        up_plain = part_copy(2, 1, middle, middle, 1)
        up_added = part_copy(3, 1, 0, middle, 1)
        down_plain = part_copy(4, 3, 0, middle, -1)
        down_added = part_copy(5, 3, middle, middle, -1)
        parts_sent = [far_up, far_down, up_plain, up_added, down_plain, down_added]
        to_sibling(2)
        to_sibling(1)
        x_send[2] = combined(2).astype(BF16)
        far_up.start()
        far_down.start()
        to_sibling(3)
        up = combined(1)
        x_send[1, middle:, :] = up[middle:].astype(BF16)
        up_plain.start()
        to_sibling(0)
        down = combined(3)
        x_send[3, :middle, :] = down[:middle].astype(BF16)
        down_plain.start()
        far_up.wait_recv()
        x_send[1, :middle, :] = (up[:middle] + x_recv[2, :middle, :].astype(F32)).astype(BF16)
        up_added.start()
        far_down.wait_recv()
        x_send[3, middle:, :] = (down[middle:] + x_recv[2, middle:, :].astype(F32)).astype(BF16)
        down_added.start()
        result = combined(0)
        for copy in (up_plain, down_plain, up_added, down_added):
            copy.wait_recv()
        result = result + x_recv[1].astype(F32) + x_recv[3].astype(F32)
    else:
        turns = [o for o in (1, 0) if o < nx]
        to_sibling(turns[0])
        for k, o in enumerate(turns):
            if k + 1 < len(turns):
                to_sibling(turns[k + 1])
            result = combined(o)
            if o:
                x_send[o] = result.astype(BF16)
                whole = part_copy(0, 1, 0, rows, 1)
                whole.start()
                parts_sent += [whole]
        for copy in parts_sent:
            copy.wait_recv()
            result = result + x_recv[1].astype(F32)
    out_ref[...] = result.astype(out_ref.dtype)

    for kind in order:
        for sign in (1, -1):
            for hop in range(1, half + 1):
                if exists(sign, kind, hop):
                    z_copy(sign, kind, hop, True).wait_send()
    y_copy("a", 1, 0, True).wait_send()
    for hop in range(half + 1):
        for sign in (1, -1):
            if (hop == 0 or hop == half) and sign == -1:
                continue
            y_copy("b", sign, hop, True).wait_send()

    @pl.when(decoder)
    def _():
        for o in range(1, 2 * nx):
            cot_copy(mp, o, sibling).wait_send()

    for part in range(2):
        wait_bytes(hop_send.at[part], send1.at[part], n_dp - 1)
        wait_bytes(hop_send.at[2 + part], send2.at[part], n_dp)
    for o in range(nx):
        sib_copy(o).wait_send()
    for copy in parts_sent:
        copy.wait_send()


def shards(n_dp, n_mp, layer_rows, cotangent, norm_gains, projections, enc_len, dec_len, enc_dev, dec_dev):
    x = layer_rows[0]
    rows, features = x.shape
    depth, _, width = projections.shape[1:]
    count = enc_len.shape[0]
    tables = [t.reshape(1, count) for t in (enc_len, dec_len, enc_dev, dec_dev)]
    keep = rows // n_dp
    turns = 2 * rows // EX_DEV // n_dp
    sides = width // LANES
    far_rows = n_dp * turns * EX_DEV
    nx = n_mp // 2
    nz = n_dp // 2
    columns = features // n_mp
    vmem = pl.BlockSpec(memory_space=pltpu.VMEM)
    hbm = pl.BlockSpec(memory_space=pl.ANY)
    dma = pltpu.SemaphoreType.DMA
    out = pl.pallas_call(
        functools.partial(kernel, n_dp, n_mp),
        out_shape=jax.ShapeDtypeStruct((rows, columns), BF16),
        in_specs=[hbm] * 4 + [vmem] * 4,
        out_specs=vmem,
        scratch_shapes=[
            pltpu.VMEM((rows, features), BF16),
            pltpu.VMEM((1, features), F32),
            pltpu.VMEM((depth, 2, width), BF16),
            pltpu.VMEM((rows, columns), BF16),
            pltpu.VMEM((features, 2 * width), BF16),
            pltpu.VMEM((features // LANES, rows, LANES), BF16),
            pltpu.VMEM((features // LANES, rows, LANES), BF16),
            pltpu.VMEM((rows, LANES), F32),
            pltpu.VMEM((rows, 2 * width), F32),
            pltpu.VMEM((rows, 2 * width), BF16),
            pltpu.VMEM((rows, 2 * width), BF16),
            pltpu.VMEM((sides * turns, count, n_dp * sides * keep), BF16),
            pltpu.VMEM((rows, LANES), F32),
            pltpu.VMEM((8, far_rows), F32),
            pltpu.VMEM((sides * LANES // HEAD, far_rows, rows), F32),
            pltpu.VMEM((n_dp * sides * keep, LANES), F32),
            pltpu.VMEM((2, n_dp, sides * keep, LANES), BF16),
            pltpu.VMEM((2, n_dp, sides * keep, LANES), BF16),
            pltpu.VMEM((2, n_dp, sides * turns * EX_DEV, LANES), BF16),
            pltpu.VMEM((2, n_dp, sides * turns * EX_DEV, LANES), BF16),
            pltpu.VMEM((nx, rows, columns), BF16),
            pltpu.VMEM((nx, rows, columns), BF16),
            pltpu.VMEM((nx, rows, columns), BF16),
            pltpu.VMEM((nx, rows, columns), BF16),
            dma((4,)),
            pltpu.SemaphoreType.REGULAR,
            dma((2, 3, max(1, nz // 2))),
            dma((nz + 1,)),
            dma((2 * nx,)),
            dma,
            dma,
            dma((4,)),
            dma((4,)),
            dma((2,)),
            dma((2,)),
            dma((nx,)),
            dma((6,)),
        ],
        compiler_params=pltpu.CompilerParams(
            collective_id=0, has_side_effects=True, vmem_limit_bytes=60 * 2**20
        ),
    )(x, norm_gains, projections[0], cotangent, *tables)
    return out[None]


def solution(mesh):
    placed = (
        P("section", "dp", None),
        P("dp", "mp"),
        P("section", None),
        P("section", "dp", None, "mp"),
        P(),
        P(),
        P(),
        P(),
    )
    return jax.shard_map(
        functools.partial(shards, mesh.shape["dp"], mesh.shape["mp"]),
        mesh=mesh,
        in_specs=placed,
        out_specs=P("section", "dp", "mp"),
        check_vma=False,
    )
```

```python
import functools

import jax
import jax.numpy as jnp
from jax import lax
from jax.experimental import pallas as pl
from jax.experimental.pallas import tpu as pltpu
from jax.sharding import PartitionSpec as P

HEAD = 64
EX_DEV = 8
EPS = 1e-06
LANES = 128
CUT = 64
MESH = pl.DeviceIdType.MESH
F32 = jnp.float32
BF16 = jnp.bfloat16


def nt(a, b):
    return lax.dot_general(a, b, (((1,), (1,)), ((), ())), preferred_element_type=F32)


def tn(a, b):
    return lax.dot_general(a, b, (((0,), (0,)), ((), ())), preferred_element_type=F32)


def nn(a, b):
    return jnp.dot(a, b, preferred_element_type=F32)


def kernel(
    n_dp,
    n_mp,
    x_hbm,
    gain_hbm,
    w_hbm,
    cot_hbm,
    el_ref,
    dl_ref,
    ed_ref,
    dd_ref,
    out_ref,
    x_ref,
    gain_ref,
    w_ref,
    cot_ref,
    wall,
    left0,
    left1,
    inv_ref,
    acc,
    qkv,
    grad,
    pick_ref,
    own_ref,
    far_ref,
    probs_ref,
    spread_ref,
    send1,
    in1,
    send2,
    in2,
    sib_send,
    sib_recv,
    x_send,
    x_recv,
    in_sems,
    cross_sem,
    z_sems,
    y_sems,
    cot_sems,
    w_send_sem,
    cot_send_sem,
    hop_send,
    hop_recv,
    hop_local,
    c_send,
    c_sib,
    c_x,
):
    nz = n_dp // 2
    nx = n_mp // 2
    half = nz // 2
    rows, features = x_ref.shape
    depth, _, width = w_ref.shape
    keep = rows // n_dp
    turns = 2 * rows // EX_DEV // n_dp
    sides = width // LANES
    section = lax.axis_index("section")
    dp = lax.axis_index("dp")
    mp = lax.axis_index("mp")
    yl = dp // nz
    z = dp % nz
    xx = mp // 2
    core = mp % 2
    encoder = section == 0
    decoder = section == 1

    inputs = [
        pltpu.make_async_copy(source, target, in_sems.at[k])
        for k, (source, target) in enumerate(
            ((w_hbm, w_ref), (cot_hbm, cot_ref), (x_hbm, x_ref), (gain_hbm, gain_ref))
        )
    ]
    for copy in inputs:
        copy.start()

    sibling = xx * 2 + 1 - core
    across = 1 - section
    greeted = [(section, yl * nz + (z + 1) % nz, mp), (section, yl * nz + (z + nz - 1) % nz, mp)]
    greeted += [(section, (1 - yl) * nz + z, mp), (across, dp, mp), (section, dp, sibling)]
    greeted += [(section, dp, ((xx + o) & (nx - 1)) * 2 + core) for o in range(1, nx)]
    barrier = pltpu.get_barrier_semaphore()
    for target in greeted:
        pl.semaphore_signal(barrier, inc=1, device_id=target, device_id_type=MESH)
    inputs[0].wait()
    own = pl.ds(pl.multiple_of(dp * depth, depth), depth)
    wall[own, :width] = w_ref[:, 0, :]
    wall[own, width:] = w_ref[:, 1, :]
    pl.semaphore_wait(barrier, len(greeted))

    spans = {"b": (CUT, depth - CUT), "a": (0, CUT), "o": (0, CUT)}
    order = ("b", "a", "o")

    def span(kind, y, zb):
        first, size = spans[kind]
        return wall.at[pl.ds(pl.multiple_of((y * nz + zb) * depth + first, 16), size), :]

    def exists(sign, kind, hop):
        if hop < half:
            return True
        return hop == half and ((kind == "b") == (sign == 1))

    def z_copy(sign, kind, hop, sending):
        y = 1 - yl if kind == "o" else yl
        back = hop - 1 if sending else hop
        part = span(kind, y, (z - sign * back) & (nz - 1))
        return pltpu.make_async_remote_copy(
            src_ref=part,
            dst_ref=part,
            send_sem=w_send_sem,
            recv_sem=z_sems.at[(1 - sign) // 2, order.index(kind), hop - 1],
            device_id=(section, yl * nz + ((z + sign) & (nz - 1)), mp),
            device_id_type=MESH,
        )

    def y_slot(sign, hop):
        if hop == 0:
            return 0
        return hop if sign == 1 else half + hop

    def y_copy(kind, sign, hop, sending):
        y = yl if sending else 1 - yl
        part = span(kind, y, (z - sign * hop) & (nz - 1))
        slot = nz if kind == "a" else y_slot(sign, hop)
        return pltpu.make_async_remote_copy(
            src_ref=part,
            dst_ref=part,
            send_sem=w_send_sem,
            recv_sem=y_sems.at[slot],
            device_id=(section, (1 - yl) * nz + z, mp),
            device_id_type=MESH,
        )

    for kind in ("b", "a"):
        for sign in (1, -1):
            if exists(sign, kind, 1):
                z_copy(sign, kind, 1, True).start()
        y_copy("a" if kind == "b" else "b", 1, 0, True).start()

    per_mp = features // n_mp // LANES

    def cot_copy(owner, slot, target):
        part = left1.at[pl.ds(owner * per_mp, per_mp)]
        return pltpu.make_async_remote_copy(
            src_ref=part,
            dst_ref=part,
            send_sem=cot_send_sem,
            recv_sem=cot_sems.at[slot],
            device_id=(section, dp, target),
            device_id_type=MESH,
        )

    inputs[1].wait()

    @pl.when(decoder)
    def _():
        for c in range(per_mp):
            left1[mp * per_mp + c] = cot_ref[:, c * LANES : (c + 1) * LANES]
        for o in (2, 1, 3):
            if o < nx:
                cot_copy(mp, o, ((xx + o) & (nx - 1)) * 2 + core).start()
        cot_copy(mp, nx, sibling).start()

    y_copy("a", 1, 0, False).wait_recv()
    for sign in (1, -1):
        if exists(sign, "o", 1):
            z_copy(sign, "o", 1, True).start()

    step = 32 if rows % 32 == 0 else rows

    def norm_rows(i):
        at = pl.ds(i * step, step)
        values = x_ref[at, :].astype(F32)
        inverse = lax.rsqrt(jnp.mean(values * values, axis=1, keepdims=True) + EPS)
        inv_ref[at, :] = jnp.broadcast_to(inverse, (step, LANES))
        normed = (values * inverse * gain_ref[...]).astype(BF16)
        for c in range(features // LANES):
            left0[c, at, :] = normed[:, c * LANES : (c + 1) * LANES]

        @pl.when(encoder)
        def _():
            for c in range(features // LANES):
                left1[c, at, :] = normed[:, c * LANES : (c + 1) * LANES]

    count = EX_DEV * n_dp
    far_rows = n_dp * turns * EX_DEV
    enc_r = tuple(t[...].astype(F32) for t in (el_ref, ed_ref))
    dec_r = tuple(t[...].astype(F32) for t in (dl_ref, dd_ref))
    len_r, dev_r = (jnp.where(encoder, a, b) for a, b in zip(enc_r, dec_r))
    far_len_r, far_dev_r = (jnp.where(encoder, b, a) for a, b in zip(enc_r, dec_r))
    here = dp.astype(F32)
    found = {}

    def starts():
        shape = (count, count)
        down = lax.broadcasted_iota(jnp.int32, shape, 0).astype(F32)
        along = lax.broadcasted_iota(jnp.int32, shape, 1).astype(F32)
        one = jnp.ones(shape, F32)

        def column(row):
            return jnp.sum(jnp.where(down == along, row, 0.0), axis=1, keepdims=True)

        len_c, dev_c, far_len_c, far_dev_c = (
            column(t) for t in (len_r, dev_r, far_len_r, far_dev_r)
        )
        above = (dev_r == dev_c) & (down < along)
        before = (dev_r == dev_c) & (along < down)
        found.update(
            down=down,
            len_c=len_c,
            dev_c=dev_c,
            far_len_c=far_len_c,
            start_r=jnp.sum(jnp.where(above, len_c * one, 0.0), axis=0, keepdims=True),
            rank_r=jnp.sum(jnp.where(above, one, 0.0), axis=0, keepdims=True),
            start_c=jnp.sum(jnp.where(before, len_r * one, 0.0), axis=1, keepdims=True),
            rank_c=jnp.sum(jnp.where(before, one, 0.0), axis=1, keepdims=True),
            far_rank_r=jnp.sum(
                jnp.where((far_dev_r == far_dev_c) & (down < along), one, 0.0),
                axis=0,
                keepdims=True,
            ),
            far_start_c=jnp.sum(
                jnp.where((far_dev_r == far_dev_c) & (along < down), far_len_r * one, 0.0),
                axis=1,
                keepdims=True,
            ),
        )

    def own_ranks():
        u_r = lax.broadcasted_iota(jnp.int32, (count, rows), 1).astype(F32)
        start_c, start_r = found["start_c"], found["start_r"]
        mine = (found["dev_c"] == here) & (start_c <= u_r) & (u_r < start_c + found["len_c"])
        along = jnp.sum(
            jnp.where(mine, found["rank_c"] * jnp.ones_like(u_r), 0.0), axis=0, keepdims=True
        )
        u_c = lax.broadcasted_iota(jnp.int32, (rows, count), 0).astype(F32)
        mine = (dev_r == here) & (start_r <= u_c) & (u_c < start_r + len_r)
        down = jnp.sum(
            jnp.where(mine, found["rank_r"] * jnp.ones_like(u_c), 0.0), axis=1, keepdims=True
        )
        far_ref[:, :rows] = jnp.broadcast_to(along, (far_ref.shape[0], rows))
        own_ref[...] = jnp.broadcast_to(down, own_ref.shape)

    def far_ranks():
        c_i = lax.broadcasted_iota(jnp.int32, (count, far_rows), 1)
        rank = (c_i % EX_DEV).astype(F32)
        hit = (found["dev_c"] == here) & (found["rank_c"] == rank)
        one = jnp.ones_like(rank)
        start = jnp.sum(jnp.where(hit, found["far_start_c"] * one, 0.0), axis=0, keepdims=True)
        length = jnp.sum(jnp.where(hit, found["far_len_c"] * one, 0.0), axis=0, keepdims=True)
        c_r = lax.broadcasted_iota(jnp.int32, (1, far_rows), 1)
        offset = (c_r // (turns * EX_DEV) - start.astype(jnp.int32)) & (n_dp - 1)
        offset = offset + c_r % (turns * EX_DEV) // EX_DEV * n_dp
        rank_r = jnp.where(offset.astype(F32) < length, (c_r % EX_DEV).astype(F32), -1.0)

        @pl.when(decoder)
        def _():
            far_ref[...] = jnp.broadcast_to(rank_r, far_ref.shape)

    def spread_rows():
        sent = lax.broadcasted_iota(jnp.int32, (rows, rows), 0)
        row = lax.broadcasted_iota(jnp.int32, (rows, rows), 1)
        here_too = sent % keep * n_dp + sent // keep == row
        spread_ref[...] = jnp.where(here_too, 1.0, 0.0).astype(BF16)

    def pick_rows(turn):
        start_i = found["start_r"].astype(jnp.int32)
        offset = ((dp - start_i) & (n_dp - 1)) + turn * n_dp
        source = dev_r * float(sides * keep) + ((start_i + offset) // n_dp).astype(F32)
        value = jnp.where(offset.astype(F32) < len_r, source + 1.0, 0.0)
        place = far_dev_r * float(EX_DEV) + found["far_rank_r"]
        down = found["down"]
        one = jnp.ones_like(down)
        found[turn] = (
            jnp.sum(jnp.where(place == down, value * one, 0.0), axis=1, keepdims=True) - 1.0
        )

    def pick_side(b, turn):
        fidx = found[turn]
        place = lax.broadcasted_iota(jnp.int32, (count, n_dp * sides * keep), 1).astype(F32)
        at = jnp.where(fidx >= 0.0, fidx + float(b * keep), -1.0)
        pick_ref[b * turns + turn] = jnp.where(place == at, 1.0, 0.0).astype(BF16)

    def product(y, zb):
        total0 = total1 = None
        for row in (y, 1 - y):
            block = row * nz + zb
            at = pl.ds(pl.multiple_of(block * depth, depth), depth)
            p0 = nn(left0[block], wall[at, :width])
            p1 = nn(left1[block], wall[at, width:])
            total0 = p0 if total0 is None else total0 + p0
            total1 = p1 if total1 is None else total1 + p1
        acc[:, :width] += total0
        acc[:, width:] += total1

    def arrived(sign, hop):
        y_copy("b", sign, hop, False).wait_recv()
        product(yl, (z - sign * hop) & (nz - 1))

    def cot_pass(o):
        @pl.when(decoder)
        def _():
            owner = (xx - o + nx) % nx * 2 + core
            cot_copy(owner, o, sibling).wait_recv()
            cot_copy(owner, nx + o, sibling).start()

    def cot_wait():
        @pl.when(decoder)
        def _():
            for o in range(nx):
                owner = (xx - o + nx) % nx * 2 + 1 - core
                cot_copy(owner, nx + o, sibling).wait_recv()

    def first_norm():
        inputs[2].wait()
        inputs[3].wait()
        norm_rows(0)

    acc[...] = jnp.zeros_like(acc)
    items = [first_norm] + [functools.partial(norm_rows, i) for i in range(1, rows // step)]
    items += [spread_rows, starts, own_ranks, far_ranks] + [functools.partial(pick_rows, t) for t in range(turns)]
    items += [functools.partial(pick_side, b, t) for b in range(sides) for t in range(turns)]
    late = [functools.partial(cot_pass, o) for o in (1, 3, 2) if o < nx] + [cot_wait]
    late += [functools.partial(arrived, 1, 0)]
    for hop in range(1, half + 1):
        if hop == max(1, half - 3):
            items += late
            late = []
        for kind in order:
            for sign in (1, -1):
                if exists(sign, kind, hop):
                    z_copy(sign, kind, hop, False).wait_recv()
                    if exists(sign, kind, hop + 1):
                        z_copy(sign, kind, hop + 1, True).start()
                    if kind == "b":
                        y_copy("b", sign, hop, True).start()
                    if items:
                        items.pop(0)()
        for sign in (1, -1) if hop < half else (1,):
            (late if late else items).append(functools.partial(arrived, sign, hop))
    for item in items:
        item()

    pl.semaphore_signal(cross_sem, inc=1, device_id=(across, dp, mp), device_id_type=MESH)

    def hop_copy(k, src, dst, target_section, target):
        return pltpu.make_async_remote_copy(
            src_ref=src,
            dst_ref=dst,
            send_sem=hop_send.at[k],
            recv_sem=hop_recv.at[k],
            device_id=(target_section, target, mp),
            device_id_type=MESH,
        )

    def wait_bytes(sem, buf, size):
        pltpu.make_async_copy(buf.at[pl.ds(0, size)], buf.at[pl.ds(0, size)], sem).wait()

    def to_all(send):
        def four(k, carry):
            away = half - 1 - k
            for sign in (1, -1):
                for y in (yl, 1 - yl):
                    send(y * nz + ((z + sign * away) & (nz - 1)))
            return carry

        for y in (yl, 1 - yl):
            send(y * nz + ((z + half) & (nz - 1)))
        lax.fori_loop(0, half - 1, four, 0)

    def local_copy(part):
        return pltpu.make_async_copy(
            send1.at[part, dp], in1.at[part, dp], hop_local.at[part]
        )

    for part in range(2):
        at = slice(part * width, (part + 1) * width)
        qkv[:, at] = acc[:, at].astype(BF16)
        moved = nn(spread_ref[...], qkv[:, at]).reshape(n_dp, keep, width)
        pieces = [moved[:, :, b * LANES : (b + 1) * LANES] for b in range(sides)]
        send1[part] = jnp.concatenate(pieces, axis=1).astype(BF16)
        local_copy(part).start()

        def send_to(target, part=part):
            hop_copy(part, send1.at[part, target], in1.at[part, dp], section, target).start()

        to_all(send_to)
        send_to((1 - yl) * nz + z)

    for part in range(2):
        local_copy(part).wait()
        wait_bytes(hop_recv.at[part], in1.at[part], n_dp - 1)
        first_in = in1[part].reshape(n_dp * sides * keep, LANES)
        pieces = [
            nn(pick_ref[k], first_in).reshape(n_dp, EX_DEV, LANES) for k in range(sides * turns)
        ]
        send2[part] = jnp.concatenate(pieces, axis=1).astype(BF16)
        if part == 0:
            pl.semaphore_wait(cross_sem, 1)

        def pass_to(target, part=part):
            hop_copy(2 + part, send2.at[part, target], in2.at[part, dp], across, target).start()

        to_all(pass_to)
        pass_to(dp)
        pass_to((1 - yl) * nz + z)

    scale = 1.0 / float(HEAD) ** 0.5
    lane = lax.broadcasted_iota(jnp.int32, (1, LANES), 1) // HEAD
    heads = LANES // HEAD
    per_side = turns * EX_DEV

    def came(part, b):
        return in2[part, :, b * per_side : (b + 1) * per_side, :].reshape(far_rows, LANES)

    def own(part, b):
        return qkv[:, part * width + b * LANES : part * width + (b + 1) * LANES]

    def one_head(t, s):
        return jnp.where(lane == s, t, jnp.zeros_like(t))

    def softmax(q, k, mask):
        weight = jnp.where(mask, jnp.exp(nt(q, k) * scale), 0.0)
        return weight * (1.0 / jnp.sum(weight, axis=1, keepdims=True))

    def backward(probs, dout_s, v):
        probs_bf = probs.astype(BF16)
        attended = nn(probs_bf, v).astype(BF16)
        delta = jnp.sum(dout_s.astype(F32) * attended.astype(F32), axis=1, keepdims=True)
        return probs_bf, (probs * (nt(dout_s, v) - delta) * scale).astype(BF16)

    def merge(news, sums, s):
        return [jnp.where(lane == s, new, old) for new, old in zip(news, sums)] if s else news

    over_z = (nz - 1) * (depth + CUT)
    over_y = CUT + nz * (depth - CUT)
    wait_bytes(w_send_sem, wall, over_z)
    wait_bytes(w_send_sem, wall, over_y)
    for part in range(2):
        wait_bytes(hop_send.at[part], send1.at[part], n_dp - 1)

    @pl.when(decoder)
    def _():
        wait_bytes(cot_send_sem, left1, (2 * nx - 1) * per_mp)

    wait_bytes(hop_recv.at[2], in2.at[0], n_dp)

    @pl.when(encoder)
    def _():
        example = lax.broadcasted_iota(jnp.int32, (far_rows, rows), 0) % EX_DEV
        mask = example.astype(F32) == far_ref[:1, :rows]
        for b in range(sides):
            q = came(0, b)
            for s in range(heads):
                probs_ref[b * heads + s] = softmax(one_head(q, s), own(0, b), mask)

    @pl.when(decoder)
    def _():
        mask = own_ref[:, :1] == far_ref[:1, :]
        for b in range(sides):
            k = came(0, b)
            for s in range(heads):
                probs = softmax(one_head(own(0, b), s), k, mask)
                for c in range(far_rows // rows):
                    probs_ref[b * heads + s, c * rows : (c + 1) * rows, :] = probs[
                        :, c * rows : (c + 1) * rows
                    ]

    wait_bytes(hop_recv.at[3], in2.at[1], n_dp)

    @pl.when(encoder)
    def _():
        for b in range(sides):
            q, dout = came(0, b), came(1, b)
            sums = []
            for s in range(heads):
                probs_bf, dscore = backward(
                    probs_ref[b * heads + s], one_head(dout, s), own(1, b)
                )
                sums = merge((tn(dscore, q), tn(probs_bf, dout)), sums, s)
            for part in range(2):
                low = part * width + b * LANES
                grad[:, low : low + LANES] = sums[part].astype(BF16)

    @pl.when(decoder)
    def _():
        for b in range(sides):
            k, v = came(0, b), came(1, b)
            sums = []
            for s in range(heads):
                probs = jnp.concatenate(
                    [
                        probs_ref[b * heads + s, c * rows : (c + 1) * rows, :]
                        for c in range(far_rows // rows)
                    ],
                    axis=1,
                )
                dscore = backward(probs, one_head(own(1, b), s), v)[1]
                sums = merge((nn(dscore, k),), sums, s)
            grad[:, b * LANES : (b + 1) * LANES] = sums[0].astype(BF16)
        grad[:, width:] = jnp.zeros((rows, width), BF16)

    columns = features // n_mp
    share = jnp.sum(grad[...].astype(F32) * qkv[...].astype(F32), axis=1, keepdims=True)
    inverse = inv_ref[:, :1]
    slope = inverse * inverse * share * (1.0 / features)

    def term(owner, low, size):
        at = pl.ds(pl.multiple_of(owner * columns, columns), columns)
        here_rows = slice(low, low + size)
        raw = nt(grad[here_rows, :], wall[at, :])
        return inverse[here_rows] * (raw * gain_ref[:, at]) - x_ref[
            here_rows, at
        ].astype(F32) * slope[here_rows]

    middle = rows // 2

    def sib_copy(o, h):
        at = pl.ds(h * middle, middle)
        return pltpu.make_async_remote_copy(
            src_ref=sib_send.at[o, at, :],
            dst_ref=sib_recv.at[o, at, :],
            send_sem=c_send.at[0],
            recv_sem=c_sib.at[o, h],
            device_id=(section, dp, sibling),
            device_id_type=MESH,
        )

    def to_sibling(o, h):
        at = slice(h * middle, (h + 1) * middle)
        sib_send[o, at, :] = term(((xx + o) & (nx - 1)) * 2 + 1 - core, h * middle, middle).astype(BF16)
        sib_copy(o, h).start()

    def combined(o, h):
        own_term = term(((xx + o) & (nx - 1)) * 2 + core, h * middle, middle)
        sib_copy(o, h).wait_recv()
        return own_term + sib_recv[o, h * middle : (h + 1) * middle, :].astype(F32)

    def part_copy(slot, o, low, size, sign):
        return pltpu.make_async_remote_copy(
            src_ref=x_send.at[o, pl.ds(low, size), :],
            dst_ref=x_recv.at[o, pl.ds(low, size), :],
            send_sem=c_send.at[1],
            recv_sem=c_x.at[slot],
            device_id=(section, dp, (xx + sign + nx) % nx * 2 + core),
            device_id_type=MESH,
        )

    top, low_half = slice(0, middle), slice(middle, rows)
    parts_sent = []
    if nx == 4:
        far_up = part_copy(0, 2, 0, middle, 1)
        far_down = part_copy(1, 2, middle, middle, -1)
        up_plain = part_copy(2, 1, middle, middle, 1)
        up_added = part_copy(3, 1, 0, middle, 1)
        down_plain = part_copy(4, 3, 0, middle, -1)
        down_added = part_copy(5, 3, middle, middle, -1)
        parts_sent = [far_up, far_down, up_plain, up_added, down_plain, down_added]
        for o, h in ((2, 0), (2, 1), (1, 1), (3, 0)):
            to_sibling(o, h)
        x_send[2, top, :] = combined(2, 0).astype(BF16)
        far_up.start()
        x_send[2, low_half, :] = combined(2, 1).astype(BF16)
        far_down.start()
        to_sibling(1, 0)
        to_sibling(3, 1)
        x_send[1, low_half, :] = combined(1, 1).astype(BF16)
        up_plain.start()
        x_send[3, top, :] = combined(3, 0).astype(BF16)
        down_plain.start()
        to_sibling(0, 0)
        to_sibling(0, 1)
        up = combined(1, 0)
        down = combined(3, 1)
        far_up.wait_recv()
        x_send[1, top, :] = (up + x_recv[2, top, :].astype(F32)).astype(BF16)
        up_added.start()
        far_down.wait_recv()
        x_send[3, low_half, :] = (down + x_recv[2, low_half, :].astype(F32)).astype(BF16)
        down_added.start()
        first, second = combined(0, 0), combined(0, 1)
        down_plain.wait_recv()
        first = first + x_recv[3, top, :].astype(F32)
        up_plain.wait_recv()
        second = second + x_recv[1, low_half, :].astype(F32)
        up_added.wait_recv()
        out_ref[top, :] = (first + x_recv[1, top, :].astype(F32)).astype(BF16)
        down_added.wait_recv()
        out_ref[low_half, :] = (second + x_recv[3, low_half, :].astype(F32)).astype(BF16)
    else:
        for o in range(nx):
            for h in range(2):
                to_sibling(o, h)
        if nx == 2:
            whole = part_copy(0, 1, 0, rows, 1)
            parts_sent += [whole]
            x_send[1, top, :] = combined(1, 0).astype(BF16)
            x_send[1, low_half, :] = combined(1, 1).astype(BF16)
            whole.start()
            whole.wait_recv()
        for h, at in enumerate((top, low_half)):
            result = combined(0, h)
            if nx == 2:
                result = result + x_recv[1, at, :].astype(F32)
            out_ref[at, :] = result.astype(BF16)

    for part in range(2):
        wait_bytes(hop_send.at[2 + part], send2.at[part], n_dp)
    wait_bytes(c_send.at[0], sib_send, nx)
    if nx > 1:
        wait_bytes(c_send.at[1], x_send, nx - 1)


def shards(n_dp, n_mp, layer_rows, cotangent, norm_gains, projections, enc_len, dec_len, enc_dev, dec_dev):
    x = layer_rows[0]
    rows, features = x.shape
    depth, _, width = projections.shape[1:]
    count = enc_len.shape[0]
    tables = [t.reshape(1, count) for t in (enc_len, dec_len, enc_dev, dec_dev)]
    keep = rows // n_dp
    turns = 2 * rows // EX_DEV // n_dp
    sides = width // LANES
    far_rows = n_dp * turns * EX_DEV
    nx = n_mp // 2
    nz = n_dp // 2
    columns = features // n_mp
    vmem = pl.BlockSpec(memory_space=pltpu.VMEM)
    hbm = pl.BlockSpec(memory_space=pl.ANY)
    dma = pltpu.SemaphoreType.DMA
    out = pl.pallas_call(
        functools.partial(kernel, n_dp, n_mp),
        out_shape=jax.ShapeDtypeStruct((rows, columns), BF16),
        in_specs=[hbm] * 4 + [vmem] * 4,
        out_specs=vmem,
        scratch_shapes=[
            pltpu.VMEM((rows, features), BF16),
            pltpu.VMEM((1, features), F32),
            pltpu.VMEM((depth, 2, width), BF16),
            pltpu.VMEM((rows, columns), BF16),
            pltpu.VMEM((features, 2 * width), BF16),
            pltpu.VMEM((features // LANES, rows, LANES), BF16),
            pltpu.VMEM((features // LANES, rows, LANES), BF16),
            pltpu.VMEM((rows, LANES), F32),
            pltpu.VMEM((rows, 2 * width), F32),
            pltpu.VMEM((rows, 2 * width), BF16),
            pltpu.VMEM((rows, 2 * width), BF16),
            pltpu.VMEM((sides * turns, count, n_dp * sides * keep), BF16),
            pltpu.VMEM((rows, LANES), F32),
            pltpu.VMEM((8, far_rows), F32),
            pltpu.VMEM((sides * LANES // HEAD, far_rows, rows), F32),
            pltpu.VMEM((rows, rows), BF16),
            pltpu.VMEM((2, n_dp, sides * keep, LANES), BF16),
            pltpu.VMEM((2, n_dp, sides * keep, LANES), BF16),
            pltpu.VMEM((2, n_dp, sides * turns * EX_DEV, LANES), BF16),
            pltpu.VMEM((2, n_dp, sides * turns * EX_DEV, LANES), BF16),
            pltpu.VMEM((nx, rows, columns), BF16),
            pltpu.VMEM((nx, rows, columns), BF16),
            pltpu.VMEM((nx, rows, columns), BF16),
            pltpu.VMEM((nx, rows, columns), BF16),
            dma((4,)),
            pltpu.SemaphoreType.REGULAR,
            dma((2, 3, max(1, nz // 2))),
            dma((nz + 1,)),
            dma((2 * nx,)),
            dma,
            dma,
            dma((4,)),
            dma((4,)),
            dma((2,)),
            dma((2,)),
            dma((nx, 2)),
            dma((6,)),
        ],
        compiler_params=pltpu.CompilerParams(
            collective_id=0, has_side_effects=True, vmem_limit_bytes=60 * 2**20
        ),
    )(x, norm_gains, projections[0], cotangent, *tables)
    return out[None]


def solution(mesh):
    placed = (
        P("section", "dp", None),
        P("dp", "mp"),
        P("section", None),
        P("section", "dp", None, "mp"),
        P(),
        P(),
        P(),
        P(),
    )
    return jax.shard_map(
        functools.partial(shards, mesh.shape["dp"], mesh.shape["mp"]),
        mesh=mesh,
        in_specs=placed,
        out_specs=P("section", "dp", "mp"),
        check_vma=False,
    )
```

```python
import functools

import jax
import jax.numpy as jnp
from jax import lax
from jax.experimental import pallas as pl
from jax.experimental.pallas import tpu as pltpu
from jax.sharding import PartitionSpec as P

HEAD = 64
EX_DEV = 8
EPS = 1e-06
LANES = 128
CUT = 48
CUT2 = 96
MESH = pl.DeviceIdType.MESH
F32 = jnp.float32
BF16 = jnp.bfloat16


def nt(a, b):
    return lax.dot_general(a, b, (((1,), (1,)), ((), ())), preferred_element_type=F32)


def tn(a, b):
    return lax.dot_general(a, b, (((0,), (0,)), ((), ())), preferred_element_type=F32)


def nn(a, b):
    return jnp.dot(a, b, preferred_element_type=F32)


def kernel(
    n_dp,
    n_mp,
    x_hbm,
    gain_hbm,
    w_hbm,
    cot_hbm,
    el_ref,
    dl_ref,
    ed_ref,
    dd_ref,
    out_ref,
    x_ref,
    gain_ref,
    w_ref,
    cot_ref,
    wall,
    left0,
    left1,
    inv_ref,
    acc,
    qkv,
    grad,
    pick_ref,
    own_ref,
    far_ref,
    probs_ref,
    spread_ref,
    send1,
    in1,
    send2,
    in2,
    sib_send,
    sib_recv,
    x_send,
    x_recv,
    in_sems,
    cross_sem,
    z_sems,
    y_sems,
    cot_sems,
    w_send_sem,
    cot_send_sem,
    hop_send,
    hop_recv,
    hop_local,
    c_send,
    c_sib,
    c_x,
):
    nz = n_dp // 2
    nx = n_mp // 2
    half = nz // 2
    rows, features = x_ref.shape
    depth, _, width = w_ref.shape
    keep = rows // n_dp
    turns = 2 * rows // EX_DEV // n_dp
    sides = width // LANES
    section = lax.axis_index("section")
    dp = lax.axis_index("dp")
    mp = lax.axis_index("mp")
    yl = dp // nz
    z = dp % nz
    xx = mp // 2
    core = mp % 2
    encoder = section == 0
    decoder = section == 1

    inputs = [
        pltpu.make_async_copy(source, target, in_sems.at[k])
        for k, (source, target) in enumerate(
            ((w_hbm, w_ref), (cot_hbm, cot_ref), (x_hbm, x_ref), (gain_hbm, gain_ref))
        )
    ]
    for copy in inputs:
        copy.start()

    sibling = xx * 2 + 1 - core
    across = 1 - section
    greeted = [(section, yl * nz + (z + 1) % nz, mp), (section, yl * nz + (z + nz - 1) % nz, mp)]
    greeted += [(section, (1 - yl) * nz + z, mp), (across, dp, mp), (section, dp, sibling)]
    greeted += [(section, dp, ((xx + o) & (nx - 1)) * 2 + core) for o in range(1, nx)]
    barrier = pltpu.get_barrier_semaphore()
    for target in greeted:
        pl.semaphore_signal(barrier, inc=1, device_id=target, device_id_type=MESH)
    inputs[0].wait()
    own = pl.ds(pl.multiple_of(dp * depth, depth), depth)
    wall[own, :width] = w_ref[:, 0, :]
    wall[own, width:] = w_ref[:, 1, :]
    pl.semaphore_wait(barrier, len(greeted))

    spans = {"b": (CUT, CUT2 - CUT), "c": (CUT2, depth - CUT2), "a": (0, CUT), "o": (0, CUT)}
    order = ("b", "c", "a", "o")

    def span(kind, y, zb):
        first, size = spans[kind]
        return wall.at[pl.ds(pl.multiple_of((y * nz + zb) * depth + first, 16), size), :]

    def at_last(sign, kind):
        return (kind in "bc") == (sign == 1)

    def z_copy(sign, kind, hop, sending):
        y = 1 - yl if kind == "o" else yl
        back = hop - 1 if sending else hop
        part = span(kind, y, (z - sign * back) & (nz - 1))
        return pltpu.make_async_remote_copy(
            src_ref=part,
            dst_ref=part,
            send_sem=w_send_sem,
            recv_sem=z_sems.at[(1 - sign) // 2, order.index(kind), hop - 1],
            device_id=(section, yl * nz + ((z + sign) & (nz - 1)), mp),
            device_id_type=MESH,
        )

    def y_copy(kind, zb, slot, sending):
        piece = span(kind, yl if sending else 1 - yl, zb)
        return pltpu.make_async_remote_copy(
            src_ref=piece,
            dst_ref=piece,
            send_sem=w_send_sem,
            recv_sem=y_sems.at["bca".index(kind), slot],
            device_id=(section, (1 - yl) * nz + z, mp),
            device_id_type=MESH,
        )

    for kind in ("b", "c", "a"):
        for sign in (1, -1):
            if half > 1 or at_last(sign, kind):
                z_copy(sign, kind, 1, True).start()
        if kind == "b":
            y_copy("a", z, 0, True).start()
    for kind in "bc":
        y_copy(kind, z, 0, True).start()

    per_mp = features // n_mp // LANES

    def cot_copy(owner, slot, target):
        part = left1.at[pl.ds(owner * per_mp, per_mp)]
        return pltpu.make_async_remote_copy(
            src_ref=part,
            dst_ref=part,
            send_sem=cot_send_sem,
            recv_sem=cot_sems.at[slot],
            device_id=(section, dp, target),
            device_id_type=MESH,
        )

    inputs[1].wait()

    @pl.when(decoder)
    def _():
        for c in range(per_mp):
            left1[mp * per_mp + c] = cot_ref[:, c * LANES : (c + 1) * LANES]
        for o in (2, 1, 3):
            if o < nx:
                cot_copy(mp, o, ((xx + o) & (nx - 1)) * 2 + core).start()
        cot_copy(mp, nx, sibling).start()

    y_copy("a", z, 0, False).wait_recv()
    for sign in (1, -1):
        if half > 1 or at_last(sign, "o"):
            z_copy(sign, "o", 1, True).start()

    step = 32 if rows % 32 == 0 else rows

    def norm_rows(i, carry):
        at = pl.ds(pl.multiple_of(i * step, step), step)
        values = x_ref[at, :].astype(F32)
        inverse = lax.rsqrt(jnp.mean(values * values, axis=1, keepdims=True) + EPS)
        inv_ref[at, :] = jnp.broadcast_to(inverse, (step, LANES))
        normed = (values * inverse * gain_ref[...]).astype(BF16)
        for c in range(features // LANES):
            left0[c, at, :] = normed[:, c * LANES : (c + 1) * LANES]

        @pl.when(encoder)
        def _():
            for c in range(features // LANES):
                left1[c, at, :] = normed[:, c * LANES : (c + 1) * LANES]

        return carry

    count = EX_DEV * n_dp
    far_rows = n_dp * turns * EX_DEV
    enc_r = tuple(t[...].astype(F32) for t in (el_ref, ed_ref))
    dec_r = tuple(t[...].astype(F32) for t in (dl_ref, dd_ref))
    len_r, dev_r = (jnp.where(encoder, a, b) for a, b in zip(enc_r, dec_r))
    far_len_r, far_dev_r = (jnp.where(encoder, b, a) for a, b in zip(enc_r, dec_r))
    here = dp.astype(F32)
    found = {}

    def starts():
        shape = (count, count)
        down = lax.broadcasted_iota(jnp.int32, shape, 0).astype(F32)
        along = lax.broadcasted_iota(jnp.int32, shape, 1).astype(F32)
        one = jnp.ones(shape, F32)

        def column(row):
            return jnp.sum(jnp.where(down == along, row, 0.0), axis=1, keepdims=True)

        len_c, dev_c, far_len_c, far_dev_c = (
            column(t) for t in (len_r, dev_r, far_len_r, far_dev_r)
        )
        above = (dev_r == dev_c) & (down < along)
        before = (dev_r == dev_c) & (along < down)
        found.update(
            down=down,
            len_c=len_c,
            dev_c=dev_c,
            far_len_c=far_len_c,
            start_r=jnp.sum(jnp.where(above, len_c * one, 0.0), axis=0, keepdims=True),
            rank_r=jnp.sum(jnp.where(above, one, 0.0), axis=0, keepdims=True),
            start_c=jnp.sum(jnp.where(before, len_r * one, 0.0), axis=1, keepdims=True),
            rank_c=jnp.sum(jnp.where(before, one, 0.0), axis=1, keepdims=True),
            far_rank_r=jnp.sum(
                jnp.where((far_dev_r == far_dev_c) & (down < along), one, 0.0),
                axis=0,
                keepdims=True,
            ),
            far_start_c=jnp.sum(
                jnp.where((far_dev_r == far_dev_c) & (along < down), far_len_r * one, 0.0),
                axis=1,
                keepdims=True,
            ),
        )

    def own_ranks():
        u_r = lax.broadcasted_iota(jnp.int32, (count, rows), 1).astype(F32)
        start_c, start_r = found["start_c"], found["start_r"]
        mine = (found["dev_c"] == here) & (start_c <= u_r) & (u_r < start_c + found["len_c"])
        along = jnp.sum(
            jnp.where(mine, found["rank_c"] * jnp.ones_like(u_r), 0.0), axis=0, keepdims=True
        )
        u_c = lax.broadcasted_iota(jnp.int32, (rows, count), 0).astype(F32)
        mine = (dev_r == here) & (start_r <= u_c) & (u_c < start_r + len_r)
        down = jnp.sum(
            jnp.where(mine, found["rank_r"] * jnp.ones_like(u_c), 0.0), axis=1, keepdims=True
        )
        far_ref[:, :rows] = jnp.broadcast_to(along, (far_ref.shape[0], rows))
        own_ref[...] = jnp.broadcast_to(down, own_ref.shape)

    def far_ranks():
        c_i = lax.broadcasted_iota(jnp.int32, (count, far_rows), 1)
        rank = (c_i % EX_DEV).astype(F32)
        hit = (found["dev_c"] == here) & (found["rank_c"] == rank)
        one = jnp.ones_like(rank)
        start = jnp.sum(jnp.where(hit, found["far_start_c"] * one, 0.0), axis=0, keepdims=True)
        length = jnp.sum(jnp.where(hit, found["far_len_c"] * one, 0.0), axis=0, keepdims=True)
        c_r = lax.broadcasted_iota(jnp.int32, (1, far_rows), 1)
        offset = (c_r // (turns * EX_DEV) - start.astype(jnp.int32)) & (n_dp - 1)
        offset = offset + c_r % (turns * EX_DEV) // EX_DEV * n_dp
        rank_r = jnp.where(offset.astype(F32) < length, (c_r % EX_DEV).astype(F32), -1.0)

        @pl.when(decoder)
        def _():
            far_ref[...] = jnp.broadcast_to(rank_r, far_ref.shape)

    def spread_rows():
        sent = lax.broadcasted_iota(jnp.int32, (rows, rows), 0)
        row = lax.broadcasted_iota(jnp.int32, (rows, rows), 1)
        here_too = sent % keep * n_dp + sent // keep == row
        spread_ref[...] = jnp.where(here_too, 1.0, 0.0).astype(BF16)

    def pick_rows(turn):
        start_i = found["start_r"].astype(jnp.int32)
        offset = ((dp - start_i) & (n_dp - 1)) + turn * n_dp
        source = dev_r * float(sides * keep) + ((start_i + offset) // n_dp).astype(F32)
        value = jnp.where(offset.astype(F32) < len_r, source + 1.0, 0.0)
        place = far_dev_r * float(EX_DEV) + found["far_rank_r"]
        down = found["down"]
        one = jnp.ones_like(down)
        found[turn] = (
            jnp.sum(jnp.where(place == down, value * one, 0.0), axis=1, keepdims=True) - 1.0
        )

    def pick_side(b, turn):
        fidx = found[turn]
        place = lax.broadcasted_iota(jnp.int32, (count, n_dp * sides * keep), 1).astype(F32)
        at = jnp.where(fidx >= 0.0, fidx + float(b * keep), -1.0)
        pick_ref[b * turns + turn] = jnp.where(place == at, 1.0, 0.0).astype(BF16)

    def product(y, zb):
        total0 = total1 = None
        for row in (y, 1 - y):
            block = row * nz + zb
            at = pl.ds(pl.multiple_of(block * depth, depth), depth)
            p0 = nn(left0[block], wall[at, :width])
            p1 = nn(left1[block], wall[at, width:])
            total0 = p0 if total0 is None else total0 + p0
            total1 = p1 if total1 is None else total1 + p1
        acc[:, :width] += total0
        acc[:, width:] += total1

    def arrived(k, carry):
        hop, up = (k + 1) // 2, k & 1
        zb = (z - jnp.where(up == 1, hop, -hop)) & (nz - 1)
        slot = jnp.where(k == 0, 0, hop + (1 - up) * half)
        for kind in "bc":
            y_copy(kind, zb, slot, False).wait_recv()
        product(yl, zb)
        return carry

    def cot_pass(now):
        @pl.when(decoder & now)
        def _():
            for o in (1, 3, 2):
                if o < nx:
                    owner = (xx - o + nx) % nx * 2 + core
                    cot_copy(owner, o, sibling).wait_recv()
                    cot_copy(owner, nx + o, sibling).start()

    def cot_wait(now):
        @pl.when(decoder & now)
        def _():
            for o in range(nx):
                owner = (xx - o + nx) % nx * 2 + 1 - core
                cot_copy(owner, nx + o, sibling).wait_recv()

    def pass_on(hop, last):
        for kind in order:
            for sign in (1, -1):
                if last and not at_last(sign, kind):
                    continue
                z_copy(sign, kind, hop, False).wait_recv()
                if not last:
                    onward = z_copy(sign, kind, hop + 1, True)
                    if at_last(sign, kind):
                        onward.start()
                    else:
                        pl.when(hop + 1 < half)(onward.start)
                if kind in "bc":
                    slot = hop if sign == 1 else half + hop
                    y_copy(kind, (z - sign * hop) & (nz - 1), slot, True).start()

    acc[...] = jnp.zeros_like(acc)
    spread_rows()
    inputs[2].wait()
    inputs[3].wait()
    norm_hops = max(1, min(4, half - 1))
    chunks = rows // step
    share_of = -(-chunks // norm_hops)

    def one_hop(hop, carry):
        pass_on(hop, False)
        low = jnp.minimum((hop - 1) * share_of, chunks)
        lax.fori_loop(low, jnp.minimum(low + share_of, chunks), norm_rows, 0)
        cot_pass(hop == norm_hops)
        cot_wait(hop == norm_hops + 1)
        high = jnp.where(hop > norm_hops, 2 * hop - 1, 0)
        low = jnp.where(hop > norm_hops + 1, 2 * hop - 3, 0)
        lax.fori_loop(low, high, arrived, 0)
        return carry

    lax.fori_loop(1, half, one_hop, 0)
    if half == 1:
        lax.fori_loop(0, chunks, norm_rows, 0)
        cot_pass(True)
    pass_on(half, True)
    if half - 1 > norm_hops:
        lax.fori_loop(2 * half - 3, 2 * half, arrived, 0)
    else:
        cot_wait(True)
        lax.fori_loop(0, 2 * half, arrived, 0)

    pl.semaphore_signal(cross_sem, inc=1, device_id=(across, dp, mp), device_id_type=MESH)

    def hop_copy(k, src, dst, target_section, target):
        return pltpu.make_async_remote_copy(
            src_ref=src,
            dst_ref=dst,
            send_sem=hop_send.at[k],
            recv_sem=hop_recv.at[k],
            device_id=(target_section, target, mp),
            device_id_type=MESH,
        )

    def wait_bytes(sem, buf, size):
        pltpu.make_async_copy(buf.at[pl.ds(0, size)], buf.at[pl.ds(0, size)], sem).wait()

    def to_all(send):
        def four(k, carry):
            away = half - 1 - k
            for sign in (1, -1):
                for y in (yl, 1 - yl):
                    send(y * nz + ((z + sign * away) & (nz - 1)))
            return carry

        for y in (yl, 1 - yl):
            send(y * nz + ((z + half) & (nz - 1)))
        lax.fori_loop(0, half - 1, four, 0)

    def local_copy(part):
        return pltpu.make_async_copy(
            send1.at[part, dp], in1.at[part, dp], hop_local.at[part]
        )

    for part in range(2):
        at = slice(part * width, (part + 1) * width)
        qkv[:, at] = acc[:, at].astype(BF16)
        moved = nn(spread_ref[...], qkv[:, at]).reshape(n_dp, keep, width)
        pieces = [moved[:, :, b * LANES : (b + 1) * LANES] for b in range(sides)]
        send1[part] = jnp.concatenate(pieces, axis=1).astype(BF16)
        local_copy(part).start()

        def send_to(target, part=part):
            hop_copy(part, send1.at[part, target], in1.at[part, dp], section, target).start()

        to_all(send_to)
        send_to((1 - yl) * nz + z)

    starts()
    own_ranks()
    far_ranks()
    for turn in range(turns):
        pick_rows(turn)
        for b in range(sides):
            pick_side(b, turn)

    for part in range(2):
        local_copy(part).wait()
        wait_bytes(hop_recv.at[part], in1.at[part], n_dp - 1)
        first_in = in1[part].reshape(n_dp * sides * keep, LANES)
        pieces = [
            nn(pick_ref[k], first_in).reshape(n_dp, EX_DEV, LANES) for k in range(sides * turns)
        ]
        send2[part] = jnp.concatenate(pieces, axis=1).astype(BF16)
        if part == 0:
            pl.semaphore_wait(cross_sem, 1)

        def pass_to(target, part=part):
            hop_copy(2 + part, send2.at[part, target], in2.at[part, dp], across, target).start()

        to_all(pass_to)
        pass_to(dp)
        pass_to((1 - yl) * nz + z)

    scale = 1.0 / float(HEAD) ** 0.5
    lane = lax.broadcasted_iota(jnp.int32, (1, LANES), 1) // HEAD
    heads = LANES // HEAD
    per_side = turns * EX_DEV

    def came(part, b):
        return in2[part, :, b * per_side : (b + 1) * per_side, :].reshape(far_rows, LANES)

    def own(part, b):
        return qkv[:, part * width + b * LANES : part * width + (b + 1) * LANES]

    def one_head(t, s):
        return jnp.where(lane == s, t, jnp.zeros_like(t))

    def softmax(q, k, mask):
        weight = jnp.where(mask, jnp.exp(nt(q, k) * scale), 0.0)
        return weight * (1.0 / jnp.sum(weight, axis=1, keepdims=True))

    def backward(probs, dout_s, v):
        probs_bf = probs.astype(BF16)
        attended = nn(probs_bf, v).astype(BF16)
        delta = jnp.sum(dout_s.astype(F32) * attended.astype(F32), axis=1, keepdims=True)
        return probs_bf, (probs * (nt(dout_s, v) - delta) * scale).astype(BF16)

    def merge(news, sums, s):
        return [jnp.where(lane == s, new, old) for new, old in zip(news, sums)] if s else news

    over_z = (nz - 1) * (depth + CUT)
    over_y = CUT + nz * (depth - CUT)
    wait_bytes(w_send_sem, wall, over_z)
    wait_bytes(w_send_sem, wall, over_y)
    for part in range(2):
        wait_bytes(hop_send.at[part], send1.at[part], n_dp - 1)

    @pl.when(decoder)
    def _():
        wait_bytes(cot_send_sem, left1, (2 * nx - 1) * per_mp)

    wait_bytes(hop_recv.at[2], in2.at[0], n_dp)

    @pl.when(encoder)
    def _():
        example = lax.broadcasted_iota(jnp.int32, (far_rows, rows), 0) % EX_DEV
        mask = example.astype(F32) == far_ref[:1, :rows]
        for b in range(sides):
            q = came(0, b)
            for s in range(heads):
                probs_ref[b * heads + s] = softmax(one_head(q, s), own(0, b), mask)

    @pl.when(decoder)
    def _():
        mask = own_ref[:, :1] == far_ref[:1, :]
        for b in range(sides):
            k = came(0, b)
            for s in range(heads):
                probs = softmax(one_head(own(0, b), s), k, mask)
                for c in range(far_rows // rows):
                    probs_ref[b * heads + s, c * rows : (c + 1) * rows, :] = probs[
                        :, c * rows : (c + 1) * rows
                    ]

    wait_bytes(hop_recv.at[3], in2.at[1], n_dp)

    @pl.when(encoder)
    def _():
        for b in range(sides):
            q, dout = came(0, b), came(1, b)
            sums = []
            for s in range(heads):
                probs_bf, dscore = backward(
                    probs_ref[b * heads + s], one_head(dout, s), own(1, b)
                )
                sums = merge((tn(dscore, q), tn(probs_bf, dout)), sums, s)
            for part in range(2):
                low = part * width + b * LANES
                grad[:, low : low + LANES] = sums[part].astype(BF16)

    @pl.when(decoder)
    def _():
        for b in range(sides):
            k, v = came(0, b), came(1, b)
            sums = []
            for s in range(heads):
                probs = jnp.concatenate(
                    [
                        probs_ref[b * heads + s, c * rows : (c + 1) * rows, :]
                        for c in range(far_rows // rows)
                    ],
                    axis=1,
                )
                dscore = backward(probs, one_head(own(1, b), s), v)[1]
                sums = merge((nn(dscore, k),), sums, s)
            grad[:, b * LANES : (b + 1) * LANES] = sums[0].astype(BF16)
        grad[:, width:] = jnp.zeros((rows, width), BF16)

    columns = features // n_mp
    share = jnp.sum(grad[...].astype(F32) * qkv[...].astype(F32), axis=1, keepdims=True)
    inverse = inv_ref[:, :1]
    slope = inverse * inverse * share * (1.0 / features)

    def term(owner, low, size):
        at = pl.ds(pl.multiple_of(owner * columns, columns), columns)
        here_rows = slice(low, low + size)
        raw = nt(grad[here_rows, :], wall[at, :])
        return inverse[here_rows] * (raw * gain_ref[:, at]) - x_ref[
            here_rows, at
        ].astype(F32) * slope[here_rows]

    middle = rows // 2

    def sib_copy(o, h):
        at = pl.ds(h * middle, middle)
        return pltpu.make_async_remote_copy(
            src_ref=sib_send.at[o, at, :],
            dst_ref=sib_recv.at[o, at, :],
            send_sem=c_send.at[0],
            recv_sem=c_sib.at[o, h],
            device_id=(section, dp, sibling),
            device_id_type=MESH,
        )

    def to_sibling(o, h):
        at = slice(h * middle, (h + 1) * middle)
        sib_send[o, at, :] = term(((xx + o) & (nx - 1)) * 2 + 1 - core, h * middle, middle).astype(BF16)
        sib_copy(o, h).start()

    def combined(o, h):
        own_term = term(((xx + o) & (nx - 1)) * 2 + core, h * middle, middle)
        sib_copy(o, h).wait_recv()
        return own_term + sib_recv[o, h * middle : (h + 1) * middle, :].astype(F32)

    def part_copy(slot, o, low, size, sign):
        return pltpu.make_async_remote_copy(
            src_ref=x_send.at[o, pl.ds(low, size), :],
            dst_ref=x_recv.at[o, pl.ds(low, size), :],
            send_sem=c_send.at[1],
            recv_sem=c_x.at[slot],
            device_id=(section, dp, (xx + sign + nx) % nx * 2 + core),
            device_id_type=MESH,
        )

    top, low_half = slice(0, middle), slice(middle, rows)
    parts_sent = []
    if nx == 4:
        far_up = part_copy(0, 2, 0, middle, 1)
        far_down = part_copy(1, 2, middle, middle, -1)
        up_plain = part_copy(2, 1, middle, middle, 1)
        up_added = part_copy(3, 1, 0, middle, 1)
        down_plain = part_copy(4, 3, 0, middle, -1)
        down_added = part_copy(5, 3, middle, middle, -1)
        parts_sent = [far_up, far_down, up_plain, up_added, down_plain, down_added]
        for o, h in ((2, 0), (2, 1), (1, 1), (3, 0)):
            to_sibling(o, h)
        x_send[2, top, :] = combined(2, 0).astype(BF16)
        far_up.start()
        x_send[2, low_half, :] = combined(2, 1).astype(BF16)
        far_down.start()
        to_sibling(1, 0)
        to_sibling(3, 1)
        x_send[1, low_half, :] = combined(1, 1).astype(BF16)
        up_plain.start()
        x_send[3, top, :] = combined(3, 0).astype(BF16)
        down_plain.start()
        to_sibling(0, 0)
        to_sibling(0, 1)
        up = combined(1, 0)
        down = combined(3, 1)
        far_up.wait_recv()
        x_send[1, top, :] = (up + x_recv[2, top, :].astype(F32)).astype(BF16)
        up_added.start()
        far_down.wait_recv()
        x_send[3, low_half, :] = (down + x_recv[2, low_half, :].astype(F32)).astype(BF16)
        down_added.start()
        first, second = combined(0, 0), combined(0, 1)
        down_plain.wait_recv()
        first = first + x_recv[3, top, :].astype(F32)
        up_plain.wait_recv()
        second = second + x_recv[1, low_half, :].astype(F32)
        up_added.wait_recv()
        out_ref[top, :] = (first + x_recv[1, top, :].astype(F32)).astype(BF16)
        down_added.wait_recv()
        out_ref[low_half, :] = (second + x_recv[3, low_half, :].astype(F32)).astype(BF16)
    else:
        for o in range(nx):
            for h in range(2):
                to_sibling(o, h)
        if nx == 2:
            whole = part_copy(0, 1, 0, rows, 1)
            parts_sent += [whole]
            x_send[1, top, :] = combined(1, 0).astype(BF16)
            x_send[1, low_half, :] = combined(1, 1).astype(BF16)
            whole.start()
            whole.wait_recv()
        for h, at in enumerate((top, low_half)):
            result = combined(0, h)
            if nx == 2:
                result = result + x_recv[1, at, :].astype(F32)
            out_ref[at, :] = result.astype(BF16)

    for part in range(2):
        wait_bytes(hop_send.at[2 + part], send2.at[part], n_dp)
    wait_bytes(c_send.at[0], sib_send, nx)
    if nx > 1:
        wait_bytes(c_send.at[1], x_send, nx - 1)


def shards(n_dp, n_mp, layer_rows, cotangent, norm_gains, projections, enc_len, dec_len, enc_dev, dec_dev):
    x = layer_rows[0]
    rows, features = x.shape
    depth, _, width = projections.shape[1:]
    count = enc_len.shape[0]
    tables = [t.reshape(1, count) for t in (enc_len, dec_len, enc_dev, dec_dev)]
    keep = rows // n_dp
    turns = 2 * rows // EX_DEV // n_dp
    sides = width // LANES
    far_rows = n_dp * turns * EX_DEV
    nx = n_mp // 2
    nz = n_dp // 2
    columns = features // n_mp
    vmem = pl.BlockSpec(memory_space=pltpu.VMEM)
    hbm = pl.BlockSpec(memory_space=pl.ANY)
    dma = pltpu.SemaphoreType.DMA
    out = pl.pallas_call(
        functools.partial(kernel, n_dp, n_mp),
        out_shape=jax.ShapeDtypeStruct((rows, columns), BF16),
        in_specs=[hbm] * 4 + [vmem] * 4,
        out_specs=vmem,
        scratch_shapes=[
            pltpu.VMEM((rows, features), BF16),
            pltpu.VMEM((1, features), F32),
            pltpu.VMEM((depth, 2, width), BF16),
            pltpu.VMEM((rows, columns), BF16),
            pltpu.VMEM((features, 2 * width), BF16),
            pltpu.VMEM((features // LANES, rows, LANES), BF16),
            pltpu.VMEM((features // LANES, rows, LANES), BF16),
            pltpu.VMEM((rows, LANES), F32),
            pltpu.VMEM((rows, 2 * width), F32),
            pltpu.VMEM((rows, 2 * width), BF16),
            pltpu.VMEM((rows, 2 * width), BF16),
            pltpu.VMEM((sides * turns, count, n_dp * sides * keep), BF16),
            pltpu.VMEM((rows, LANES), F32),
            pltpu.VMEM((8, far_rows), F32),
            pltpu.VMEM((sides * LANES // HEAD, far_rows, rows), F32),
            pltpu.VMEM((rows, rows), BF16),
            pltpu.VMEM((2, n_dp, sides * keep, LANES), BF16),
            pltpu.VMEM((2, n_dp, sides * keep, LANES), BF16),
            pltpu.VMEM((2, n_dp, sides * turns * EX_DEV, LANES), BF16),
            pltpu.VMEM((2, n_dp, sides * turns * EX_DEV, LANES), BF16),
            pltpu.VMEM((nx, rows, columns), BF16),
            pltpu.VMEM((nx, rows, columns), BF16),
            pltpu.VMEM((nx, rows, columns), BF16),
            pltpu.VMEM((nx, rows, columns), BF16),
            dma((4,)),
            pltpu.SemaphoreType.REGULAR,
            dma((2, 4, max(1, nz // 2))),
            dma((3, nz)),
            dma((2 * nx,)),
            dma,
            dma,
            dma((4,)),
            dma((4,)),
            dma((2,)),
            dma((2,)),
            dma((nx, 2)),
            dma((6,)),
        ],
        compiler_params=pltpu.CompilerParams(
            collective_id=0, has_side_effects=True, vmem_limit_bytes=60 * 2**20
        ),
    )(x, norm_gains, projections[0], cotangent, *tables)
    return out[None]


def solution(mesh):
    placed = (
        P("section", "dp", None),
        P("dp", "mp"),
        P("section", None),
        P("section", "dp", None, "mp"),
        P(),
        P(),
        P(),
        P(),
    )
    return jax.shard_map(
        functools.partial(shards, mesh.shape["dp"], mesh.shape["mp"]),
        mesh=mesh,
        in_specs=placed,
        out_specs=P("section", "dp", "mp"),
        check_vma=False,
    )
```

```python
import functools

import jax
import jax.numpy as jnp
from jax import lax
from jax.experimental import pallas as pl
from jax.experimental.pallas import tpu as pltpu
from jax.sharding import PartitionSpec as P

HEAD = 64
EX_DEV = 8
EPS = 1e-06
LANES = 128
CUT = 48
CUT2 = 96
MESH = pl.DeviceIdType.MESH
F32 = jnp.float32
BF16 = jnp.bfloat16


def nt(a, b):
    return lax.dot_general(a, b, (((1,), (1,)), ((), ())), preferred_element_type=F32)


def tn(a, b):
    return lax.dot_general(a, b, (((0,), (0,)), ((), ())), preferred_element_type=F32)


def nn(a, b):
    return jnp.dot(a, b, preferred_element_type=F32)


def kernel(
    n_dp,
    n_mp,
    x_hbm,
    gain_hbm,
    w_hbm,
    cot_hbm,
    el_ref,
    dl_ref,
    ed_ref,
    dd_ref,
    out_ref,
    x_ref,
    gain_ref,
    w_ref,
    cot_ref,
    wall,
    left0,
    left1,
    inv_ref,
    acc,
    qkv,
    grad,
    pick_ref,
    own_ref,
    far_ref,
    probs_ref,
    spread_ref,
    send1,
    in1,
    send2,
    in2,
    sib_send,
    sib_recv,
    x_send,
    x_recv,
    in_sems,
    cross_sem,
    z_sems,
    y_sems,
    cot_sems,
    w_send_sem,
    cot_send_sem,
    hop_send,
    hop_recv,
    hop_local,
    c_send,
    c_sib,
    c_x,
):
    nz = n_dp // 2
    nx = n_mp // 2
    half = nz // 2
    rows, features = x_ref.shape
    depth, _, width = w_ref.shape
    keep = rows // n_dp
    turns = 2 * rows // EX_DEV // n_dp
    sides = width // LANES
    section = lax.axis_index("section")
    dp = lax.axis_index("dp")
    mp = lax.axis_index("mp")
    yl = dp // nz
    z = dp % nz
    xx = mp // 2
    core = mp % 2
    encoder = section == 0
    decoder = section == 1

    inputs = [
        pltpu.make_async_copy(source, target, in_sems.at[k])
        for k, (source, target) in enumerate(
            ((w_hbm, w_ref), (cot_hbm, cot_ref), (x_hbm, x_ref), (gain_hbm, gain_ref))
        )
    ]
    for copy in inputs:
        copy.start()

    sibling = xx * 2 + 1 - core
    across = 1 - section
    greeted = [(section, yl * nz + (z + 1) % nz, mp), (section, yl * nz + (z + nz - 1) % nz, mp)]
    greeted += [(section, (1 - yl) * nz + z, mp), (across, dp, mp), (section, dp, sibling)]
    greeted += [(section, dp, ((xx + o) & (nx - 1)) * 2 + core) for o in range(1, nx)]
    barrier = pltpu.get_barrier_semaphore()
    for target in greeted:
        pl.semaphore_signal(barrier, inc=1, device_id=target, device_id_type=MESH)
    inputs[0].wait()
    own = pl.ds(pl.multiple_of(dp * depth, depth), depth)
    wall[own, :width] = w_ref[:, 0, :]
    wall[own, width:] = w_ref[:, 1, :]
    pl.semaphore_wait(barrier, len(greeted))

    spans = {"b": (CUT, CUT2 - CUT), "c": (CUT2, depth - CUT2), "a": (0, CUT), "o": (0, CUT)}
    order = ("b", "c", "a", "o")

    def span(kind, y, zb):
        first, size = spans[kind]
        return wall.at[pl.ds(pl.multiple_of((y * nz + zb) * depth + first, 16), size), :]

    def at_last(sign, kind):
        return (kind in "bc") == (sign == 1)

    def z_copy(sign, kind, hop, sending):
        y = 1 - yl if kind == "o" else yl
        back = hop - 1 if sending else hop
        part = span(kind, y, (z - sign * back) & (nz - 1))
        return pltpu.make_async_remote_copy(
            src_ref=part,
            dst_ref=part,
            send_sem=w_send_sem,
            recv_sem=z_sems.at[(1 - sign) // 2, order.index(kind), hop - 1],
            device_id=(section, yl * nz + ((z + sign) & (nz - 1)), mp),
            device_id_type=MESH,
        )

    def y_copy(kind, zb, slot, sending):
        piece = span(kind, yl if sending else 1 - yl, zb)
        return pltpu.make_async_remote_copy(
            src_ref=piece,
            dst_ref=piece,
            send_sem=w_send_sem,
            recv_sem=y_sems.at["bca".index(kind), slot],
            device_id=(section, (1 - yl) * nz + z, mp),
            device_id_type=MESH,
        )

    for kind in ("b", "c", "a"):
        for sign in (1, -1):
            if half > 1 or at_last(sign, kind):
                z_copy(sign, kind, 1, True).start()
        if kind == "b":
            y_copy("a", z, 0, True).start()
    for kind in "bc":
        y_copy(kind, z, 0, True).start()

    per_mp = features // n_mp // LANES

    def cot_copy(owner, slot, target):
        part = left1.at[pl.ds(owner * per_mp, per_mp)]
        return pltpu.make_async_remote_copy(
            src_ref=part,
            dst_ref=part,
            send_sem=cot_send_sem,
            recv_sem=cot_sems.at[slot],
            device_id=(section, dp, target),
            device_id_type=MESH,
        )

    inputs[1].wait()

    @pl.when(decoder)
    def _():
        for c in range(per_mp):
            left1[mp * per_mp + c] = cot_ref[:, c * LANES : (c + 1) * LANES]
        for o in (2, 1, 3):
            if o < nx:
                cot_copy(mp, o, ((xx + o) & (nx - 1)) * 2 + core).start()
        cot_copy(mp, nx, sibling).start()

    y_copy("a", z, 0, False).wait_recv()
    for sign in (1, -1):
        if half > 1 or at_last(sign, "o"):
            z_copy(sign, "o", 1, True).start()

    step = 32 if rows % 32 == 0 else rows

    def norm_rows(i, carry):
        at = pl.ds(pl.multiple_of(i * step, step), step)
        values = x_ref[at, :].astype(F32)
        inverse = lax.rsqrt(jnp.mean(values * values, axis=1, keepdims=True) + EPS)
        inv_ref[at, :] = jnp.broadcast_to(inverse, (step, LANES))
        normed = (values * inverse * gain_ref[...]).astype(BF16)
        for c in range(features // LANES):
            left0[c, at, :] = normed[:, c * LANES : (c + 1) * LANES]

        @pl.when(encoder)
        def _():
            for c in range(features // LANES):
                left1[c, at, :] = normed[:, c * LANES : (c + 1) * LANES]

        return carry

    count = EX_DEV * n_dp
    far_rows = n_dp * turns * EX_DEV
    enc_r = tuple(t[...].astype(F32) for t in (el_ref, ed_ref))
    dec_r = tuple(t[...].astype(F32) for t in (dl_ref, dd_ref))
    len_r, dev_r = (jnp.where(encoder, a, b) for a, b in zip(enc_r, dec_r))
    far_len_r, far_dev_r = (jnp.where(encoder, b, a) for a, b in zip(enc_r, dec_r))
    here = dp.astype(F32)
    found = {}

    def starts():
        shape = (count, count)
        down = lax.broadcasted_iota(jnp.int32, shape, 0).astype(F32)
        along = lax.broadcasted_iota(jnp.int32, shape, 1).astype(F32)
        one = jnp.ones(shape, F32)

        def column(row):
            return jnp.sum(jnp.where(down == along, row, 0.0), axis=1, keepdims=True)

        len_c, dev_c, far_len_c, far_dev_c = (
            column(t) for t in (len_r, dev_r, far_len_r, far_dev_r)
        )
        above = (dev_r == dev_c) & (down < along)
        before = (dev_r == dev_c) & (along < down)
        found.update(
            down=down,
            len_c=len_c,
            dev_c=dev_c,
            far_len_c=far_len_c,
            start_r=jnp.sum(jnp.where(above, len_c * one, 0.0), axis=0, keepdims=True),
            rank_r=jnp.sum(jnp.where(above, one, 0.0), axis=0, keepdims=True),
            start_c=jnp.sum(jnp.where(before, len_r * one, 0.0), axis=1, keepdims=True),
            rank_c=jnp.sum(jnp.where(before, one, 0.0), axis=1, keepdims=True),
            far_rank_r=jnp.sum(
                jnp.where((far_dev_r == far_dev_c) & (down < along), one, 0.0),
                axis=0,
                keepdims=True,
            ),
            far_start_c=jnp.sum(
                jnp.where((far_dev_r == far_dev_c) & (along < down), far_len_r * one, 0.0),
                axis=1,
                keepdims=True,
            ),
        )

    def own_ranks():
        u_r = lax.broadcasted_iota(jnp.int32, (count, rows), 1).astype(F32)
        start_c, start_r = found["start_c"], found["start_r"]
        mine = (found["dev_c"] == here) & (start_c <= u_r) & (u_r < start_c + found["len_c"])
        along = jnp.sum(
            jnp.where(mine, found["rank_c"] * jnp.ones_like(u_r), 0.0), axis=0, keepdims=True
        )
        u_c = lax.broadcasted_iota(jnp.int32, (rows, count), 0).astype(F32)
        mine = (dev_r == here) & (start_r <= u_c) & (u_c < start_r + len_r)
        down = jnp.sum(
            jnp.where(mine, found["rank_r"] * jnp.ones_like(u_c), 0.0), axis=1, keepdims=True
        )
        far_ref[:, :rows] = jnp.broadcast_to(along, (far_ref.shape[0], rows))
        own_ref[...] = jnp.broadcast_to(down, own_ref.shape)

    def far_ranks():
        c_i = lax.broadcasted_iota(jnp.int32, (count, far_rows), 1)
        rank = (c_i % EX_DEV).astype(F32)
        hit = (found["dev_c"] == here) & (found["rank_c"] == rank)
        one = jnp.ones_like(rank)
        start = jnp.sum(jnp.where(hit, found["far_start_c"] * one, 0.0), axis=0, keepdims=True)
        length = jnp.sum(jnp.where(hit, found["far_len_c"] * one, 0.0), axis=0, keepdims=True)
        c_r = lax.broadcasted_iota(jnp.int32, (1, far_rows), 1)
        offset = (c_r // (turns * EX_DEV) - start.astype(jnp.int32)) & (n_dp - 1)
        offset = offset + c_r % (turns * EX_DEV) // EX_DEV * n_dp
        rank_r = jnp.where(offset.astype(F32) < length, (c_r % EX_DEV).astype(F32), -1.0)

        @pl.when(decoder)
        def _():
            far_ref[...] = jnp.broadcast_to(rank_r, far_ref.shape)

    def spread_rows():
        sent = lax.broadcasted_iota(jnp.int32, (rows, rows), 0)
        row = lax.broadcasted_iota(jnp.int32, (rows, rows), 1)
        here_too = sent % keep * n_dp + sent // keep == row
        spread_ref[...] = jnp.where(here_too, 1.0, 0.0).astype(BF16)

    def pick_rows(turn):
        start_i = found["start_r"].astype(jnp.int32)
        offset = ((dp - start_i) & (n_dp - 1)) + turn * n_dp
        source = dev_r * float(sides * keep) + ((start_i + offset) // n_dp).astype(F32)
        value = jnp.where(offset.astype(F32) < len_r, source + 1.0, 0.0)
        place = far_dev_r * float(EX_DEV) + found["far_rank_r"]
        down = found["down"]
        one = jnp.ones_like(down)
        found[turn] = (
            jnp.sum(jnp.where(place == down, value * one, 0.0), axis=1, keepdims=True) - 1.0
        )

    def pick_side(b, turn):
        fidx = found[turn]
        place = lax.broadcasted_iota(jnp.int32, (count, n_dp * sides * keep), 1).astype(F32)
        at = jnp.where(fidx >= 0.0, fidx + float(b * keep), -1.0)
        pick_ref[b * turns + turn] = jnp.where(place == at, 1.0, 0.0).astype(BF16)

    def product(y, zb):
        total0 = total1 = None
        for row in (y, 1 - y):
            block = row * nz + zb
            at = pl.ds(pl.multiple_of(block * depth, depth), depth)
            p0 = nn(left0[block], wall[at, :width])
            p1 = nn(left1[block], wall[at, width:])
            total0 = p0 if total0 is None else total0 + p0
            total1 = p1 if total1 is None else total1 + p1
        acc[:, :width] += total0
        acc[:, width:] += total1

    def arrived(k, carry):
        hop, up = (k + 1) // 2, k & 1
        zb = (z - jnp.where(up == 1, hop, -hop)) & (nz - 1)
        slot = jnp.where(k == 0, 0, hop + (1 - up) * half)
        for kind in "bc":
            y_copy(kind, zb, slot, False).wait_recv()
        product(yl, zb)
        return carry

    def cot_pass(now):
        @pl.when(decoder & now)
        def _():
            for o in (1, 3, 2):
                if o < nx:
                    owner = (xx - o + nx) % nx * 2 + core
                    cot_copy(owner, o, sibling).wait_recv()
                    cot_copy(owner, nx + o, sibling).start()

    def cot_wait(now):
        @pl.when(decoder & now)
        def _():
            for o in range(nx):
                owner = (xx - o + nx) % nx * 2 + 1 - core
                cot_copy(owner, nx + o, sibling).wait_recv()

    def pass_on(hop, last, kinds=order):
        for kind in kinds:
            for sign in (1, -1):
                if last and not at_last(sign, kind):
                    continue
                z_copy(sign, kind, hop, False).wait_recv()
                if not last:
                    onward = z_copy(sign, kind, hop + 1, True)
                    if at_last(sign, kind):
                        onward.start()
                    else:
                        pl.when(hop + 1 < half)(onward.start)
                if kind in "bc":
                    slot = hop if sign == 1 else half + hop
                    y_copy(kind, (z - sign * hop) & (nz - 1), slot, True).start()

    acc[...] = jnp.zeros_like(acc)
    spread_rows()
    inputs[2].wait()
    inputs[3].wait()
    norm_hops = max(1, min(4, half - 1))
    chunks = rows // step
    share_of = -(-chunks // norm_hops)
    quota = 5

    def some_work(hop, slot):
        first = jnp.minimum((hop - 1) * share_of, chunks)
        middle = jnp.minimum(first + share_of // 2, chunks)
        end = jnp.minimum(first + share_of, chunks)
        bounds = (first, middle, end)
        lax.fori_loop(bounds[slot], bounds[slot + 1], norm_rows, 0)
        first = (hop - norm_hops - 1) * quota
        bounds = (first, first + 3, jnp.minimum(first + quota, 2 * hop - 1))
        late = hop > norm_hops
        low = jnp.where(late, bounds[slot], 0)
        high = jnp.where(late, jnp.minimum(bounds[slot + 1], 2 * hop - 1), 0)
        lax.fori_loop(low, high, arrived, 0)

    def one_hop(hop, carry):
        pass_on(hop, False, order[:2])
        cot_pass(hop == norm_hops)
        cot_wait(hop == norm_hops + 1)
        some_work(hop, 0)
        pass_on(hop, False, order[2:])
        some_work(hop, 1)
        return carry

    lax.fori_loop(1, half, one_hop, 0)
    if half == 1:
        lax.fori_loop(0, chunks, norm_rows, 0)
        cot_pass(True)
    pass_on(half, True)
    if half - 1 > norm_hops:
        done = min((half - 1 - norm_hops) * quota, 2 * half - 3)
        lax.fori_loop(done, 2 * half, arrived, 0)
    else:
        cot_wait(True)
        lax.fori_loop(0, 2 * half, arrived, 0)

    pl.semaphore_signal(cross_sem, inc=1, device_id=(across, dp, mp), device_id_type=MESH)

    def hop_copy(k, src, dst, target_section, target):
        return pltpu.make_async_remote_copy(
            src_ref=src,
            dst_ref=dst,
            send_sem=hop_send.at[k],
            recv_sem=hop_recv.at[k],
            device_id=(target_section, target, mp),
            device_id_type=MESH,
        )

    def wait_bytes(sem, buf, size):
        pltpu.make_async_copy(buf.at[pl.ds(0, size)], buf.at[pl.ds(0, size)], sem).wait()

    def to_all(send):
        def four(k, carry):
            away = half - 1 - k
            for sign in (1, -1):
                for y in (yl, 1 - yl):
                    send(y * nz + ((z + sign * away) & (nz - 1)))
            return carry

        for y in (yl, 1 - yl):
            send(y * nz + ((z + half) & (nz - 1)))
        lax.fori_loop(0, half - 1, four, 0)

    def local_copy(part):
        return pltpu.make_async_copy(
            send1.at[part, dp], in1.at[part, dp], hop_local.at[part]
        )

    for part in range(2):
        at = slice(part * width, (part + 1) * width)
        qkv[:, at] = acc[:, at].astype(BF16)
        moved = nn(spread_ref[...], qkv[:, at]).reshape(n_dp, keep, width)
        pieces = [moved[:, :, b * LANES : (b + 1) * LANES] for b in range(sides)]
        send1[part] = jnp.concatenate(pieces, axis=1).astype(BF16)
        local_copy(part).start()

        def send_to(target, part=part):
            hop_copy(part, send1.at[part, target], in1.at[part, dp], section, target).start()

        to_all(send_to)
        send_to((1 - yl) * nz + z)

    starts()
    own_ranks()
    far_ranks()
    for turn in range(turns):
        pick_rows(turn)
        for b in range(sides):
            pick_side(b, turn)

    for part in range(2):
        local_copy(part).wait()
        wait_bytes(hop_recv.at[part], in1.at[part], n_dp - 1)
        first_in = in1[part].reshape(n_dp * sides * keep, LANES)
        pieces = [
            nn(pick_ref[k], first_in).reshape(n_dp, EX_DEV, LANES) for k in range(sides * turns)
        ]
        send2[part] = jnp.concatenate(pieces, axis=1).astype(BF16)
        if part == 0:
            pl.semaphore_wait(cross_sem, 1)

        def pass_to(target, part=part):
            hop_copy(2 + part, send2.at[part, target], in2.at[part, dp], across, target).start()

        to_all(pass_to)
        pass_to(dp)
        pass_to((1 - yl) * nz + z)

    scale = 1.0 / float(HEAD) ** 0.5
    lane = lax.broadcasted_iota(jnp.int32, (1, LANES), 1) // HEAD
    heads = LANES // HEAD
    per_side = turns * EX_DEV

    def came(part, b):
        return in2[part, :, b * per_side : (b + 1) * per_side, :].reshape(far_rows, LANES)

    def own(part, b):
        return qkv[:, part * width + b * LANES : part * width + (b + 1) * LANES]

    def one_head(t, s):
        return jnp.where(lane == s, t, jnp.zeros_like(t))

    def softmax(q, k, mask):
        weight = jnp.where(mask, jnp.exp(nt(q, k) * scale), 0.0)
        return weight * (1.0 / jnp.sum(weight, axis=1, keepdims=True))

    def backward(probs, dout_s, v):
        probs_bf = probs.astype(BF16)
        attended = nn(probs_bf, v).astype(BF16)
        delta = jnp.sum(dout_s.astype(F32) * attended.astype(F32), axis=1, keepdims=True)
        return probs_bf, (probs * (nt(dout_s, v) - delta) * scale).astype(BF16)

    def merge(news, sums, s):
        return [jnp.where(lane == s, new, old) for new, old in zip(news, sums)] if s else news

    over_z = (nz - 1) * (depth + CUT)
    over_y = CUT + nz * (depth - CUT)
    wait_bytes(w_send_sem, wall, over_z)
    wait_bytes(w_send_sem, wall, over_y)
    for part in range(2):
        wait_bytes(hop_send.at[part], send1.at[part], n_dp - 1)

    @pl.when(decoder)
    def _():
        wait_bytes(cot_send_sem, left1, (2 * nx - 1) * per_mp)

    wait_bytes(hop_recv.at[2], in2.at[0], n_dp)

    @pl.when(encoder)
    def _():
        example = lax.broadcasted_iota(jnp.int32, (far_rows, rows), 0) % EX_DEV
        mask = example.astype(F32) == far_ref[:1, :rows]
        for b in range(sides):
            q = came(0, b)
            for s in range(heads):
                probs_ref[b * heads + s] = softmax(one_head(q, s), own(0, b), mask)

    @pl.when(decoder)
    def _():
        mask = own_ref[:, :1] == far_ref[:1, :]
        for b in range(sides):
            k = came(0, b)
            for s in range(heads):
                probs = softmax(one_head(own(0, b), s), k, mask)
                for c in range(far_rows // rows):
                    probs_ref[b * heads + s, c * rows : (c + 1) * rows, :] = probs[
                        :, c * rows : (c + 1) * rows
                    ]

    wait_bytes(hop_recv.at[3], in2.at[1], n_dp)

    @pl.when(encoder)
    def _():
        for b in range(sides):
            q, dout = came(0, b), came(1, b)
            sums = []
            for s in range(heads):
                probs_bf, dscore = backward(
                    probs_ref[b * heads + s], one_head(dout, s), own(1, b)
                )
                sums = merge((tn(dscore, q), tn(probs_bf, dout)), sums, s)
            for part in range(2):
                low = part * width + b * LANES
                grad[:, low : low + LANES] = sums[part].astype(BF16)

    @pl.when(decoder)
    def _():
        for b in range(sides):
            k, v = came(0, b), came(1, b)
            sums = []
            for s in range(heads):
                probs = jnp.concatenate(
                    [
                        probs_ref[b * heads + s, c * rows : (c + 1) * rows, :]
                        for c in range(far_rows // rows)
                    ],
                    axis=1,
                )
                dscore = backward(probs, one_head(own(1, b), s), v)[1]
                sums = merge((nn(dscore, k),), sums, s)
            grad[:, b * LANES : (b + 1) * LANES] = sums[0].astype(BF16)
        grad[:, width:] = jnp.zeros((rows, width), BF16)

    columns = features // n_mp
    share = jnp.sum(grad[...].astype(F32) * qkv[...].astype(F32), axis=1, keepdims=True)
    inverse = inv_ref[:, :1]
    slope = inverse * inverse * share * (1.0 / features)

    def term(owner, low, size):
        at = pl.ds(pl.multiple_of(owner * columns, columns), columns)
        here_rows = slice(low, low + size)
        raw = nt(grad[here_rows, :], wall[at, :])
        return inverse[here_rows] * (raw * gain_ref[:, at]) - x_ref[
            here_rows, at
        ].astype(F32) * slope[here_rows]

    middle = rows // 2

    def sib_copy(o, h):
        at = pl.ds(h * middle, middle)
        return pltpu.make_async_remote_copy(
            src_ref=sib_send.at[o, at, :],
            dst_ref=sib_recv.at[o, at, :],
            send_sem=c_send.at[0],
            recv_sem=c_sib.at[o, h],
            device_id=(section, dp, sibling),
            device_id_type=MESH,
        )

    def to_sibling(o, h):
        at = slice(h * middle, (h + 1) * middle)
        sib_send[o, at, :] = term(((xx + o) & (nx - 1)) * 2 + 1 - core, h * middle, middle).astype(BF16)
        sib_copy(o, h).start()

    def combined(o, h):
        own_term = term(((xx + o) & (nx - 1)) * 2 + core, h * middle, middle)
        sib_copy(o, h).wait_recv()
        return own_term + sib_recv[o, h * middle : (h + 1) * middle, :].astype(F32)

    def part_copy(slot, o, low, size, sign):
        return pltpu.make_async_remote_copy(
            src_ref=x_send.at[o, pl.ds(low, size), :],
            dst_ref=x_recv.at[o, pl.ds(low, size), :],
            send_sem=c_send.at[1],
            recv_sem=c_x.at[slot],
            device_id=(section, dp, (xx + sign + nx) % nx * 2 + core),
            device_id_type=MESH,
        )

    top, low_half = slice(0, middle), slice(middle, rows)
    parts_sent = []
    if nx == 4:
        far_up = part_copy(0, 2, 0, middle, 1)
        far_down = part_copy(1, 2, middle, middle, -1)
        up_plain = part_copy(2, 1, middle, middle, 1)
        up_added = part_copy(3, 1, 0, middle, 1)
        down_plain = part_copy(4, 3, 0, middle, -1)
        down_added = part_copy(5, 3, middle, middle, -1)
        parts_sent = [far_up, far_down, up_plain, up_added, down_plain, down_added]
        for o, h in ((2, 0), (2, 1), (1, 1), (3, 0)):
            to_sibling(o, h)
        x_send[2, top, :] = combined(2, 0).astype(BF16)
        far_up.start()
        x_send[2, low_half, :] = combined(2, 1).astype(BF16)
        far_down.start()
        to_sibling(1, 0)
        to_sibling(3, 1)
        x_send[1, low_half, :] = combined(1, 1).astype(BF16)
        up_plain.start()
        x_send[3, top, :] = combined(3, 0).astype(BF16)
        down_plain.start()
        to_sibling(0, 0)
        to_sibling(0, 1)
        up = combined(1, 0)
        down = combined(3, 1)
        far_up.wait_recv()
        x_send[1, top, :] = (up + x_recv[2, top, :].astype(F32)).astype(BF16)
        up_added.start()
        far_down.wait_recv()
        x_send[3, low_half, :] = (down + x_recv[2, low_half, :].astype(F32)).astype(BF16)
        down_added.start()
        first, second = combined(0, 0), combined(0, 1)
        down_plain.wait_recv()
        first = first + x_recv[3, top, :].astype(F32)
        up_plain.wait_recv()
        second = second + x_recv[1, low_half, :].astype(F32)
        up_added.wait_recv()
        out_ref[top, :] = (first + x_recv[1, top, :].astype(F32)).astype(BF16)
        down_added.wait_recv()
        out_ref[low_half, :] = (second + x_recv[3, low_half, :].astype(F32)).astype(BF16)
    else:
        for o in range(nx):
            for h in range(2):
                to_sibling(o, h)
        if nx == 2:
            whole = part_copy(0, 1, 0, rows, 1)
            parts_sent += [whole]
            x_send[1, top, :] = combined(1, 0).astype(BF16)
            x_send[1, low_half, :] = combined(1, 1).astype(BF16)
            whole.start()
            whole.wait_recv()
        for h, at in enumerate((top, low_half)):
            result = combined(0, h)
            if nx == 2:
                result = result + x_recv[1, at, :].astype(F32)
            out_ref[at, :] = result.astype(BF16)

    for part in range(2):
        wait_bytes(hop_send.at[2 + part], send2.at[part], n_dp)
    wait_bytes(c_send.at[0], sib_send, nx)
    if nx > 1:
        wait_bytes(c_send.at[1], x_send, nx - 1)


def shards(n_dp, n_mp, layer_rows, cotangent, norm_gains, projections, enc_len, dec_len, enc_dev, dec_dev):
    x = layer_rows[0]
    rows, features = x.shape
    depth, _, width = projections.shape[1:]
    count = enc_len.shape[0]
    tables = [t.reshape(1, count) for t in (enc_len, dec_len, enc_dev, dec_dev)]
    keep = rows // n_dp
    turns = 2 * rows // EX_DEV // n_dp
    sides = width // LANES
    far_rows = n_dp * turns * EX_DEV
    nx = n_mp // 2
    nz = n_dp // 2
    columns = features // n_mp
    vmem = pl.BlockSpec(memory_space=pltpu.VMEM)
    hbm = pl.BlockSpec(memory_space=pl.ANY)
    dma = pltpu.SemaphoreType.DMA
    out = pl.pallas_call(
        functools.partial(kernel, n_dp, n_mp),
        out_shape=jax.ShapeDtypeStruct((rows, columns), BF16),
        in_specs=[hbm] * 4 + [vmem] * 4,
        out_specs=vmem,
        scratch_shapes=[
            pltpu.VMEM((rows, features), BF16),
            pltpu.VMEM((1, features), F32),
            pltpu.VMEM((depth, 2, width), BF16),
            pltpu.VMEM((rows, columns), BF16),
            pltpu.VMEM((features, 2 * width), BF16),
            pltpu.VMEM((features // LANES, rows, LANES), BF16),
            pltpu.VMEM((features // LANES, rows, LANES), BF16),
            pltpu.VMEM((rows, LANES), F32),
            pltpu.VMEM((rows, 2 * width), F32),
            pltpu.VMEM((rows, 2 * width), BF16),
            pltpu.VMEM((rows, 2 * width), BF16),
            pltpu.VMEM((sides * turns, count, n_dp * sides * keep), BF16),
            pltpu.VMEM((rows, LANES), F32),
            pltpu.VMEM((8, far_rows), F32),
            pltpu.VMEM((sides * LANES // HEAD, far_rows, rows), F32),
            pltpu.VMEM((rows, rows), BF16),
            pltpu.VMEM((2, n_dp, sides * keep, LANES), BF16),
            pltpu.VMEM((2, n_dp, sides * keep, LANES), BF16),
            pltpu.VMEM((2, n_dp, sides * turns * EX_DEV, LANES), BF16),
            pltpu.VMEM((2, n_dp, sides * turns * EX_DEV, LANES), BF16),
            pltpu.VMEM((nx, rows, columns), BF16),
            pltpu.VMEM((nx, rows, columns), BF16),
            pltpu.VMEM((nx, rows, columns), BF16),
            pltpu.VMEM((nx, rows, columns), BF16),
            dma((4,)),
            pltpu.SemaphoreType.REGULAR,
            dma((2, 4, max(1, nz // 2))),
            dma((3, nz)),
            dma((2 * nx,)),
            dma,
            dma,
            dma((4,)),
            dma((4,)),
            dma((2,)),
            dma((2,)),
            dma((nx, 2)),
            dma((6,)),
        ],
        compiler_params=pltpu.CompilerParams(
            collective_id=0, has_side_effects=True, vmem_limit_bytes=60 * 2**20
        ),
    )(x, norm_gains, projections[0], cotangent, *tables)
    return out[None]


def solution(mesh):
    placed = (
        P("section", "dp", None),
        P("dp", "mp"),
        P("section", None),
        P("section", "dp", None, "mp"),
        P(),
        P(),
        P(),
        P(),
    )
    return jax.shard_map(
        functools.partial(shards, mesh.shape["dp"], mesh.shape["mp"]),
        mesh=mesh,
        in_specs=placed,
        out_specs=P("section", "dp", "mp"),
        check_vma=False,
    )
```

```python
import functools

import jax
import jax.numpy as jnp
from jax import lax
from jax.experimental import pallas as pl
from jax.experimental.pallas import tpu as pltpu
from jax.sharding import PartitionSpec as P

HEAD = 64
EX_DEV = 8
EPS = 1e-06
LANES = 128
CUT = 48
CUT2 = 96
MESH = pl.DeviceIdType.MESH
F32 = jnp.float32
BF16 = jnp.bfloat16


def nt(a, b):
    return lax.dot_general(a, b, (((1,), (1,)), ((), ())), preferred_element_type=F32)


def tn(a, b):
    return lax.dot_general(a, b, (((0,), (0,)), ((), ())), preferred_element_type=F32)


def nn(a, b):
    return jnp.dot(a, b, preferred_element_type=F32)


def kernel(
    n_dp,
    n_mp,
    x_hbm,
    gain_hbm,
    w_hbm,
    cot_hbm,
    el_ref,
    dl_ref,
    ed_ref,
    dd_ref,
    out_ref,
    x_ref,
    gain_ref,
    w_ref,
    cot_ref,
    wall,
    left0,
    left1,
    inv_ref,
    acc,
    qkv,
    grad,
    pick_ref,
    own_ref,
    far_ref,
    probs_ref,
    spread_ref,
    send1,
    in1,
    send2,
    in2,
    sib_send,
    sib_recv,
    x_send,
    x_recv,
    in_sems,
    cross_sem,
    z_sems,
    y_sems,
    cot_sems,
    w_send_sem,
    cot_send_sem,
    hop_send,
    hop_recv,
    hop_local,
    c_send,
    c_sib,
    c_x,
):
    nz = n_dp // 2
    nx = n_mp // 2
    half = nz // 2
    rows, features = x_ref.shape
    depth, _, width = w_ref.shape
    keep = rows // n_dp
    turns = 2 * rows // EX_DEV // n_dp
    sides = width // LANES
    section = lax.axis_index("section")
    dp = lax.axis_index("dp")
    mp = lax.axis_index("mp")
    yl = dp // nz
    z = dp % nz
    xx = mp // 2
    core = mp % 2
    encoder = section == 0
    decoder = section == 1

    inputs = [
        pltpu.make_async_copy(source, target, in_sems.at[k])
        for k, (source, target) in enumerate(
            ((w_hbm, w_ref), (cot_hbm, cot_ref), (x_hbm, x_ref), (gain_hbm, gain_ref))
        )
    ]
    for copy in inputs:
        copy.start()

    sibling = xx * 2 + 1 - core
    across = 1 - section
    greeted = [(section, yl * nz + (z + 1) % nz, mp), (section, yl * nz + (z + nz - 1) % nz, mp)]
    greeted += [(section, (1 - yl) * nz + z, mp), (across, dp, mp), (section, dp, sibling)]
    greeted += [(section, dp, ((xx + o) & (nx - 1)) * 2 + core) for o in range(1, nx)]
    barrier = pltpu.get_barrier_semaphore()
    for target in greeted:
        pl.semaphore_signal(barrier, inc=1, device_id=target, device_id_type=MESH)
    inputs[0].wait()
    own = pl.ds(pl.multiple_of(dp * depth, depth), depth)
    wall[own, :width] = w_ref[:, 0, :]
    wall[own, width:] = w_ref[:, 1, :]
    pl.semaphore_wait(barrier, len(greeted))

    spans = {"b": (CUT, CUT2 - CUT), "c": (CUT2, depth - CUT2), "a": (0, CUT), "o": (0, CUT)}
    order = ("b", "c", "a", "o")

    def span(kind, y, zb):
        first, size = spans[kind]
        return wall.at[pl.ds(pl.multiple_of((y * nz + zb) * depth + first, 16), size), :]

    def at_last(sign, kind):
        return (kind in "bc") == (sign == 1)

    def z_copy(sign, kind, hop, sending):
        y = 1 - yl if kind == "o" else yl
        back = hop - 1 if sending else hop
        part = span(kind, y, (z - sign * back) & (nz - 1))
        return pltpu.make_async_remote_copy(
            src_ref=part,
            dst_ref=part,
            send_sem=w_send_sem,
            recv_sem=z_sems.at[(1 - sign) // 2, order.index(kind), hop - 1],
            device_id=(section, yl * nz + ((z + sign) & (nz - 1)), mp),
            device_id_type=MESH,
        )

    def y_copy(kind, zb, slot, sending):
        piece = span(kind, yl if sending else 1 - yl, zb)
        return pltpu.make_async_remote_copy(
            src_ref=piece,
            dst_ref=piece,
            send_sem=w_send_sem,
            recv_sem=y_sems.at["bca".index(kind), slot],
            device_id=(section, (1 - yl) * nz + z, mp),
            device_id_type=MESH,
        )

    for kind in ("b", "c", "a"):
        for sign in (1, -1):
            if half > 1 or at_last(sign, kind):
                z_copy(sign, kind, 1, True).start()
        if kind == "b":
            y_copy("a", z, 0, True).start()
    for kind in "bc":
        y_copy(kind, z, 0, True).start()

    per_mp = features // n_mp // LANES

    def cot_copy(owner, slot, target):
        part = left1.at[pl.ds(owner * per_mp, per_mp)]
        return pltpu.make_async_remote_copy(
            src_ref=part,
            dst_ref=part,
            send_sem=cot_send_sem,
            recv_sem=cot_sems.at[slot],
            device_id=(section, dp, target),
            device_id_type=MESH,
        )

    inputs[1].wait()

    @pl.when(decoder)
    def _():
        for c in range(per_mp):
            left1[mp * per_mp + c] = cot_ref[:, c * LANES : (c + 1) * LANES]
        for o in (2, 1, 3):
            if o < nx:
                cot_copy(mp, o, ((xx + o) & (nx - 1)) * 2 + core).start()
        cot_copy(mp, nx, sibling).start()

    y_copy("a", z, 0, False).wait_recv()
    for sign in (1, -1):
        if half > 1 or at_last(sign, "o"):
            z_copy(sign, "o", 1, True).start()

    step = 32 if rows % 32 == 0 else rows

    def norm_rows(i, carry):
        at = pl.ds(pl.multiple_of(i * step, step), step)
        values = x_ref[at, :].astype(F32)
        inverse = lax.rsqrt(jnp.mean(values * values, axis=1, keepdims=True) + EPS)
        inv_ref[at, :] = jnp.broadcast_to(inverse, (step, LANES))
        normed = (values * inverse * gain_ref[...]).astype(BF16)
        for c in range(features // LANES):
            left0[c, at, :] = normed[:, c * LANES : (c + 1) * LANES]

        @pl.when(encoder)
        def _():
            for c in range(features // LANES):
                left1[c, at, :] = normed[:, c * LANES : (c + 1) * LANES]

        return carry

    count = EX_DEV * n_dp
    far_rows = n_dp * turns * EX_DEV
    enc_r = tuple(t[...].astype(F32) for t in (el_ref, ed_ref))
    dec_r = tuple(t[...].astype(F32) for t in (dl_ref, dd_ref))
    len_r, dev_r = (jnp.where(encoder, a, b) for a, b in zip(enc_r, dec_r))
    far_len_r, far_dev_r = (jnp.where(encoder, b, a) for a, b in zip(enc_r, dec_r))
    here = dp.astype(F32)
    found = {}

    def starts():
        shape = (count, count)
        down = lax.broadcasted_iota(jnp.int32, shape, 0).astype(F32)
        along = lax.broadcasted_iota(jnp.int32, shape, 1).astype(F32)
        one = jnp.ones(shape, F32)

        def column(row):
            return jnp.sum(jnp.where(down == along, row, 0.0), axis=1, keepdims=True)

        len_c, dev_c, far_len_c, far_dev_c = (
            column(t) for t in (len_r, dev_r, far_len_r, far_dev_r)
        )
        above = (dev_r == dev_c) & (down < along)
        before = (dev_r == dev_c) & (along < down)
        found.update(
            down=down,
            len_c=len_c,
            dev_c=dev_c,
            far_len_c=far_len_c,
            start_r=jnp.sum(jnp.where(above, len_c * one, 0.0), axis=0, keepdims=True),
            rank_r=jnp.sum(jnp.where(above, one, 0.0), axis=0, keepdims=True),
            start_c=jnp.sum(jnp.where(before, len_r * one, 0.0), axis=1, keepdims=True),
            rank_c=jnp.sum(jnp.where(before, one, 0.0), axis=1, keepdims=True),
            far_rank_r=jnp.sum(
                jnp.where((far_dev_r == far_dev_c) & (down < along), one, 0.0),
                axis=0,
                keepdims=True,
            ),
            far_start_c=jnp.sum(
                jnp.where((far_dev_r == far_dev_c) & (along < down), far_len_r * one, 0.0),
                axis=1,
                keepdims=True,
            ),
        )

    def own_ranks():
        u_r = lax.broadcasted_iota(jnp.int32, (count, rows), 1).astype(F32)
        start_c, start_r = found["start_c"], found["start_r"]
        mine = (found["dev_c"] == here) & (start_c <= u_r) & (u_r < start_c + found["len_c"])
        along = jnp.sum(
            jnp.where(mine, found["rank_c"] * jnp.ones_like(u_r), 0.0), axis=0, keepdims=True
        )
        u_c = lax.broadcasted_iota(jnp.int32, (rows, count), 0).astype(F32)
        mine = (dev_r == here) & (start_r <= u_c) & (u_c < start_r + len_r)
        down = jnp.sum(
            jnp.where(mine, found["rank_r"] * jnp.ones_like(u_c), 0.0), axis=1, keepdims=True
        )
        far_ref[:, :rows] = jnp.broadcast_to(along, (far_ref.shape[0], rows))
        own_ref[...] = jnp.broadcast_to(down, own_ref.shape)

    def far_ranks():
        c_i = lax.broadcasted_iota(jnp.int32, (count, far_rows), 1)
        rank = (c_i % EX_DEV).astype(F32)
        hit = (found["dev_c"] == here) & (found["rank_c"] == rank)
        one = jnp.ones_like(rank)
        start = jnp.sum(jnp.where(hit, found["far_start_c"] * one, 0.0), axis=0, keepdims=True)
        length = jnp.sum(jnp.where(hit, found["far_len_c"] * one, 0.0), axis=0, keepdims=True)
        c_r = lax.broadcasted_iota(jnp.int32, (1, far_rows), 1)
        offset = (c_r // (turns * EX_DEV) - start.astype(jnp.int32)) & (n_dp - 1)
        offset = offset + c_r % (turns * EX_DEV) // EX_DEV * n_dp
        rank_r = jnp.where(offset.astype(F32) < length, (c_r % EX_DEV).astype(F32), -1.0)

        @pl.when(decoder)
        def _():
            far_ref[...] = jnp.broadcast_to(rank_r, far_ref.shape)

    def spread_rows():
        sent = lax.broadcasted_iota(jnp.int32, (rows, rows), 0)
        row = lax.broadcasted_iota(jnp.int32, (rows, rows), 1)
        here_too = sent % keep * n_dp + sent // keep == row
        spread_ref[...] = jnp.where(here_too, 1.0, 0.0).astype(BF16)

    def pick_rows(turn):
        start_i = found["start_r"].astype(jnp.int32)
        offset = ((dp - start_i) & (n_dp - 1)) + turn * n_dp
        source = dev_r * float(sides * keep) + ((start_i + offset) // n_dp).astype(F32)
        value = jnp.where(offset.astype(F32) < len_r, source + 1.0, 0.0)
        place = far_dev_r * float(EX_DEV) + found["far_rank_r"]
        down = found["down"]
        one = jnp.ones_like(down)
        found[turn] = (
            jnp.sum(jnp.where(place == down, value * one, 0.0), axis=1, keepdims=True) - 1.0
        )

    def pick_side(b, turn):
        fidx = found[turn]
        place = lax.broadcasted_iota(jnp.int32, (count, n_dp * sides * keep), 1).astype(F32)
        at = jnp.where(fidx >= 0.0, fidx + float(b * keep), -1.0)
        pick_ref[b * turns + turn] = jnp.where(place == at, 1.0, 0.0).astype(BF16)

    def product(y, zb):
        total0 = total1 = None
        for row in (y, 1 - y):
            block = row * nz + zb
            at = pl.ds(pl.multiple_of(block * depth, depth), depth)
            p0 = nn(left0[block], wall[at, :width])
            p1 = nn(left1[block], wall[at, width:])
            total0 = p0 if total0 is None else total0 + p0
            total1 = p1 if total1 is None else total1 + p1
        acc[:, :width] += total0
        acc[:, width:] += total1

    def arrived(k, carry):
        hop, up = (k + 1) // 2, k & 1
        zb = (z - jnp.where(up == 1, hop, -hop)) & (nz - 1)
        slot = jnp.where(k == 0, 0, hop + (1 - up) * half)
        for kind in "bc":
            y_copy(kind, zb, slot, False).wait_recv()
        product(yl, zb)
        return carry

    def cot_pass(now):
        @pl.when(decoder & now)
        def _():
            for o in (1, 3, 2):
                if o < nx:
                    owner = (xx - o + nx) % nx * 2 + core
                    cot_copy(owner, o, sibling).wait_recv()
                    cot_copy(owner, nx + o, sibling).start()

    def cot_wait(now):
        @pl.when(decoder & now)
        def _():
            for o in range(nx):
                owner = (xx - o + nx) % nx * 2 + 1 - core
                cot_copy(owner, nx + o, sibling).wait_recv()

    def pass_on(hop, last, kinds=order):
        for kind in kinds:
            for sign in (1, -1):
                if last and not at_last(sign, kind):
                    continue
                z_copy(sign, kind, hop, False).wait_recv()
                if not last:
                    onward = z_copy(sign, kind, hop + 1, True)
                    if at_last(sign, kind):
                        onward.start()
                    else:
                        pl.when(hop + 1 < half)(onward.start)
                if kind in "bc":
                    slot = hop if sign == 1 else half + hop
                    y_copy(kind, (z - sign * hop) & (nz - 1), slot, True).start()

    acc[...] = jnp.zeros_like(acc)
    spread_rows()
    inputs[2].wait()
    inputs[3].wait()
    norm_hops = max(1, min(4, half - 1))
    chunks = rows // step
    share_of = -(-chunks // norm_hops)
    quota = 5

    def some_work(hop, slot):
        first = jnp.minimum((hop - 1) * share_of, chunks)
        middle = jnp.minimum(first + share_of // 2, chunks)
        end = jnp.minimum(first + share_of, chunks)
        bounds = (first, middle, end)
        lax.fori_loop(bounds[slot], bounds[slot + 1], norm_rows, 0)
        first = (hop - norm_hops - 1) * quota
        bounds = (first, first + 3, jnp.minimum(first + quota, 2 * hop - 1))
        late = hop > norm_hops
        low = jnp.where(late, bounds[slot], 0)
        high = jnp.where(late, jnp.minimum(bounds[slot + 1], 2 * hop - 1), 0)
        lax.fori_loop(low, high, arrived, 0)

    def one_hop(hop, carry):
        pass_on(hop, False, order[:2])
        cot_pass(hop == norm_hops)
        cot_wait(hop == norm_hops + 1)
        some_work(hop, 0)
        pass_on(hop, False, order[2:])
        some_work(hop, 1)
        return carry

    lax.fori_loop(1, half, one_hop, 0)
    if half == 1:
        lax.fori_loop(0, chunks, norm_rows, 0)
        cot_pass(True)
    pass_on(half, True)
    if half - 1 > norm_hops:
        done = min((half - 1 - norm_hops) * quota, 2 * half - 3)
        lax.fori_loop(done, 2 * half, arrived, 0)
    else:
        cot_wait(True)
        lax.fori_loop(0, 2 * half, arrived, 0)

    pl.semaphore_signal(cross_sem, inc=1, device_id=(across, dp, mp), device_id_type=MESH)

    def hop_copy(k, src, dst, target_section, target):
        return pltpu.make_async_remote_copy(
            src_ref=src,
            dst_ref=dst,
            send_sem=hop_send.at[k],
            recv_sem=hop_recv.at[k],
            device_id=(target_section, target, mp),
            device_id_type=MESH,
        )

    def wait_bytes(sem, buf, size):
        pltpu.make_async_copy(buf.at[pl.ds(0, size)], buf.at[pl.ds(0, size)], sem).wait()

    def to_all(send):
        def four(k, carry):
            away = half - 1 - k
            for sign in (1, -1):
                for y in (yl, 1 - yl):
                    send(y * nz + ((z + sign * away) & (nz - 1)))
            return carry

        for y in (yl, 1 - yl):
            send(y * nz + ((z + half) & (nz - 1)))
        lax.fori_loop(0, half - 1, four, 0)

    def local_copy(part):
        return pltpu.make_async_copy(
            send1.at[part, dp], in1.at[part, dp], hop_local.at[part]
        )

    for part in range(2):
        at = slice(part * width, (part + 1) * width)
        qkv[:, at] = acc[:, at].astype(BF16)
        moved = nn(spread_ref[...], qkv[:, at]).reshape(n_dp, keep, width)
        pieces = [moved[:, :, b * LANES : (b + 1) * LANES] for b in range(sides)]
        send1[part] = jnp.concatenate(pieces, axis=1).astype(BF16)
        local_copy(part).start()

        def send_to(target, part=part):
            hop_copy(part, send1.at[part, target], in1.at[part, dp], section, target).start()

        to_all(send_to)
        send_to((1 - yl) * nz + z)

    starts()
    own_ranks()
    far_ranks()
    for turn in range(turns):
        pick_rows(turn)
        for b in range(sides):
            pick_side(b, turn)

    for part in range(2):
        local_copy(part).wait()
        wait_bytes(hop_recv.at[part], in1.at[part], n_dp - 1)
        first_in = in1[part].reshape(n_dp * sides * keep, LANES)
        pieces = [
            nn(pick_ref[k], first_in).reshape(n_dp, EX_DEV, LANES) for k in range(sides * turns)
        ]
        send2[part] = jnp.concatenate(pieces, axis=1).astype(BF16)
        if part == 0:
            pl.semaphore_wait(cross_sem, 1)

        def pass_to(target, part=part):
            hop_copy(2 + part, send2.at[part, target], in2.at[part, dp], across, target).start()

        to_all(pass_to)
        pass_to(dp)
        pass_to((1 - yl) * nz + z)

    scale = 1.0 / float(HEAD) ** 0.5
    lane = lax.broadcasted_iota(jnp.int32, (1, LANES), 1) // HEAD
    heads = LANES // HEAD
    per_side = turns * EX_DEV

    def came(part, b):
        return in2[part, :, b * per_side : (b + 1) * per_side, :].reshape(far_rows, LANES)

    def own(part, b):
        return qkv[:, part * width + b * LANES : part * width + (b + 1) * LANES]

    def one_head(t, s):
        return jnp.where(lane == s, t, jnp.zeros_like(t))

    def softmax(q, k, mask):
        weight = jnp.where(mask, jnp.exp(nt(q, k) * scale), 0.0)
        return weight / jnp.sum(weight, axis=1, keepdims=True)

    def backward(probs, dout_s, v):
        probs_bf = probs.astype(BF16)
        attended = nn(probs_bf, v).astype(BF16)
        delta = jnp.sum(dout_s.astype(F32) * attended.astype(F32), axis=1, keepdims=True)
        return probs_bf, (probs * (nt(dout_s, v) - delta) * scale).astype(BF16)

    def merge(news, sums, s):
        return [jnp.where(lane == s, new, old) for new, old in zip(news, sums)] if s else news

    over_z = (nz - 1) * (depth + CUT)
    over_y = CUT + nz * (depth - CUT)
    wait_bytes(w_send_sem, wall, over_z)
    wait_bytes(w_send_sem, wall, over_y)
    for part in range(2):
        wait_bytes(hop_send.at[part], send1.at[part], n_dp - 1)

    @pl.when(decoder)
    def _():
        wait_bytes(cot_send_sem, left1, (2 * nx - 1) * per_mp)

    wait_bytes(hop_recv.at[2], in2.at[0], n_dp)

    @pl.when(encoder)
    def _():
        example = lax.broadcasted_iota(jnp.int32, (far_rows, rows), 0) % EX_DEV
        mask = example.astype(F32) == far_ref[:1, :rows]
        for b in range(sides):
            q = came(0, b)
            for s in range(heads):
                probs_ref[b * heads + s] = softmax(one_head(q, s), own(0, b), mask)

    @pl.when(decoder)
    def _():
        mask = own_ref[:, :1] == far_ref[:1, :]
        for b in range(sides):
            k = came(0, b)
            for s in range(heads):
                probs = softmax(one_head(own(0, b), s), k, mask)
                for c in range(far_rows // rows):
                    probs_ref[b * heads + s, c * rows : (c + 1) * rows, :] = probs[
                        :, c * rows : (c + 1) * rows
                    ]

    wait_bytes(hop_recv.at[3], in2.at[1], n_dp)

    @pl.when(encoder)
    def _():
        for b in range(sides):
            q, dout = came(0, b), came(1, b)
            sums = []
            for s in range(heads):
                probs_bf, dscore = backward(
                    probs_ref[b * heads + s], one_head(dout, s), own(1, b)
                )
                sums = merge((tn(dscore, q), tn(probs_bf, dout)), sums, s)
            for part in range(2):
                low = part * width + b * LANES
                grad[:, low : low + LANES] = sums[part].astype(BF16)

    @pl.when(decoder)
    def _():
        for b in range(sides):
            k, v = came(0, b), came(1, b)
            sums = []
            for s in range(heads):
                probs = jnp.concatenate(
                    [
                        probs_ref[b * heads + s, c * rows : (c + 1) * rows, :]
                        for c in range(far_rows // rows)
                    ],
                    axis=1,
                )
                dscore = backward(probs, one_head(own(1, b), s), v)[1]
                sums = merge((nn(dscore, k),), sums, s)
            grad[:, b * LANES : (b + 1) * LANES] = sums[0].astype(BF16)
        grad[:, width:] = jnp.zeros((rows, width), BF16)

    columns = features // n_mp
    share = jnp.sum(grad[...].astype(F32) * qkv[...].astype(F32), axis=1, keepdims=True)
    inverse = inv_ref[:, :1]
    slope = inverse * inverse * share * (1.0 / features)

    def term(owner, low, size):
        at = pl.ds(pl.multiple_of(owner * columns, columns), columns)
        here_rows = slice(low, low + size)
        raw = nt(grad[here_rows, :], wall[at, :])
        return inverse[here_rows] * (raw * gain_ref[:, at]) - x_ref[
            here_rows, at
        ].astype(F32) * slope[here_rows]

    middle = rows // 2

    def sib_copy(o, h):
        at = pl.ds(h * middle, middle)
        return pltpu.make_async_remote_copy(
            src_ref=sib_send.at[o, at, :],
            dst_ref=sib_recv.at[o, at, :],
            send_sem=c_send.at[0],
            recv_sem=c_sib.at[o, h],
            device_id=(section, dp, sibling),
            device_id_type=MESH,
        )

    def to_sibling(o, h):
        at = slice(h * middle, (h + 1) * middle)
        sib_send[o, at, :] = term(((xx + o) & (nx - 1)) * 2 + 1 - core, h * middle, middle).astype(BF16)
        sib_copy(o, h).start()

    def combined(o, h):
        own_term = term(((xx + o) & (nx - 1)) * 2 + core, h * middle, middle)
        sib_copy(o, h).wait_recv()
        return own_term + sib_recv[o, h * middle : (h + 1) * middle, :].astype(F32)

    def part_copy(slot, o, low, size, sign):
        return pltpu.make_async_remote_copy(
            src_ref=x_send.at[o, pl.ds(low, size), :],
            dst_ref=x_recv.at[o, pl.ds(low, size), :],
            send_sem=c_send.at[1],
            recv_sem=c_x.at[slot],
            device_id=(section, dp, (xx + sign + nx) % nx * 2 + core),
            device_id_type=MESH,
        )

    top, low_half = slice(0, middle), slice(middle, rows)
    parts_sent = []
    if nx == 4:
        far_up = part_copy(0, 2, 0, middle, 1)
        far_down = part_copy(1, 2, middle, middle, -1)
        up_plain = part_copy(2, 1, middle, middle, 1)
        up_added = part_copy(3, 1, 0, middle, 1)
        down_plain = part_copy(4, 3, 0, middle, -1)
        down_added = part_copy(5, 3, middle, middle, -1)
        parts_sent = [far_up, far_down, up_plain, up_added, down_plain, down_added]
        for o, h in ((2, 0), (2, 1), (1, 1), (3, 0)):
            to_sibling(o, h)
        x_send[2, top, :] = combined(2, 0).astype(BF16)
        far_up.start()
        x_send[2, low_half, :] = combined(2, 1).astype(BF16)
        far_down.start()
        to_sibling(1, 0)
        to_sibling(3, 1)
        x_send[1, low_half, :] = combined(1, 1).astype(BF16)
        up_plain.start()
        x_send[3, top, :] = combined(3, 0).astype(BF16)
        down_plain.start()
        to_sibling(0, 0)
        to_sibling(0, 1)
        up = combined(1, 0)
        down = combined(3, 1)
        far_up.wait_recv()
        x_send[1, top, :] = (up + x_recv[2, top, :].astype(F32)).astype(BF16)
        up_added.start()
        far_down.wait_recv()
        x_send[3, low_half, :] = (down + x_recv[2, low_half, :].astype(F32)).astype(BF16)
        down_added.start()
        first, second = combined(0, 0), combined(0, 1)
        down_plain.wait_recv()
        first = first + x_recv[3, top, :].astype(F32)
        up_plain.wait_recv()
        second = second + x_recv[1, low_half, :].astype(F32)
        up_added.wait_recv()
        out_ref[top, :] = (first + x_recv[1, top, :].astype(F32)).astype(BF16)
        down_added.wait_recv()
        out_ref[low_half, :] = (second + x_recv[3, low_half, :].astype(F32)).astype(BF16)
    else:
        for o in range(nx):
            for h in range(2):
                to_sibling(o, h)
        if nx == 2:
            whole = part_copy(0, 1, 0, rows, 1)
            parts_sent += [whole]
            x_send[1, top, :] = combined(1, 0).astype(BF16)
            x_send[1, low_half, :] = combined(1, 1).astype(BF16)
            whole.start()
            whole.wait_recv()
        for h, at in enumerate((top, low_half)):
            result = combined(0, h)
            if nx == 2:
                result = result + x_recv[1, at, :].astype(F32)
            out_ref[at, :] = result.astype(BF16)

    for part in range(2):
        wait_bytes(hop_send.at[2 + part], send2.at[part], n_dp)
    wait_bytes(c_send.at[0], sib_send, nx)
    if nx > 1:
        wait_bytes(c_send.at[1], x_send, nx - 1)


def shards(n_dp, n_mp, layer_rows, cotangent, norm_gains, projections, enc_len, dec_len, enc_dev, dec_dev):
    x = layer_rows[0]
    rows, features = x.shape
    depth, _, width = projections.shape[1:]
    count = enc_len.shape[0]
    tables = [t.reshape(1, count) for t in (enc_len, dec_len, enc_dev, dec_dev)]
    keep = rows // n_dp
    turns = 2 * rows // EX_DEV // n_dp
    sides = width // LANES
    far_rows = n_dp * turns * EX_DEV
    nx = n_mp // 2
    nz = n_dp // 2
    columns = features // n_mp
    vmem = pl.BlockSpec(memory_space=pltpu.VMEM)
    hbm = pl.BlockSpec(memory_space=pl.ANY)
    dma = pltpu.SemaphoreType.DMA
    out = pl.pallas_call(
        functools.partial(kernel, n_dp, n_mp),
        out_shape=jax.ShapeDtypeStruct((rows, columns), BF16),
        in_specs=[hbm] * 4 + [vmem] * 4,
        out_specs=vmem,
        scratch_shapes=[
            pltpu.VMEM((rows, features), BF16),
            pltpu.VMEM((1, features), F32),
            pltpu.VMEM((depth, 2, width), BF16),
            pltpu.VMEM((rows, columns), BF16),
            pltpu.VMEM((features, 2 * width), BF16),
            pltpu.VMEM((features // LANES, rows, LANES), BF16),
            pltpu.VMEM((features // LANES, rows, LANES), BF16),
            pltpu.VMEM((rows, LANES), F32),
            pltpu.VMEM((rows, 2 * width), F32),
            pltpu.VMEM((rows, 2 * width), BF16),
            pltpu.VMEM((rows, 2 * width), BF16),
            pltpu.VMEM((sides * turns, count, n_dp * sides * keep), BF16),
            pltpu.VMEM((rows, LANES), F32),
            pltpu.VMEM((8, far_rows), F32),
            pltpu.VMEM((sides * LANES // HEAD, far_rows, rows), F32),
            pltpu.VMEM((rows, rows), BF16),
            pltpu.VMEM((2, n_dp, sides * keep, LANES), BF16),
            pltpu.VMEM((2, n_dp, sides * keep, LANES), BF16),
            pltpu.VMEM((2, n_dp, sides * turns * EX_DEV, LANES), BF16),
            pltpu.VMEM((2, n_dp, sides * turns * EX_DEV, LANES), BF16),
            pltpu.VMEM((nx, rows, columns), BF16),
            pltpu.VMEM((nx, rows, columns), BF16),
            pltpu.VMEM((nx, rows, columns), BF16),
            pltpu.VMEM((nx, rows, columns), BF16),
            dma((4,)),
            pltpu.SemaphoreType.REGULAR,
            dma((2, 4, max(1, nz // 2))),
            dma((3, nz)),
            dma((2 * nx,)),
            dma,
            dma,
            dma((4,)),
            dma((4,)),
            dma((2,)),
            dma((2,)),
            dma((nx, 2)),
            dma((6,)),
        ],
        compiler_params=pltpu.CompilerParams(
            collective_id=0, has_side_effects=True, vmem_limit_bytes=60 * 2**20
        ),
    )(x, norm_gains, projections[0], cotangent, *tables)
    return out[None]


def solution(mesh):
    placed = (
        P("section", "dp", None),
        P("dp", "mp"),
        P("section", None),
        P("section", "dp", None, "mp"),
        P(),
        P(),
        P(),
        P(),
    )
    return jax.shard_map(
        functools.partial(shards, mesh.shape["dp"], mesh.shape["mp"]),
        mesh=mesh,
        in_specs=placed,
        out_specs=P("section", "dp", "mp"),
        check_vma=False,
    )
```
